32 devices in a mesh: tx: 8 (over y, x, core), ty: 4 (over z).
Axes of the slice: x: 2, y: 2, z: 4, core: 2. Of those that a mesh axis runs over, the one named last changes fastest.
Arguments:
- points: bfloat16 [131072, 128], P(('tx', 'ty')), may hold values from -6 to 6
- embed_weight: bfloat16 [128, 512], replicated, may hold values from -0.5 to 0.5
- inner_weights: bfloat16 [1, 512, 512], replicated, may hold values from -0.25 to 0.25
- output_weight: bfloat16 [512, 128], replicated, may hold values from -0.25 to 0.25
- counts: int32 [32, 128], replicated, may hold values from 1 to 64, as said below
- point_order: int32 [32, 4096], P(('tx', 'ty')), may hold values from 0 to 4095, each once within a row
- inducing: bfloat16 [128, 128], replicated, may hold values from -6 to 6
- first_proj: bfloat16 [4, 128, 128], replicated, may hold values from -0.5 to 0.5
- second_proj: bfloat16 [4, 128, 128], replicated, may hold values from -0.5 to 0.5
- mixing: bfloat16 [8, 128, 128], replicated, may hold values from -0.1875 to 0.1875
Outputs:
- encoded: bfloat16 [131072, 128], P(('tx', 'ty'))
The draws below stay inside these ranges and needn't reach their ends.
Inputs may be any that keep to these rules, and one draw needn't show every extreme that they name: Row s sums to 4096. For every source s and every device, the counts of s in the 4 tiles that device holds sum to exactly 128, and one of those 4 entries equals 64. Row s is a permutation of the local points of source s: the points of tile g are point_order[s, offsets[s, g] + c] for c below counts[s, g].
All inputs are finite; a program needn't handle non-finite values.
Results may differ from the reference program's by a relative error of at most 0.025.
Values may be sent and summed in bfloat16 or wider, within the bound.
No kernel may reach another device: no remote copies, remote signals or barrier semaphores. Data moves between devices by JAX's collectives and lax.ppermute only.
A program may use at most 64 MiB of HBM per device.

```python
import jax
import jax.numpy as jnp
from jax import lax

PTS_DEV = 4096
IN = 128
HID = 512
MIDS = 1
C = 128
NI = 128
HEADS = 2
TLX = 2
TLY = 2
GX = 16
GY = 8
TILES = 128
CAP = 64
POINTS = 131072
N_TX = 8
N_TY = 4


def draw_counts(key, part):
    sources = N_TX * N_TY
    quota = PTS_DEV // sources
    spare = quota - CAP - 3
    key_a, key_b, key_c = jax.random.split(jax.random.fold_in(key, 17), 3)
    shape = (sources, N_TX, N_TY)
    cut_a = jax.random.randint(key_a, shape, 0, spare + 1, dtype=jnp.int32)
    cut_b = jax.random.randint(key_b, shape, 0, spare + 1, dtype=jnp.int32)
    lower = jnp.minimum(cut_a, cut_b)
    upper = jnp.maximum(cut_a, cut_b)
    pieces = jnp.stack([1 + lower, 1 + upper - lower, 1 + spare - upper], axis=-1)
    peak = jax.random.randint(key_c, shape, 0, TLX * TLY, dtype=jnp.int32)
    slots = jnp.arange(TLX * TLY, dtype=jnp.int32)
    rank = slots[None, None, None, :] - (slots[None, None, None, :] > peak[..., None]).astype(jnp.int32)
    rank = jnp.clip(rank, 0, 2).astype(jnp.int32)
    picked = jnp.take_along_axis(pieces, rank, axis=-1)
    values = jnp.where(slots[None, None, None, :] == peak[..., None], CAP, picked)
    values = values.reshape(sources, N_TX, N_TY, TLX, TLY).transpose(0, 1, 3, 2, 4)
    return values.reshape(sources, N_TX * TLX * N_TY * TLY).astype(jnp.int32)


def levels(rng, shape, shards, smallest, top_value):
    def one(position, blocks):
        steps = jax.random.uniform(jax.random.fold_in(jax.random.fold_in(rng, 6), position), (blocks,), jnp.float32, smallest / len(shards), top_value / len(shards))
        return jnp.repeat(jnp.exp(steps), shape[position] // blocks).reshape((-1,) + (1,) * (len(shape) - position - 1))

    loudness = one(*shards[0])
    for cut in shards[1:]:
        loudness = loudness * one(*cut)
    return loudness


def noise(stream_key, shape, width, reach, shards=(), held_as=jnp.bfloat16):
    drawn = width * jax.random.normal(stream_key, shape, jnp.float32)
    if shards:
        drawn = drawn * levels(stream_key, shape, shards, -0.22, 0.18)
    return jnp.clip(drawn, -reach, reach).astype(held_as)


def setup_inputs(seed: int = 0) -> dict:
    key_of = jax.random.split(jax.random.key(seed), 11)
    points = noise(key_of[0], (POINTS, IN), 1.0, 6.0, ((0, 32),))
    embed_weight = noise(key_of[1], (IN, HID), IN ** -0.5, 0.5)
    inner_weights = noise(key_of[2], (MIDS, HID, HID), HID ** -0.5, 0.25)
    output_weight = noise(key_of[3], (HID, C), HID ** -0.5, 0.25)
    counts = draw_counts(jax.random.fold_in(key_of[10], 71), 0)
    point_order = jax.vmap(lambda own: jax.random.permutation(own, PTS_DEV))(jax.random.split(key_of[5], (N_TX * N_TY))).reshape((N_TX * N_TY, PTS_DEV)).astype(jnp.int32)
    inducing = noise(key_of[6], (NI, C), 1.0, 6.0)
    first_proj = noise(key_of[7], (4, C, C), C ** -0.5, 0.5)
    second_proj = noise(key_of[8], (4, C, C), C ** -0.5, 0.5)
    mixing = noise(key_of[9], (8, C, C), (8 * C) ** -0.5, 0.1875)
    return dict(points=points, embed_weight=embed_weight, inner_weights=inner_weights, output_weight=output_weight, counts=counts, point_order=point_order, inducing=inducing, first_proj=first_proj, second_proj=second_proj, mixing=mixing)


sharpness = 32.0
epsilon = 1e-06
neighbour_steps = ((-1, -1), (-1, 0), (-1, 1), (0, -1), (0, 1), (1, -1), (1, 0), (1, 1))

def unit_heads(projected, head_count):
    pieces = projected.reshape(projected.shape[:-1] + (head_count, projected.shape[-1] // head_count))
    magnitude = jnp.sqrt(lax.optimization_barrier(jnp.sum(pieces * pieces, axis=-1, keepdims=True)) + epsilon)
    return (pieces / magnitude).reshape(projected.shape).astype(jnp.bfloat16)

def attend(query_rows, key_rows, value_rows, weight_mask, head_count):
    head_width = query_rows.shape[-1] // head_count
    outputs = []
    for head_id in range(head_count):
        lower = head_id * head_width
        upper = lower + head_width
        scores = jnp.dot(query_rows[:, lower:upper], key_rows[:, lower:upper].T, preferred_element_type=jnp.float32)
        weights = jnp.exp(sharpness * scores) * weight_mask[None, :]
        totals = lax.optimization_barrier(jnp.sum(weights, axis=1, keepdims=True))
        numer = jnp.dot(weights.astype(jnp.bfloat16), value_rows[:, lower:upper], preferred_element_type=jnp.float32)
        outputs.append(numer / totals)
    return jnp.concatenate(outputs, axis=1).astype(jnp.bfloat16)

def reference(points, embed_weight, inner_weights, output_weight, counts, point_order, inducing, first_proj, second_proj, mixing):
    devices = N_TX * N_TY
    hidden = jax.nn.silu(jnp.dot(points, embed_weight, preferred_element_type=jnp.float32)).astype(jnp.bfloat16)
    for layer_id in range(MIDS):
        hidden = jax.nn.silu(jnp.dot(hidden, inner_weights[layer_id], preferred_element_type=jnp.float32)).astype(jnp.bfloat16)
    features = jnp.dot(hidden, output_weight, preferred_element_type=jnp.float32).astype(jnp.bfloat16)
    offsets = (jnp.cumsum(counts, axis=1) - counts).astype(jnp.int32)
    slot_ids = jnp.arange(CAP, dtype=jnp.int32)
    sources = jnp.arange(devices, dtype=jnp.int32)

    def tile_input(tile_id):
        starts = lax.dynamic_index_in_dim(offsets, tile_id, 1, keepdims=False)
        tallies = lax.dynamic_index_in_dim(counts, tile_id, 1, keepdims=False)
        filled = slot_ids[None, :] < tallies[:, None]
        positions = jnp.where(filled, starts[:, None] + slot_ids[None, :], 0).astype(jnp.int32)
        local_index = jnp.take_along_axis(point_order, positions, axis=1)
        indices = (local_index + sources[:, None] * PTS_DEV).reshape(-1).astype(jnp.int32)
        filled = filled.reshape(-1)
        picked = jnp.where(filled[:, None], features[indices], jnp.zeros((), jnp.bfloat16))
        return (picked, filled, indices)
    inducing_queries = unit_heads(jnp.dot(inducing, first_proj[0], preferred_element_type=jnp.float32), HEADS)

    def summarize(tile_id):
        picked, filled, unused = tile_input(tile_id)
        key_rows = unit_heads(jnp.dot(picked, first_proj[1], preferred_element_type=jnp.float32), HEADS)
        value_rows = jnp.dot(picked, first_proj[2], preferred_element_type=jnp.float32).astype(jnp.bfloat16)
        attended = attend(inducing_queries, key_rows, value_rows, filled.astype(jnp.float32), HEADS)
        return (inducing.astype(jnp.float32) + jnp.dot(attended, first_proj[3], preferred_element_type=jnp.float32)).astype(jnp.bfloat16)
    summary = lax.map(summarize, jnp.arange(TILES, dtype=jnp.int32)).reshape(GX, GY, NI, C)
    padded = jnp.pad(summary, ((1, 1), (1, 1), (0, 0), (0, 0)))
    mixture = summary.astype(jnp.float32)
    for direction, steps in enumerate(neighbour_steps):
        shifted = padded[1 + steps[0]:1 + steps[0] + GX, 1 + steps[1]:1 + steps[1] + GY].astype(jnp.float32)
        mixture = mixture + jnp.einsum('xyic,ce->xyie', shifted, mixing[direction].astype(jnp.float32))
    mixture = mixture.astype(jnp.bfloat16).reshape(TILES, NI, C)

    def finish(tile_id, encoded):
        picked, filled, indices = tile_input(tile_id)
        mixed_tile = lax.dynamic_index_in_dim(mixture, tile_id, 0, keepdims=False)
        point_queries = unit_heads(jnp.dot(picked, second_proj[0], preferred_element_type=jnp.float32), HEADS)
        key_rows = unit_heads(jnp.dot(mixed_tile, second_proj[1], preferred_element_type=jnp.float32), HEADS)
        value_rows = jnp.dot(mixed_tile, second_proj[2], preferred_element_type=jnp.float32).astype(jnp.bfloat16)
        attended = attend(point_queries, key_rows, value_rows, jnp.ones((NI,), jnp.float32), HEADS)
        result = (picked.astype(jnp.float32) + jnp.dot(attended, second_proj[3], preferred_element_type=jnp.float32)).astype(jnp.bfloat16)
        targets = jnp.where(filled, indices, devices * PTS_DEV).astype(jnp.int32)
        return encoded.at[targets].set(result, mode='drop')
    return lax.fori_loop(0, TILES, finish, jnp.zeros((devices * PTS_DEV, C), jnp.bfloat16))
```

```python
import functools
import math

import jax
import jax.numpy as jnp
from jax import lax
from jax.experimental import pallas as pl
from jax.experimental.pallas import tpu as pltpu
from jax.sharding import PartitionSpec as P

HEADS = 2
TLX = 2
TLY = 2
LANES = 128
BF = jnp.bfloat16
F32 = jnp.float32

sharpness = 32.0
epsilon = 1e-06
neighbour_steps = ((-1, -1), (-1, 0), (-1, 1), (0, -1), (0, 1), (1, -1), (1, 0), (1, 1))
VMEM = pltpu.VMEM
SMEM = pltpu.SMEM


def dot(a, b):
    return jnp.dot(a, b, preferred_element_type=F32)


def dot_t(a, b):
    return lax.dot_general(a, b, (((1,), (1,)), ((), ())), preferred_element_type=F32)


def head_ones():
    row = lax.broadcasted_iota(jnp.int32, (2 * LANES, LANES), 0)
    col = lax.broadcasted_iota(jnp.int32, (2 * LANES, LANES), 1)
    half = LANES // HEADS
    same = ((row % LANES) // half) == (col // half)
    return jnp.where(same, 1.0, 0.0).astype(BF)


def unit(v, ones):
    square = v * v
    high = square.astype(BF)
    low = (square - high.astype(F32)).astype(BF)
    total = dot(jnp.concatenate([high, low], axis=1), ones)
    return v * lax.rsqrt(total + epsilon)


def silu(v):
    half = 0.5 * v
    return half + half * jnp.tanh(half)


def encode_kernel(
    grid_y,
    along_y,
    quota,
    points_ref,
    w1_ref,
    w2_ref,
    w3_ref,
    counts_ref,
    order_ref,
    feat_ref,
    index_ref,
    off_ref,
    index_s,
    wide_ref,
    xa_ref,
    xb_ref,
    sem,
):
    tiles = counts_ref.shape[0]
    order_rows = order_ref.shape[0]
    rows_total = points_ref.shape[0]
    chunk = xa_ref.shape[0]

    def add_up(g, total):
        off_ref[g] = total
        return total + counts_ref[g]

    lax.fori_loop(0, tiles, add_up, jnp.int32(0), unroll=8)
    wide_ref[...] = points_ref[...].astype(F32)
    lane = lax.broadcasted_iota(jnp.int32, (1, LANES), 1)

    def run_of(start):
        line = start >> 7
        shift = start & (LANES - 1)
        first = order_ref[pl.ds(jnp.clip(line, 0, order_rows - 1), 1), :]
        second = order_ref[pl.ds(jnp.clip(line + 1, 0, order_rows - 1), 1), :]
        merged = jnp.where(lane < shift, second, first)
        return pltpu.roll(merged, (LANES - shift) & (LANES - 1), 1)

    per_line = LANES // quota

    def index_line(line, carry):
        value = jnp.zeros((1, LANES), jnp.int32)
        for k in range(per_line):
            d = line * per_line + k
            g1 = (d // along_y) * (TLX * grid_y) + (d % along_y) * TLY
            n1 = counts_ref[g1] + counts_ref[g1 + 1]
            run1 = run_of(off_ref[g1] - k * quota)
            run2 = run_of(off_ref[g1 + grid_y] - n1 - k * quota)
            both = jnp.where(lane < k * quota + n1, run1, run2)
            value = both if k == 0 else jnp.where(lane >= k * quota, both, value)
        index_ref[pl.ds(line, 1), :] = value
        return carry

    lax.fori_loop(0, rows_total // LANES, index_line, 0)
    copy = pltpu.make_async_copy(index_ref, index_s, sem)
    copy.start()
    copy.wait()

    def gather(c, buffer):
        for r in range(chunk):
            i = index_s[c * (chunk // LANES) + r // LANES, r % LANES]
            buffer[pl.ds(r, 1), :] = wide_ref[pl.ds(i, 1), :]

    def network(c, buffer):
        x = buffer[...].astype(BF)
        hidden = silu(dot(x, w1_ref[...])).astype(BF)
        hidden = silu(dot(hidden, w2_ref[0])).astype(BF)
        start = pl.multiple_of(c * chunk, chunk)
        feat_ref[pl.ds(start, chunk), :] = dot(hidden, w3_ref[...]).astype(BF)

    chunks = rows_total // chunk
    gather(0, xa_ref)

    def step(k, carry):
        c = 2 * k
        gather(c + 1, xb_ref)
        network(c, xa_ref)
        gather(jnp.minimum(c + 2, chunks - 1), xa_ref)
        network(c + 1, xb_ref)
        return carry

    lax.fori_loop(0, chunks // 2, step, 0)


def tile_bounds(n0, n1, n2):
    return (0, n0, n0 + n1, n0 + n1 + n2)


def summarize_kernel(
    along_y, quota, rows_ref, counts_ref, where_ref, inducing_ref, proj_ref, out_ref, kv_ref, num_ref
):
    total_rows = rows_ref.shape[0]
    grid_y = along_y * TLY
    half = LANES // HEADS
    chunk = min(512, total_rows)
    ones = head_ones()
    lane = lax.broadcasted_iota(jnp.int32, (1, LANES), 1)
    left = lane < half
    base = where_ref[0] * (TLX * grid_y) + where_ref[1] * TLY
    inducing = inducing_ref[...]
    queries = unit(dot(inducing, proj_ref[0]), ones)
    queries = jnp.concatenate(
        [jnp.where(left, queries, 0.0), jnp.where(left, 0.0, queries)], axis=0
    ).astype(BF)
    wk = proj_ref[1]
    wv = proj_ref[2]
    wv0, wv1 = wv[:, :half], wv[:, half:]
    weights = jnp.concatenate([wk, wv0, wv0, wv1, wv1], axis=1)
    kv_ref[...] = weights
    num_ref[...] = jnp.zeros_like(num_ref)
    block_row = lax.broadcasted_iota(jnp.int32, (quota, LANES), 0)

    def step(c, carry):
        x = rows_ref[pl.ds(pl.multiple_of(c * chunk, chunk), chunk), :]
        projected = dot(x, kv_ref[...])
        keys = unit(projected[:, :LANES], ones).astype(BF)
        scores = dot_t(queries, keys)
        weights = jnp.exp2(scores * (sharpness * math.log2(math.e))).astype(BF)
        masks = [[], []]
        for k in range(chunk // quota):
            s = c * (chunk // quota) + k
            n0 = counts_ref[s, base]
            n1 = counts_ref[s, base + 1]
            n2 = counts_ref[s, base + grid_y]
            b = tile_bounds(n0, n1, n2) + (quota,)
            for pair in range(2):
                low = jnp.where(left, b[2 * pair], b[2 * pair + 1])
                high = jnp.where(left, b[2 * pair + 1], b[2 * pair + 2])
                masks[pair].append(
                    jnp.where((block_row >= low) & (block_row < high), 1.0, 0.0)
                )
        masks = [jnp.concatenate(m, axis=0) for m in masks]
        mask_bf = [m.astype(BF) for m in masks]
        for h in range(HEADS):
            value = projected[:, (1 + h) * LANES : (2 + h) * LANES]
            right = jnp.concatenate(
                [(value * m).astype(BF) for m in masks] + mask_bf, axis=1
            )
            num_ref[h] += dot(weights[h * LANES : (h + 1) * LANES], right)
        return carry

    lax.fori_loop(0, total_rows // chunk, step, 0)
    for pair in range(2):
        cols = slice(pair * LANES, (pair + 1) * LANES)
        tots = slice((2 + pair) * LANES, (3 + pair) * LANES)
        a0 = num_ref[0, :, cols] / num_ref[0, :, tots]
        a1 = num_ref[1, :, cols] / num_ref[1, :, tots]
        first = jnp.where(left, a0, pltpu.roll(a1, half, 1))
        second = jnp.where(left, pltpu.roll(a0, half, 1), a1)
        for k, attended in enumerate((first, second)):
            t = pair * 2 + k
            value = inducing.astype(F32) + dot(attended.astype(BF), proj_ref[3])
            out_ref[t * LANES : (t + 1) * LANES, :] = value.astype(BF)


def finish_kernel(
    along_x,
    along_y,
    quota,
    summary_hbm,
    feat_ref,
    counts_ref,
    index_ref,
    proj_ref,
    mixing_ref,
    out_ref,
    grid_ref,
    mid_ref,
    side_ref,
    kv_ref,
    wide_ref,
    res_ref,
    sems,
):
    grid_x = along_x * TLX
    grid_y = along_y * TLY
    half = LANES // HEADS
    devices = along_x * along_y

    def load(d):
        ax, ay = d // along_y, d % along_y
        return pltpu.make_async_copy(
            summary_hbm.at[d],
            grid_ref.at[pl.ds(2 * ax + 1, TLX), pl.ds(2 * ay + 1, TLY)],
            sems.at[d],
        )

    lax.fori_loop(0, devices, lambda d, c: (load(d).start(), c)[1], 0)

    blank = jnp.zeros((LANES, LANES), BF)

    def blank_x(i, c):
        grid_ref[i, 0] = blank
        grid_ref[i, grid_y + 1] = blank
        return c

    lax.fori_loop(0, grid_x + 2, blank_x, 0)
    for j in range(1, grid_y + 1):
        grid_ref[0, j] = blank
        grid_ref[grid_x + 1, j] = blank

    row = lax.broadcasted_iota(jnp.int32, (LANES, LANES), 0)
    col = lax.broadcasted_iota(jnp.int32, (LANES, LANES), 1)
    eye = jnp.where(row == col, 1.0, 0.0).astype(BF)

    def mix(a, b):
        return eye if (a, b) == (0, 0) else mixing_ref[neighbour_steps.index((a, b))]

    for k, a in enumerate((-1, 0, 1)):
        rows = slice(k * 2 * LANES, (k + 1) * 2 * LANES)
        mid_ref[rows, :] = jnp.concatenate(
            [
                jnp.concatenate([mix(a, 0), mix(a, -1)], axis=1),
                jnp.concatenate([mix(a, 1), mix(a, 0)], axis=1),
            ],
            axis=0,
        )
    for k, b in enumerate((-1, 1)):
        side_ref[k] = jnp.concatenate(
            [
                jnp.concatenate([mix(0, b), mix(-1, b)], axis=1),
                jnp.concatenate([mix(1, b), mix(0, b)], axis=1),
                jnp.concatenate([mix(-1, b), blank], axis=1),
                jnp.concatenate([blank, mix(1, b)], axis=1),
            ],
            axis=0,
        )
    kv_ref[...] = jnp.concatenate([proj_ref[1], proj_ref[2]], axis=1)
    ones = head_ones()
    lane = lax.broadcasted_iota(jnp.int32, (1, LANES), 1)
    left = lane < half
    ones_block = jnp.ones((LANES, LANES), BF)
    block_row = lax.broadcasted_iota(jnp.int32, (quota, LANES), 0)
    lax.fori_loop(0, devices, lambda d, c: (load(d).wait(), c)[1], 0)

    def band(ax, carry):
        def tile(i, j):
            return grid_ref[2 * ax + i, j]

        mids, lefts, rights = [], [], []
        for i in range(2):
            for ay in range(along_y):
                mids.append(
                    jnp.concatenate(
                        [tile(i + r, 2 * ay + 1 + s) for r in range(3) for s in range(2)], axis=1
                    )
                )
        for ay in range(along_y):
            lefts.append(jnp.concatenate([tile(i, 2 * ay) for i in (1, 2, 0, 3)], axis=1))
            rights.append(jnp.concatenate([tile(i, 2 * ay + 3) for i in (1, 2, 0, 3)], axis=1))
        middle = dot(jnp.concatenate(mids, axis=0), mid_ref[...])
        from_left = dot(jnp.concatenate(lefts, axis=0), side_ref[0])
        from_right = dot(jnp.concatenate(rights, axis=0), side_ref[1])
        mixtures = []
        for ay in range(along_y):
            span = slice(ay * LANES, (ay + 1) * LANES)
            for i in range(2):
                m = middle[(i * along_y + ay) * LANES : (i * along_y + ay + 1) * LANES]
                cols = slice(i * LANES, (i + 1) * LANES)
                mixtures.append((m[:, :LANES] + from_left[span, cols]).astype(BF))
                mixtures.append((m[:, LANES:] + from_right[span, cols]).astype(BF))
        kv = dot(jnp.concatenate(mixtures, axis=0), kv_ref[...])
        keys = unit(kv[:, :LANES], ones).astype(BF)
        values = kv[:, LANES:].astype(BF)
        band_rows = along_y * quota
        start = pl.multiple_of(ax * band_rows, band_rows)
        x_band = feat_ref[pl.ds(start, band_rows), :]
        query_band = unit(dot(x_band, proj_ref[0]), ones)
        attended = []
        for ay in range(along_y):
            base = ax * (TLX * grid_y) + ay * TLY
            b = tile_bounds(
                counts_ref[base], counts_ref[base + 1], counts_ref[base + grid_y]
            ) + (quota,)
            inside = [(block_row >= b[t]) & (block_row < b[t + 1]) for t in range(4)]
            query = query_band[ay * quota : (ay + 1) * quota]
            expanded = jnp.concatenate(
                [
                    jnp.concatenate(
                        [
                            jnp.where(inside[t] & (left if h == 0 else ~left), query, 0.0)
                            for t in range(4)
                        ],
                        axis=1,
                    )
                    for h in range(HEADS)
                ],
                axis=0,
            ).astype(BF)
            spans = [slice((ay * 4 + t) * LANES, (ay * 4 + t + 1) * LANES) for t in range(4)]
            key_cat = jnp.concatenate([keys[s] for s in spans], axis=1)
            scores = dot_t(expanded, key_cat)
            weights = jnp.exp2(scores * (sharpness * math.log2(math.e)))
            spread = jnp.concatenate(
                [
                    jnp.concatenate(
                        [
                            jnp.where(inside[t], weights[h * quota : (h + 1) * quota], 0.0)
                            for t in range(4)
                        ],
                        axis=1,
                    )
                    for h in range(HEADS)
                ],
                axis=0,
            ).astype(BF)
            value_cat = jnp.concatenate(
                [jnp.concatenate([values[s], ones_block], axis=1) for s in spans], axis=0
            )
            both = dot(spread, value_cat)
            picked = jnp.where(left, both[:quota, :LANES], both[quota:, :LANES])
            totals = jnp.where(left, both[:quota, LANES:], both[quota:, LANES:])
            attended.append((picked / totals).astype(BF))
        result = x_band.astype(F32) + dot(jnp.concatenate(attended, axis=0), proj_ref[3])
        res_ref[...] = result
        for r in range(band_rows):
            line = ax * (band_rows // LANES) + r // LANES
            i = index_ref[line, r % LANES]
            wide_ref[pl.ds(i, 1), :] = res_ref[pl.ds(r, 1), :]
        return carry

    lax.fori_loop(0, along_x, band, 0)
    out_ref[...] = wide_ref[...].astype(BF)


def spec(space):
    return pl.BlockSpec(memory_space=space)


def body(
    points,
    embed_weight,
    inner_weights,
    output_weight,
    counts,
    point_order,
    inducing,
    first_proj,
    second_proj,
    mixing,
):
    along_x = lax.axis_size("tx")
    along_y = lax.axis_size("ty")
    devices = along_x * along_y
    index_x = lax.axis_index("tx")
    index_y = lax.axis_index("ty")
    own_index = index_x * along_y + index_y
    point_count, width = points.shape
    quota = point_count // devices
    grid_x, grid_y = along_x * TLX, along_y * TLY
    lines = point_count // LANES
    chunk = 512
    own_counts = lax.dynamic_index_in_dim(counts, own_index, 0, keepdims=False)
    position = jnp.stack([index_x, index_y]).astype(jnp.int32)
    limit = pltpu.CompilerParams(vmem_limit_bytes=56 * 1024 * 1024)

    features, index = pl.pallas_call(
        functools.partial(encode_kernel, grid_y, along_y, quota),
        out_shape=(
            jax.ShapeDtypeStruct((point_count, width), BF),
            jax.ShapeDtypeStruct((lines, LANES), jnp.int32),
        ),
        in_specs=[spec(VMEM)] * 4 + [spec(SMEM), spec(VMEM)],
        out_specs=(spec(VMEM), spec(VMEM)),
        scratch_shapes=[
            SMEM((counts.shape[1],), jnp.int32),
            SMEM((lines, LANES), jnp.int32),
            VMEM((point_count, width), F32),
            VMEM((chunk, width), F32),
            VMEM((chunk, width), F32),
            pltpu.SemaphoreType.DMA,
        ],
        compiler_params=limit,
        name="encode_points",
    )(
        points,
        embed_weight,
        inner_weights,
        output_weight,
        own_counts,
        point_order.reshape(lines, LANES),
    )

    arrived = lax.all_to_all(
        features.reshape(devices, quota, width), ("tx", "ty"), split_axis=0, concat_axis=0, tiled=True
    ).reshape(point_count, width)

    summary = pl.pallas_call(
        functools.partial(summarize_kernel, along_y, quota),
        out_shape=jax.ShapeDtypeStruct((TLX * TLY * LANES, width), BF),
        in_specs=[spec(VMEM), spec(SMEM), spec(SMEM), spec(VMEM), spec(VMEM)],
        out_specs=spec(VMEM),
        scratch_shapes=[
            VMEM((width, 3 * LANES), BF),
            VMEM((HEADS, LANES, 4 * LANES), F32),
        ],
        compiler_params=limit,
        name="summarize_tiles",
    )(arrived, counts, position, inducing, first_proj)

    everyone = lax.all_gather(summary, ("tx", "ty"), axis=0, tiled=True)
    everyone = everyone.reshape(devices, TLX, TLY, LANES, width)

    return pl.pallas_call(
        functools.partial(finish_kernel, along_x, along_y, quota),
        out_shape=jax.ShapeDtypeStruct((point_count, width), BF),
        in_specs=[
            spec(pl.ANY),
            spec(VMEM),
            spec(SMEM),
            spec(SMEM),
            spec(VMEM),
            spec(VMEM),
        ],
        out_specs=spec(VMEM),
        scratch_shapes=[
            VMEM((grid_x + 2, grid_y + 2, LANES, width), BF),
            VMEM((6 * LANES, 2 * LANES), BF),
            VMEM((2, 4 * LANES, 2 * LANES), BF),
            VMEM((width, 2 * LANES), BF),
            VMEM((point_count, width), F32),
            VMEM((along_y * quota, width), F32),
            pltpu.SemaphoreType.DMA((devices,)),
        ],
        compiler_params=limit,
        name="finish_points",
    )(everyone, features, own_counts, index, second_proj, mixing)


def solution(mesh):
    placed = (P(("tx", "ty"), None), P(), P(), P(), P(), P(("tx", "ty"), None), P(), P(), P(), P())
    return jax.shard_map(
        body, mesh=mesh, in_specs=placed, out_specs=P(("tx", "ty"), None), check_vma=False
    )
```

```python
import functools
import math

import jax
import jax.numpy as jnp
from jax import lax
from jax.experimental import pallas as pl
from jax.experimental.pallas import tpu as pltpu
from jax.sharding import PartitionSpec as P

HEADS = 2
TLX = 2
TLY = 2
LANES = 128
BF = jnp.bfloat16
F32 = jnp.float32

sharpness = 32.0
epsilon = 1e-06
neighbour_steps = ((-1, -1), (-1, 0), (-1, 1), (0, -1), (0, 1), (1, -1), (1, 0), (1, 1))
VMEM = pltpu.VMEM
SMEM = pltpu.SMEM


def dot(a, b):
    return jnp.dot(a, b, preferred_element_type=F32)


def dot_t(a, b):
    return lax.dot_general(a, b, (((1,), (1,)), ((), ())), preferred_element_type=F32)


def head_ones():
    row = lax.broadcasted_iota(jnp.int32, (2 * LANES, LANES), 0)
    col = lax.broadcasted_iota(jnp.int32, (2 * LANES, LANES), 1)
    half = LANES // HEADS
    same = ((row % LANES) // half) == (col // half)
    return jnp.where(same, 1.0, 0.0).astype(BF)


def unit(v, ones):
    square = v * v
    high = square.astype(BF)
    low = (square - high.astype(F32)).astype(BF)
    total = dot(jnp.concatenate([high, low], axis=1), ones)
    return v * lax.rsqrt(total + epsilon)


def silu(v):
    half = 0.5 * v
    return half + half * jnp.tanh(half)


def encode_kernel(
    grid_y,
    along_y,
    quota,
    points_ref,
    w1_ref,
    w2_ref,
    w3_ref,
    counts_ref,
    order_ref,
    feat_ref,
    index_ref,
    off_ref,
    index_s,
    wide_ref,
    xa_ref,
    xb_ref,
    sem,
):
    tiles = counts_ref.shape[0]
    order_rows = order_ref.shape[0]
    rows_total = points_ref.shape[0]
    chunk = xa_ref.shape[0]

    def add_up(g, total):
        off_ref[g] = total
        return total + counts_ref[g]

    lax.fori_loop(0, tiles, add_up, jnp.int32(0), unroll=8)
    wide_ref[...] = points_ref[...].astype(F32)
    lane = lax.broadcasted_iota(jnp.int32, (1, LANES), 1)

    def run_of(start):
        line = start >> 7
        shift = start & (LANES - 1)
        first = order_ref[pl.ds(jnp.clip(line, 0, order_rows - 1), 1), :]
        second = order_ref[pl.ds(jnp.clip(line + 1, 0, order_rows - 1), 1), :]
        merged = jnp.where(lane < shift, second, first)
        return pltpu.roll(merged, (LANES - shift) & (LANES - 1), 1)

    per_line = LANES // quota

    def index_line(line, carry):
        value = jnp.zeros((1, LANES), jnp.int32)
        for k in range(per_line):
            d = line * per_line + k
            g1 = (d // along_y) * (TLX * grid_y) + (d % along_y) * TLY
            n1 = counts_ref[g1] + counts_ref[g1 + 1]
            run1 = run_of(off_ref[g1] - k * quota)
            run2 = run_of(off_ref[g1 + grid_y] - n1 - k * quota)
            both = jnp.where(lane < k * quota + n1, run1, run2)
            value = both if k == 0 else jnp.where(lane >= k * quota, both, value)
        index_ref[pl.ds(line, 1), :] = value
        return carry

    lax.fori_loop(0, rows_total // LANES, index_line, 0)
    copy = pltpu.make_async_copy(index_ref, index_s, sem)
    copy.start()
    copy.wait()

    def gather(c, buffer):
        for r in range(chunk):
            i = index_s[c * (chunk // LANES) + r // LANES, r % LANES]
            buffer[pl.ds(r, 1), :] = wide_ref[pl.ds(i, 1), :]

    def network(c, buffer):
        x = buffer[...].astype(BF)
        hidden = silu(dot(x, w1_ref[...])).astype(BF)
        hidden = silu(dot(hidden, w2_ref[0])).astype(BF)
        start = pl.multiple_of(c * chunk, chunk)
        feat_ref[pl.ds(start, chunk), :] = dot(hidden, w3_ref[...]).astype(BF)

    chunks = rows_total // chunk
    gather(0, xa_ref)

    def step(k, carry):
        c = 2 * k
        gather(c + 1, xb_ref)
        network(c, xa_ref)
        gather(jnp.minimum(c + 2, chunks - 1), xa_ref)
        network(c + 1, xb_ref)
        return carry

    lax.fori_loop(0, chunks // 2, step, 0)


def tile_bounds(n0, n1, n2):
    return (n0, n0 + n1, n0 + n1 + n2)


def tile_of(position, counts_ref, pieces, piece_id, grid_y):
    bounds = [None, None, None]
    for k, (s, base) in enumerate(pieces):
        found = tile_bounds(
            counts_ref[s, base], counts_ref[s, base + 1], counts_ref[s, base + grid_y]
        )
        for i in range(3):
            if k == 0:
                bounds[i] = jnp.full(position.shape, found[i], jnp.int32)
            else:
                bounds[i] = jnp.where(piece_id >= k, found[i], bounds[i])
    return sum((position >= b).astype(jnp.int32) for b in bounds)


def source_of(member, where_ref, low_count, along_y):
    return (member // low_count) * along_y + where_ref[1] * low_count + member % low_count


def tile_base(block, where_ref, low_blocks, grid_y):
    return where_ref[0] * (TLX * grid_y) + (where_ref[2] * low_blocks + block) * TLY


def partial_kernel(
    along_y, rows_ref, counts_ref, where_ref, inducing_ref, proj_ref, own_ref, send_ref, num_ref
):
    members, blocks, quota, width = rows_ref.shape
    grid_y = along_y * TLY
    half = LANES // HEADS
    group = min(512 // quota, members)
    chunk = group * quota
    ones = head_ones()
    lane = lax.broadcasted_iota(jnp.int32, (1, LANES), 1)
    left = lane < half
    queries = unit(dot(inducing_ref[...], proj_ref[0]), ones)
    queries = jnp.concatenate(
        [jnp.where(left, queries, 0.0), jnp.where(left, 0.0, queries)], axis=0
    ).astype(BF)
    wv_t = proj_ref[2].astype(F32).T.astype(BF)
    num_ref[...] = jnp.zeros_like(num_ref)
    spot = lax.broadcasted_iota(jnp.int32, (1, chunk), 1)
    tile_row = lax.broadcasted_iota(jnp.int32, (16, chunk), 0)
    low_count = along_y // blocks

    def step(c, carry):
        for b in range(blocks):
            x = jnp.concatenate([rows_ref[c * group + k, b] for k in range(group)], axis=0)
            keys = unit(dot(x, proj_ref[1]), ones).astype(BF)
            weights = jnp.exp2(dot_t(keys, queries) * (sharpness * math.log2(math.e))).astype(BF)
            values = dot_t(wv_t, x)
            base = tile_base(b, where_ref, blocks, grid_y)
            pieces = [
                (source_of(c * group + k, where_ref, low_count, along_y), base)
                for k in range(group)
            ]
            tile = tile_of(spot % quota, counts_ref, pieces, spot // quota, grid_y)
            stacked = [jnp.where(tile == t, values, 0.0).astype(BF) for t in range(4)]
            stacked.append(jnp.where(tile_row == tile, 1.0, 0.0).astype(BF))
            num_ref[b] += dot(jnp.concatenate(stacked, axis=0), weights)
        return carry

    lax.fori_loop(0, members // group, step, 0)
    totals = []
    for b in range(blocks):
        for t in range(4):
            rows = slice((b * 4 + t) * LANES, (b * 4 + t + 1) * LANES)
            value = jnp.concatenate(
                [
                    num_ref[b, t * LANES : t * LANES + half, :LANES],
                    num_ref[b, t * LANES + half : (t + 1) * LANES, LANES:],
                ],
                axis=0,
            )
            own_ref[rows, :] = value
            send_ref[rows, :] = value.astype(BF)
        for h in range(HEADS):
            totals.append(num_ref[b, 4 * LANES : 4 * LANES + 4, h * LANES : (h + 1) * LANES])
    totals = jnp.concatenate(totals, axis=0)
    own_ref[blocks * 4 * LANES :, :] = totals
    send_ref[blocks * 4 * LANES :, :] = totals.astype(BF)


def combine_kernel(blocks, own_ref, other_ref, inducing_ref, proj_ref, out_ref):
    half = LANES // HEADS
    last = blocks * 4 * LANES
    totals = own_ref[last:, :] + other_ref[last:, :].astype(F32)
    for b in range(blocks):
        for t in range(4):
            rows = slice((b * 4 + t) * LANES, (b * 4 + t + 1) * LANES)
            value = own_ref[rows, :] + other_ref[rows, :].astype(F32)
            line = b * HEADS * 4 + t
            attended = jnp.concatenate(
                [
                    value[:half] / totals[line : line + 1],
                    value[half:] / totals[line + 4 : line + 5],
                ],
                axis=0,
            )
            attended = attended.T.astype(BF)
            out = inducing_ref[...].astype(F32) + dot(attended, proj_ref[3])
            out_ref[t // 2, b * TLY + t % 2] = out.astype(BF)


def finish_kernel(
    along_y,
    summary_ref,
    column_ref,
    below_ref,
    above_ref,
    rows_ref,
    counts_ref,
    where_ref,
    proj_ref,
    mixing_ref,
    out_ref,
    mid_ref,
    side_ref,
    key_ref,
    value_ref,
):
    members, blocks, quota, width = rows_ref.shape
    grid_y = along_y * TLY
    half = LANES // HEADS
    group = min(512 // quota, members)
    chunk = group * quota
    low = where_ref[2]
    tall = summary_ref.shape[1]

    row = lax.broadcasted_iota(jnp.int32, (LANES, LANES), 0)
    col = lax.broadcasted_iota(jnp.int32, (LANES, LANES), 1)
    eye = jnp.where(row == col, 1.0, 0.0).astype(BF)
    blank = jnp.zeros((LANES, LANES), BF)

    def mix(a, b):
        return eye if (a, b) == (0, 0) else mixing_ref[neighbour_steps.index((a, b))]

    for k, a in enumerate((-1, 0, 1)):
        rows = slice(k * 2 * LANES, (k + 1) * 2 * LANES)
        mid_ref[rows, :] = jnp.concatenate(
            [
                jnp.concatenate([mix(a, 0), mix(a, -1)], axis=1),
                jnp.concatenate([mix(a, 1), mix(a, 0)], axis=1),
            ],
            axis=0,
        )
    for k, b in enumerate((-1, 1)):
        side_ref[k] = jnp.concatenate(
            [
                jnp.concatenate([mix(0, b), mix(-1, b)], axis=1),
                jnp.concatenate([mix(1, b), mix(0, b)], axis=1),
                jnp.concatenate([mix(-1, b), blank], axis=1),
                jnp.concatenate([blank, mix(1, b)], axis=1),
            ],
            axis=0,
        )
    ones = head_ones()
    lane = lax.broadcasted_iota(jnp.int32, (1, LANES), 1)
    left = lane < half

    def tile(i, j):
        if 0 <= j < tall:
            return below_ref[j] if i == 0 else above_ref[j] if i == 3 else summary_ref[i - 1, j]
        held = below_ref[tall] if i == 0 else above_ref[tall] if i == 3 else column_ref[i - 1]
        wanted = 1 if j < 0 else 0
        return jnp.where(low == wanted, held, blank)

    mids, lefts, rights = [], [], []
    for i in range(2):
        for b in range(blocks):
            mids.append(
                jnp.concatenate(
                    [tile(i + r, 2 * b + s) for r in range(3) for s in range(2)], axis=1
                )
            )
    for b in range(blocks):
        lefts.append(jnp.concatenate([tile(i, 2 * b - 1) for i in (1, 2, 0, 3)], axis=1))
        rights.append(jnp.concatenate([tile(i, 2 * b + 2) for i in (1, 2, 0, 3)], axis=1))
    middle = dot(jnp.concatenate(mids, axis=0), mid_ref[...])
    from_left = dot(jnp.concatenate(lefts, axis=0), side_ref[0])
    from_right = dot(jnp.concatenate(rights, axis=0), side_ref[1])
    mixtures = []
    for b in range(blocks):
        span = slice(b * LANES, (b + 1) * LANES)
        for i in range(2):
            m = middle[(i * blocks + b) * LANES : (i * blocks + b + 1) * LANES]
            cols = slice(i * LANES, (i + 1) * LANES)
            mixtures.append((m[:, :LANES] + from_left[span, cols]).astype(BF))
            mixtures.append((m[:, LANES:] + from_right[span, cols]).astype(BF))
    mixtures = jnp.concatenate(mixtures, axis=0)
    keys = unit(dot(mixtures, proj_ref[1]), ones)
    values = dot(mixtures, proj_ref[2])
    for b in range(blocks):
        spans = [slice((b * 4 + t) * LANES, (b * 4 + t + 1) * LANES) for t in range(4)]
        for h in range(HEADS):
            mine = left if h == 0 else ~left
            key_ref[b, h * LANES : (h + 1) * LANES, :] = jnp.concatenate(
                [jnp.where(mine, keys[s], 0.0) for s in spans], axis=1
            ).astype(BF)
            flags = jnp.broadcast_to(jnp.where(mine, 1.0, 0.0), (LANES, LANES))
            for t, s in enumerate(spans):
                rows = slice((t * HEADS + h) * LANES, (t * HEADS + h + 1) * LANES)
                value_ref[b, rows, :] = jnp.concatenate(
                    [jnp.where(mine, values[s], 0.0), flags], axis=1
                ).astype(BF)
    spot = lax.broadcasted_iota(jnp.int32, (chunk, LANES), 0)

    def step(c, carry):
        for b in range(blocks):
            x = jnp.concatenate([rows_ref[c * group + k, b] for k in range(group)], axis=0)
            query = unit(dot(x, proj_ref[0]), ones)
            base = tile_base(b, where_ref, blocks, grid_y)
            pieces = [
                (source_of(c * group + k, where_ref, along_y // blocks, along_y), base)
                for k in range(group)
            ]
            which = tile_of(spot % quota, counts_ref, pieces, spot // quota, grid_y)
            inside = [which == t for t in range(4)]
            expanded = jnp.concatenate(
                [jnp.where(m, query, 0.0).astype(BF) for m in inside], axis=1
            )
            scores = dot_t(expanded, key_ref[b])
            weights = jnp.exp2(scores * (sharpness * math.log2(math.e)))
            spread = jnp.concatenate(
                [
                    jnp.where(m, weights[:, h * LANES : (h + 1) * LANES], 0.0).astype(BF)
                    for m in inside
                    for h in range(HEADS)
                ],
                axis=1,
            )
            both = dot(spread, value_ref[b])
            attended = (both[:, :LANES] / both[:, LANES:]).astype(BF)
            result = (x.astype(F32) + dot(attended, proj_ref[3])).astype(BF)
            for k in range(group):
                out_ref[c * group + k, b] = result[k * quota : (k + 1) * quota]
        return carry

    lax.fori_loop(0, members // group, step, 0)


def scatter_kernel(rows_ref, index_ref, out_ref, wide_ref, part_ref):
    chunk = part_ref.shape[0]
    total = rows_ref.shape[0]

    def step(c, carry):
        start = pl.multiple_of(c * chunk, chunk)
        part_ref[...] = rows_ref[pl.ds(start, chunk), :].astype(F32)
        for r in range(chunk):
            i = index_ref[c * (chunk // LANES) + r // LANES, r % LANES]
            wide_ref[pl.ds(i, 1), :] = part_ref[pl.ds(r, 1), :]
        return carry

    lax.fori_loop(0, total // chunk, step, 0)
    out_ref[...] = wide_ref[...].astype(BF)


def spec(space):
    return pl.BlockSpec(memory_space=space)


def body(
    points,
    embed_weight,
    inner_weights,
    output_weight,
    counts,
    point_order,
    inducing,
    first_proj,
    second_proj,
    mixing,
):
    along_x = lax.axis_size("tx")
    highs = lax.axis_size("zh")
    lows = lax.axis_size("zl")
    along_y = highs * lows
    devices = along_x * along_y
    index_x = lax.axis_index("tx")
    index_h = lax.axis_index("zh")
    index_l = lax.axis_index("zl")
    own_index = index_x * along_y + index_h * lows + index_l
    point_count, width = points.shape
    quota = point_count // devices
    grid_y = along_y * TLY
    blocks = along_y // lows
    members = along_x * lows
    tall = blocks * TLY
    lines = point_count // LANES
    chunk = 512
    group_axes = ("tx", "zl")
    own_counts = lax.dynamic_index_in_dim(counts, own_index, 0, keepdims=False)
    position = jnp.stack([index_x, index_h, index_l]).astype(jnp.int32)
    limit = pltpu.CompilerParams(vmem_limit_bytes=56 * 1024 * 1024)

    features, index = pl.pallas_call(
        functools.partial(encode_kernel, grid_y, along_y, quota),
        out_shape=(
            jax.ShapeDtypeStruct((point_count, width), BF),
            jax.ShapeDtypeStruct((lines, LANES), jnp.int32),
        ),
        in_specs=[spec(VMEM)] * 4 + [spec(SMEM), spec(VMEM)],
        out_specs=(spec(VMEM), spec(VMEM)),
        scratch_shapes=[
            SMEM((counts.shape[1],), jnp.int32),
            SMEM((lines, LANES), jnp.int32),
            VMEM((point_count, width), F32),
            VMEM((chunk, width), F32),
            VMEM((chunk, width), F32),
            pltpu.SemaphoreType.DMA,
        ],
        compiler_params=limit,
        name="encode_points",
    )(
        points,
        embed_weight,
        inner_weights,
        output_weight,
        own_counts,
        point_order.reshape(lines, LANES),
    )

    arrived = lax.all_to_all(
        features.reshape(members, blocks * quota, width),
        group_axes,
        split_axis=0,
        concat_axis=0,
        tiled=True,
    ).reshape(members, blocks, quota, width)

    part_rows = blocks * 4 * LANES + blocks * HEADS * 4
    own, send = pl.pallas_call(
        functools.partial(partial_kernel, along_y),
        out_shape=(
            jax.ShapeDtypeStruct((part_rows, LANES), F32),
            jax.ShapeDtypeStruct((part_rows, LANES), BF),
        ),
        in_specs=[spec(VMEM), spec(SMEM), spec(SMEM), spec(VMEM), spec(VMEM)],
        out_specs=(spec(VMEM), spec(VMEM)),
        scratch_shapes=[VMEM((blocks, 4 * LANES + 16, HEADS * LANES), F32)],
        compiler_params=limit,
        name="partial_attention",
    )(arrived, counts, position, inducing, first_proj)

    other = lax.ppermute(send, "zh", [(i, highs - 1 - i) for i in range(highs)])

    summary = pl.pallas_call(
        functools.partial(combine_kernel, blocks),
        out_shape=jax.ShapeDtypeStruct((TLX, tall, LANES, width), BF),
        in_specs=[spec(VMEM)] * 4,
        out_specs=spec(VMEM),
        compiler_params=limit,
        name="combine_partials",
    )(own, other, inducing, first_proj)

    edge = jnp.where(index_l == 0, summary[:, tall - 1], summary[:, 0])
    column = lax.ppermute(edge, "zl", [(i, lows - 1 - i) for i in range(lows)])
    wider = jnp.concatenate([summary, column[:, None]], axis=1)
    forward = [(i, i + 1) for i in range(along_x - 1)]
    backward = [(i + 1, i) for i in range(along_x - 1)]
    below = lax.ppermute(wider[TLX - 1], "tx", forward)
    above = lax.ppermute(wider[0], "tx", backward)

    result = pl.pallas_call(
        functools.partial(finish_kernel, along_y),
        out_shape=jax.ShapeDtypeStruct((members, blocks, quota, width), BF),
        in_specs=[spec(VMEM)] * 5 + [spec(SMEM)] * 2 + [spec(VMEM)] * 2,
        out_specs=spec(VMEM),
        scratch_shapes=[
            VMEM((6 * LANES, 2 * LANES), BF),
            VMEM((2, 4 * LANES, 2 * LANES), BF),
            VMEM((blocks, HEADS * LANES, 4 * LANES), BF),
            VMEM((blocks, 4 * HEADS * LANES, 2 * LANES), BF),
        ],
        compiler_params=limit,
        name="finish_rows",
    )(summary, column, below, above, arrived, counts, position, second_proj, mixing)

    returned = lax.all_to_all(
        result.reshape(members, blocks * quota, width),
        group_axes,
        split_axis=0,
        concat_axis=0,
        tiled=True,
    ).reshape(point_count, width)

    return pl.pallas_call(
        scatter_kernel,
        out_shape=jax.ShapeDtypeStruct((point_count, width), BF),
        in_specs=[spec(VMEM), spec(SMEM)],
        out_specs=spec(VMEM),
        scratch_shapes=[VMEM((point_count, width), F32), VMEM((chunk, width), F32)],
        compiler_params=limit,
        name="scatter_rows",
    )(returned, index)


def solution(mesh):
    along_x, along_y = mesh.devices.shape
    split = jax.sharding.Mesh(mesh.devices.reshape(along_x, 2, along_y // 2), ("tx", "zh", "zl"))
    rows = P(("tx", "zh", "zl"), None)
    placed = (rows, P(), P(), P(), P(), rows, P(), P(), P(), P())
    return jax.shard_map(body, mesh=split, in_specs=placed, out_specs=rows, check_vma=False)
```

```python
import functools
import math

import jax
import jax.numpy as jnp
from jax import lax
from jax.experimental import pallas as pl
from jax.experimental.pallas import tpu as pltpu
from jax.sharding import PartitionSpec as P

HEADS = 2
TLX = 2
TLY = 2
LANES = 128
BF = jnp.bfloat16
F32 = jnp.float32

sharpness = 32.0
epsilon = 1e-06
neighbour_steps = ((-1, -1), (-1, 0), (-1, 1), (0, -1), (0, 1), (1, -1), (1, 0), (1, 1))
VMEM = pltpu.VMEM
SMEM = pltpu.SMEM


def dot(a, b):
    return jnp.dot(a, b, preferred_element_type=F32)


def dot_t(a, b):
    return lax.dot_general(a, b, (((1,), (1,)), ((), ())), preferred_element_type=F32)


def head_ones():
    row = lax.broadcasted_iota(jnp.int32, (2 * LANES, LANES), 0)
    col = lax.broadcasted_iota(jnp.int32, (2 * LANES, LANES), 1)
    half = LANES // HEADS
    same = ((row % LANES) // half) == (col // half)
    return jnp.where(same, 1.0, 0.0).astype(BF)


def unit(v, ones):
    square = v * v
    high = square.astype(BF)
    low = (square - high.astype(F32)).astype(BF)
    total = dot(jnp.concatenate([high, low], axis=1), ones)
    return v * lax.rsqrt(total + epsilon)


def silu(v):
    half = 0.5 * v
    return half + half * jnp.tanh(half)


def place():
    return lax.axis_index("tx"), lax.axis_index("zh"), lax.axis_index("zl")


def network(x, w1_ref, w2_ref, w3_ref):
    hidden = silu(dot(x.astype(BF), w1_ref[...])).astype(BF)
    hidden = silu(dot(hidden, w2_ref[0])).astype(BF)
    return dot(hidden, w3_ref[...]).astype(BF)


def encode_rows(
    half_id, quota, chunk, points_ref, w1_ref, w2_ref, w3_ref, index_s, feat_ref, wide_ref, xs
):
    rows_total = points_ref.shape[0] // 2
    group = chunk // quota
    wide_ref[...] = points_ref[...].astype(F32)

    def gather(c, buffer):
        for r in range(chunk):
            spot = (r // quota) * 2 * quota + half_id * quota + r % quota
            i = index_s[c * (2 * chunk // LANES) + spot // LANES, spot % LANES]
            buffer[pl.ds(r, 1), :] = wide_ref[pl.ds(i, 1), :]

    def apply(c, buffer):
        out = network(buffer[...], w1_ref, w2_ref, w3_ref)
        for k in range(group):
            feat_ref[c * group + k] = out[k * quota : (k + 1) * quota]

    chunks = rows_total // chunk
    gather(0, xs[0])

    def step(k, carry):
        c = 2 * k
        gather(c + 1, xs[1])
        apply(c, xs[0])
        gather(jnp.minimum(c + 2, chunks - 1), xs[0])
        apply(c + 1, xs[1])
        return carry

    lax.fori_loop(0, chunks // 2, step, 0)


def encode_first_kernel(
    grid_y,
    along_y,
    quota,
    points_ref,
    w1_ref,
    w2_ref,
    w3_ref,
    counts_ref,
    order_ref,
    feat_ref,
    index_ref,
    off_ref,
    index_s,
    wide_ref,
    xa_ref,
    xb_ref,
    sem,
):
    tx, zh, zl = place()
    own = tx * along_y + zh * (along_y // 2) + zl
    tiles = counts_ref.shape[1]
    order_rows = order_ref.shape[0]
    rows_total = points_ref.shape[0]

    def add_up(g, total):
        off_ref[g] = total
        return total + counts_ref[own, g]

    lax.fori_loop(0, tiles, add_up, jnp.int32(0), unroll=8)
    lane = lax.broadcasted_iota(jnp.int32, (1, LANES), 1)

    def run_of(start):
        line = start >> 7
        shift = start & (LANES - 1)
        first = order_ref[pl.ds(jnp.clip(line, 0, order_rows - 1), 1), :]
        second = order_ref[pl.ds(jnp.clip(line + 1, 0, order_rows - 1), 1), :]
        merged = jnp.where(lane < shift, second, first)
        return pltpu.roll(merged, (LANES - shift) & (LANES - 1), 1)

    per_line = LANES // quota

    def index_line(line, carry):
        value = jnp.zeros((1, LANES), jnp.int32)
        for k in range(per_line):
            d = line * per_line + k
            g1 = (d // along_y) * (TLX * grid_y) + (d % along_y) * TLY
            n1 = counts_ref[own, g1] + counts_ref[own, g1 + 1]
            run1 = run_of(off_ref[g1] - k * quota)
            run2 = run_of(off_ref[g1 + grid_y] - n1 - k * quota)
            both = jnp.where(lane < k * quota + n1, run1, run2)
            value = both if k == 0 else jnp.where(lane >= k * quota, both, value)
        index_ref[pl.ds(line, 1), :] = value
        return carry

    lax.fori_loop(0, rows_total // LANES, index_line, 0, unroll=4)
    copy = pltpu.make_async_copy(index_ref, index_s, sem)
    copy.start()
    copy.wait()
    encode_rows(
        0, quota, xa_ref.shape[0], points_ref, w1_ref, w2_ref, w3_ref, index_s, feat_ref, wide_ref,
        (xa_ref, xb_ref),
    )


def encode_second_kernel(
    quota, points_ref, w1_ref, w2_ref, w3_ref, index_ref, feat_ref, wide_ref, xa_ref, xb_ref
):
    encode_rows(
        1, quota, xa_ref.shape[0], points_ref, w1_ref, w2_ref, w3_ref, index_ref, feat_ref, wide_ref,
        (xa_ref, xb_ref),
    )


def tile_of(position, counts_ref, pieces, piece_id, grid_y):
    bounds = [None, None, None]
    for k, (s, base) in enumerate(pieces):
        n0 = counts_ref[s, base]
        n1 = counts_ref[s, base + 1]
        n2 = counts_ref[s, base + grid_y]
        for i, found in enumerate((n0, n0 + n1, n0 + n1 + n2)):
            if k == 0:
                bounds[i] = jnp.full(position.shape, found, jnp.int32)
            else:
                bounds[i] = jnp.where(piece_id >= k, found, bounds[i])
    return sum((position >= b).astype(jnp.int32) for b in bounds)


def pieces_of(first, group, half_id, along_y):
    tx, zh, zl = place()
    lows = along_y // 2
    blocks = 2
    base = tx * (TLX * along_y * TLY) + (zl * blocks + half_id) * TLY
    found = []
    for k in range(group):
        member = first + k
        found.append(((member // lows) * along_y + zh * lows + member % lows, base))
    return found


def partial_kernel(half_id, along_y, rows_ref, counts_ref, inducing_ref, proj_ref, *rest):
    if half_id:
        before_ref, own_ref, send_ref, edge_ref, num_ref = rest
    else:
        own_ref, send_ref, num_ref = rest
    members, quota, width = rows_ref.shape
    grid_y = along_y * TLY
    half = LANES // HEADS
    group = min(512 // quota, members)
    chunk = group * quota
    ones = head_ones()
    lane = lax.broadcasted_iota(jnp.int32, (1, LANES), 1)
    left = lane < half
    queries = unit(dot(inducing_ref[...], proj_ref[0]), ones)
    queries = jnp.concatenate(
        [jnp.where(left, queries, 0.0), jnp.where(left, 0.0, queries)], axis=0
    ).astype(BF)
    wv_t = proj_ref[2].astype(F32).T.astype(BF)
    num_ref[...] = jnp.zeros_like(num_ref)
    spot = lax.broadcasted_iota(jnp.int32, (1, chunk), 1)
    tile_row = lax.broadcasted_iota(jnp.int32, (16, chunk), 0)

    def step(c, carry):
        x = jnp.concatenate([rows_ref[c * group + k] for k in range(group)], axis=0)
        keys = unit(dot(x, proj_ref[1]), ones).astype(BF)
        weights = jnp.exp2(dot_t(keys, queries) * (sharpness * math.log2(math.e))).astype(BF)
        values = dot_t(wv_t, x)
        pieces = pieces_of(c * group, group, half_id, along_y)
        tile = tile_of(spot % quota, counts_ref, pieces, spot // quota, grid_y)
        stacked = [jnp.where(tile == t, values, 0.0).astype(BF) for t in range(4)]
        stacked.append(jnp.where(tile_row == tile, 1.0, 0.0).astype(BF))
        num_ref[...] += dot(jnp.concatenate(stacked, axis=0), weights)
        return carry

    lax.fori_loop(0, members // group, step, 0)
    pad = jnp.zeros((8, LANES), F32)
    last = 4 * LANES

    def tile_sums(t):
        return jnp.concatenate(
            [
                num_ref[t * LANES : t * LANES + half, :LANES],
                num_ref[t * LANES + half : (t + 1) * LANES, LANES:],
            ],
            axis=0,
        )

    for t in range(4):
        rows = slice(t * LANES, (t + 1) * LANES)
        value = tile_sums(t)
        own_ref[rows, :] = value
        send_ref[rows, :] = value.astype(BF)
    totals = jnp.concatenate(
        [num_ref[last : last + 4, h * LANES : (h + 1) * LANES] for h in range(HEADS)] + [pad],
        axis=0,
    )
    own_ref[last:, :] = totals
    send_ref[last:, :] = totals.astype(BF)
    if half_id:
        zl = lax.axis_index("zl")
        for x in range(TLX):
            rows = slice(x * LANES, (x + 1) * LANES)
            here = send_ref[(2 * x + 1) * LANES : (2 * x + 2) * LANES, :]
            there = before_ref[2 * x * LANES : (2 * x + 1) * LANES, :]
            edge_ref[rows, :] = jnp.where(zl == 0, here, there)
        edge_ref[TLX * LANES :, :] = jnp.where(zl == 0, send_ref[last:, :], before_ref[last:, :])


def queries_kernel(rows0_ref, rows1_ref, proj_ref, out0_ref, out1_ref):
    ones = head_ones()
    for rows_ref, out_ref in ((rows0_ref, out0_ref), (rows1_ref, out1_ref)):
        members, quota, width = rows_ref.shape
        group = min(512 // quota, members)

        def step(c, carry):
            x = jnp.concatenate([rows_ref[c * group + k] for k in range(group)], axis=0)
            query = unit(dot(x, proj_ref[0]), ones).astype(BF)
            for k in range(group):
                out_ref[c * group + k] = query[k * quota : (k + 1) * quota]
            return carry

        lax.fori_loop(0, members // group, step, 0)


def combine_kernel(
    own0_ref, own1_ref, other0_ref, other1_ref, near_ref, far_ref, inducing_ref, proj_ref, out0_ref, out1_ref
):
    half = LANES // HEADS
    last = 4 * LANES
    outs = (out0_ref, out1_ref)
    zl = lax.axis_index("zl")

    def summarize(value, total0, total1):
        attended = jnp.concatenate([value[:half] / total0, value[half:] / total1], axis=0)
        attended = attended.T.astype(BF)
        out = inducing_ref[...].astype(F32) + dot(attended, proj_ref[3])
        return out.astype(BF)

    for b, (own_ref, other_ref) in enumerate(((own0_ref, other0_ref), (own1_ref, other1_ref))):
        totals = own_ref[last:, :] + other_ref[last:, :].astype(F32)
        for t in range(4):
            rows = slice(t * LANES, (t + 1) * LANES)
            value = own_ref[rows, :] + other_ref[rows, :].astype(F32)
            outs[t // 2][b * TLY + t % 2] = summarize(
                value, totals[t : t + 1], totals[t + 4 : t + 5]
            )
    totals = near_ref[TLX * LANES :, :].astype(F32) + far_ref[TLX * LANES :, :].astype(F32)
    for x in range(TLX):
        rows = slice(x * LANES, (x + 1) * LANES)
        value = near_ref[rows, :].astype(F32) + far_ref[rows, :].astype(F32)
        lines = [
            jnp.where(zl == 1, totals[k + 1 : k + 2], totals[k : k + 1])
            for k in (2 * x, 2 * x + 4)
        ]
        outs[x][2 * TLY] = summarize(value, *lines)


def mixture_kernel(
    own0_ref,
    own1_ref,
    below_ref,
    above_ref,
    proj_ref,
    mixing_ref,
    key_ref,
    value_ref,
    mid_ref,
    side_ref,
):
    half = LANES // HEADS
    blocks = key_ref.shape[0]
    tall = blocks * TLY
    low = lax.axis_index("zl")

    row = lax.broadcasted_iota(jnp.int32, (LANES, LANES), 0)
    col = lax.broadcasted_iota(jnp.int32, (LANES, LANES), 1)
    eye = jnp.where(row == col, 1.0, 0.0).astype(BF)
    blank = jnp.zeros((LANES, LANES), BF)

    def mix(a, b):
        return eye if (a, b) == (0, 0) else mixing_ref[neighbour_steps.index((a, b))]

    for k, a in enumerate((-1, 0, 1)):
        rows = slice(k * 2 * LANES, (k + 1) * 2 * LANES)
        mid_ref[rows, :] = jnp.concatenate(
            [
                jnp.concatenate([mix(a, 0), mix(a, -1)], axis=1),
                jnp.concatenate([mix(a, 1), mix(a, 0)], axis=1),
            ],
            axis=0,
        )
    for k, b in enumerate((-1, 1)):
        side_ref[k] = jnp.concatenate(
            [
                jnp.concatenate([mix(0, b), mix(-1, b)], axis=1),
                jnp.concatenate([mix(1, b), mix(0, b)], axis=1),
                jnp.concatenate([mix(-1, b), blank], axis=1),
                jnp.concatenate([blank, mix(1, b)], axis=1),
            ],
            axis=0,
        )
    ones = head_ones()
    lane = lax.broadcasted_iota(jnp.int32, (1, LANES), 1)
    left = lane < half
    grid = (below_ref, own0_ref, own1_ref, above_ref)

    def tile(i, j):
        if 0 <= j < tall:
            return grid[i][j]
        return jnp.where(low == (1 if j < 0 else 0), grid[i][tall], blank)

    mids, lefts, rights = [], [], []
    for i in range(2):
        for b in range(blocks):
            mids.append(
                jnp.concatenate(
                    [tile(i + r, 2 * b + s) for r in range(3) for s in range(2)], axis=1
                )
            )
    for b in range(blocks):
        lefts.append(jnp.concatenate([tile(i, 2 * b - 1) for i in (1, 2, 0, 3)], axis=1))
        rights.append(jnp.concatenate([tile(i, 2 * b + 2) for i in (1, 2, 0, 3)], axis=1))
    middle = dot(jnp.concatenate(mids, axis=0), mid_ref[...])
    from_left = dot(jnp.concatenate(lefts, axis=0), side_ref[0])
    from_right = dot(jnp.concatenate(rights, axis=0), side_ref[1])
    mixtures = []
    for b in range(blocks):
        span = slice(b * LANES, (b + 1) * LANES)
        for i in range(2):
            m = middle[(i * blocks + b) * LANES : (i * blocks + b + 1) * LANES]
            cols = slice(i * LANES, (i + 1) * LANES)
            mixtures.append((m[:, :LANES] + from_left[span, cols]).astype(BF))
            mixtures.append((m[:, LANES:] + from_right[span, cols]).astype(BF))
    mixtures = jnp.concatenate(mixtures, axis=0)
    keys = unit(dot(mixtures, proj_ref[1]), ones)
    values = dot(mixtures, proj_ref[2])
    for b in range(blocks):
        spans = [slice((b * 4 + t) * LANES, (b * 4 + t + 1) * LANES) for t in range(4)]
        for h in range(HEADS):
            mine = left if h == 0 else ~left
            key_ref[b, h * LANES : (h + 1) * LANES, :] = jnp.concatenate(
                [jnp.where(mine, keys[s], 0.0) for s in spans], axis=1
            ).astype(BF)
            flags = jnp.broadcast_to(jnp.where(mine, 1.0, 0.0), (LANES, LANES))
            for t, s in enumerate(spans):
                rows = slice((t * HEADS + h) * LANES, (t * HEADS + h + 1) * LANES)
                value_ref[b, rows, :] = jnp.concatenate(
                    [jnp.where(mine, values[s], 0.0), flags], axis=1
                ).astype(BF)


def attend_kernel(
    half_id, along_y, rows_ref, query_ref, counts_ref, key_ref, value_ref, proj_ref, out_ref
):
    members, quota, width = rows_ref.shape
    grid_y = along_y * TLY
    group = min(512 // quota, members)
    chunk = group * quota
    spot = lax.broadcasted_iota(jnp.int32, (chunk, LANES), 0)

    def step(c, carry):
        x = jnp.concatenate([rows_ref[c * group + k] for k in range(group)], axis=0)
        query = jnp.concatenate([query_ref[c * group + k] for k in range(group)], axis=0)
        query = query.astype(F32)
        pieces = pieces_of(c * group, group, half_id, along_y)
        which = tile_of(spot % quota, counts_ref, pieces, spot // quota, grid_y)
        inside = [which == t for t in range(4)]
        expanded = jnp.concatenate(
            [jnp.where(m, query, 0.0).astype(BF) for m in inside], axis=1
        )
        scores = dot_t(expanded, key_ref[half_id])
        weights = jnp.exp2(scores * (sharpness * math.log2(math.e)))
        spread = jnp.concatenate(
            [
                jnp.where(m, weights[:, h * LANES : (h + 1) * LANES], 0.0).astype(BF)
                for m in inside
                for h in range(HEADS)
            ],
            axis=1,
        )
        both = dot(spread, value_ref[half_id])
        attended = (both[:, :LANES] / both[:, LANES:]).astype(BF)
        result = (x.astype(F32) + dot(attended, proj_ref[3])).astype(BF)
        for k in range(group):
            out_ref[c * group + k] = result[k * quota : (k + 1) * quota]
        return carry

    lax.fori_loop(0, members // group, step, 0)


def scatter_rows(half_id, rows_ref, index_ref, wide_ref, part_ref):
    chunk = part_ref.shape[0]
    members, quota, width = rows_ref.shape
    group = chunk // quota

    def step(c, carry):
        for k in range(group):
            part_ref[k * quota : (k + 1) * quota, :] = rows_ref[c * group + k].astype(F32)
        for r in range(chunk):
            spot = (r // quota) * 2 * quota + half_id * quota + r % quota
            i = index_ref[c * (2 * chunk // LANES) + spot // LANES, spot % LANES]
            wide_ref[pl.ds(i, 1), :] = part_ref[pl.ds(r, 1), :]
        return carry

    lax.fori_loop(0, members // group, step, 0)


def scatter_first_kernel(rows_ref, index_ref, wide_ref, part_ref):
    scatter_rows(0, rows_ref, index_ref, wide_ref, part_ref)


def scatter_second_kernel(rows_ref, index_ref, before_ref, out_ref, wide_ref, part_ref):
    wide_ref[...] = before_ref[...]
    scatter_rows(1, rows_ref, index_ref, wide_ref, part_ref)
    out_ref[...] = wide_ref[...].astype(BF)


def call(kernel, name, out_shape, in_specs, scratch, micros, operands, megabytes=20, **more):
    spaces = {"v": pltpu.VMEM, "s": pltpu.SMEM}
    many = isinstance(out_shape, tuple)
    whole = pl.BlockSpec(memory_space=pltpu.VMEM)
    return pl.pallas_call(
        kernel,
        out_shape=out_shape,
        in_specs=[pl.BlockSpec(memory_space=spaces[c]) for c in in_specs],
        out_specs=(whole,) * len(out_shape) if many else whole,
        scratch_shapes=scratch,
        compiler_params=pltpu.CompilerParams(vmem_limit_bytes=megabytes * 1024 * 1024),
        cost_estimate=pl.CostEstimate(
            flops=int(micros * 5e8), bytes_accessed=int(micros * 1e6), transcendentals=0
        ),
        name=name,
        **more,
    )(*operands)


def body(
    points,
    embed_weight,
    inner_weights,
    output_weight,
    counts,
    point_order,
    inducing,
    first_proj,
    second_proj,
    mixing,
):
    along_x = lax.axis_size("tx")
    highs = lax.axis_size("zh")
    lows = lax.axis_size("zl")
    along_y = highs * lows
    point_count, width = points.shape
    quota = point_count // (along_x * along_y)
    grid_y = along_y * TLY
    blocks = 2
    members = along_x * lows
    tall = blocks * TLY
    lines = point_count // LANES
    chunk = 512
    half_rows = (members, quota, width)

    def shape(sizes, dtype=BF):
        return jax.ShapeDtypeStruct(sizes, dtype)

    weights = (embed_weight, inner_weights, output_weight)
    buffers = [
        VMEM((point_count, width), F32),
        VMEM((chunk, width), F32),
        VMEM((chunk, width), F32),
    ]
    first, index = call(
        functools.partial(encode_first_kernel, grid_y, along_y, quota),
        "encode_first",
        (shape(half_rows), shape((lines, LANES), jnp.int32)),
        "vvvvsv",
        [SMEM((counts.shape[1],), jnp.int32), SMEM((lines, LANES), jnp.int32)]
        + buffers
        + [pltpu.SemaphoreType.DMA],
        8,
        (points, *weights, counts, point_order.reshape(lines, LANES)),
    )
    second = call(
        functools.partial(encode_second_kernel, quota),
        "encode_second",
        shape(half_rows),
        "vvvvs",
        buffers,
        6,
        (points, *weights, index),
    )

    def exchange(rows):
        return lax.all_to_all(rows, ("tx", "zl"), split_axis=0, concat_axis=0, tiled=True)

    rows0 = exchange(first)
    rows1 = exchange(second)

    part_rows = 4 * LANES + 16
    edge_rows = TLX * LANES + 16
    parts = (shape((part_rows, LANES), F32), shape((part_rows, LANES)))
    sums = [VMEM((part_rows, HEADS * LANES), F32)]
    own0, send0 = call(
        functools.partial(partial_kernel, 0, along_y),
        "partial_first",
        parts,
        "vsvv",
        sums,
        4,
        (rows0, counts, inducing, first_proj),
    )
    own1, send1, edge = call(
        functools.partial(partial_kernel, 1, along_y),
        "partial_second",
        parts + (shape((edge_rows, LANES)),),
        "vsvvv",
        sums,
        4,
        (rows1, counts, inducing, first_proj, send0),
    )
    across = [(h * lows + l, (highs - 1 - h) * lows + l) for h in range(highs) for l in range(lows)]
    beside = [(h * lows + l, h * lows + lows - 1 - l) for h in range(highs) for l in range(lows)]
    both = [
        (h * lows + l, (highs - 1 - h) * lows + lows - 1 - l)
        for h in range(highs)
        for l in range(lows)
    ]
    z_axes = ("zh", "zl")
    other0 = lax.ppermute(send0, z_axes, across)
    other1 = lax.ppermute(send1, z_axes, across)
    near = lax.ppermute(edge, z_axes, beside)
    far = lax.ppermute(edge, z_axes, both)

    query0, query1 = call(
        queries_kernel,
        "point_queries",
        (shape(half_rows), shape(half_rows)),
        "vvv",
        [],
        3,
        (rows0, rows1, second_proj),
    )

    line = shape((tall + 1, LANES, width))
    summary0, summary1 = call(
        combine_kernel,
        "combine_partials",
        (line, line),
        "v" * 8,
        [],
        2,
        (own0, own1, other0, other1, near, far, inducing, first_proj),
    )
    forward = [(i, i + 1) for i in range(along_x - 1)]
    backward = [(i + 1, i) for i in range(along_x - 1)]
    below = lax.ppermute(summary1, "tx", forward)
    above = lax.ppermute(summary0, "tx", backward)

    keys, values = call(
        mixture_kernel,
        "mix_tiles",
        (shape((blocks, HEADS * LANES, 4 * LANES)), shape((blocks, 4 * HEADS * LANES, 2 * LANES))),
        "v" * 6,
        [VMEM((6 * LANES, 2 * LANES), BF), VMEM((2, 4 * LANES, 2 * LANES), BF)],
        4,
        (summary0, summary1, below, above, second_proj, mixing),
    )

    def attend(half_id, rows, query):
        return call(
            functools.partial(attend_kernel, half_id, along_y),
            ("attend_first", "attend_second")[half_id],
            shape(half_rows),
            "vvsvvv",
            [],
            4,
            (rows, query, counts, keys, values, second_proj),
        )

    back0 = exchange(attend(0, rows0, query0))
    back1 = exchange(attend(1, rows1, query1))
    wide = call(
        scatter_first_kernel,
        "scatter_first",
        shape((point_count, width), F32),
        "vs",
        [VMEM((chunk, width), F32)],
        3,
        (back0, index),
    )
    return call(
        scatter_second_kernel,
        "scatter_second",
        shape((point_count, width)),
        "vsv",
        [VMEM((point_count, width), F32), VMEM((chunk, width), F32)],
        4,
        (back1, index, wide),
    )


def solution(mesh):
    along_x, along_y = mesh.devices.shape
    split = jax.sharding.Mesh(mesh.devices.reshape(along_x, 2, along_y // 2), ("tx", "zh", "zl"))
    rows = P(("tx", "zh", "zl"), None)
    placed = (rows, P(), P(), P(), P(), rows, P(), P(), P(), P())
    return jax.shard_map(body, mesh=split, in_specs=placed, out_specs=rows, check_vma=False)
```

```python
import functools
import math

import jax
import jax.numpy as jnp
from jax import lax
from jax.experimental import pallas as pl
from jax.experimental.pallas import tpu as pltpu
from jax.sharding import PartitionSpec as P

HEADS = 2
TLX = 2
TLY = 2
LANES = 128
BF = jnp.bfloat16
F32 = jnp.float32

sharpness = 32.0
epsilon = 1e-06
neighbour_steps = ((-1, -1), (-1, 0), (-1, 1), (0, -1), (0, 1), (1, -1), (1, 0), (1, 1))
VMEM = pltpu.VMEM
SMEM = pltpu.SMEM


def dot(a, b):
    return jnp.dot(a, b, preferred_element_type=F32)


def dot_t(a, b):
    return lax.dot_general(a, b, (((1,), (1,)), ((), ())), preferred_element_type=F32)


def head_ones():
    row = lax.broadcasted_iota(jnp.int32, (2 * LANES, LANES), 0)
    col = lax.broadcasted_iota(jnp.int32, (2 * LANES, LANES), 1)
    half = LANES // HEADS
    same = ((row % LANES) // half) == (col // half)
    return jnp.where(same, 1.0, 0.0).astype(BF)


def unit(v, ones):
    square = v * v
    high = square.astype(BF)
    low = (square - high.astype(F32)).astype(BF)
    total = dot(jnp.concatenate([high, low], axis=1), ones)
    return v * lax.rsqrt(total + epsilon)


def silu(v):
    half = 0.5 * v
    return half + half * jnp.tanh(half)


def place():
    return lax.axis_index("tx"), lax.axis_index("zh"), lax.axis_index("zl")


def block_of(half_id, low):
    return low if half_id else 1 - low


def encode_rows(half_id, quota, chunk, points, weights_ready, w1_ref, w2_ref, w3_ref, index_s, feat_ref, wide_ref, xs):
    rows_total = points.shape[0] // 2
    group = chunk // quota
    wide_ref[...] = points[...].astype(F32)

    def gather(c, buffer, first, last):
        for r in range(first, last):
            member = r // quota
            spot = (member * 2 + block_of(half_id, member % 2)) * quota + r % quota
            i = index_s[c * (2 * chunk // LANES) + spot // LANES, spot % LANES]
            buffer[pl.ds(r, 1), :] = wide_ref[pl.ds(i, 1), :]

    def apply(c, buffer, ahead):
        cuts = [chunk * k // 4 for k in range(5)]
        ahead(cuts[0], cuts[1])
        hidden = silu(dot(buffer[...].astype(BF), w1_ref[...])).astype(BF)
        ahead(cuts[1], cuts[3])
        hidden = silu(dot(hidden, w2_ref[0])).astype(BF)
        ahead(cuts[3], cuts[4])
        out = dot(hidden, w3_ref[...]).astype(BF)
        for k in range(group):
            feat_ref[c * group + k] = out[k * quota : (k + 1) * quota]

    chunks = rows_total // chunk
    gather(0, xs[0], 0, chunk)
    weights_ready()

    def step(k, carry):
        c = 2 * k
        apply(c, xs[0], lambda a, b: gather(c + 1, xs[1], a, b))
        apply(c + 1, xs[1], lambda a, b: gather(jnp.minimum(c + 2, chunks - 1), xs[0], a, b))
        return carry

    lax.fori_loop(0, chunks // 2, step, 0)


def encode_first_kernel(
    grid_y,
    along_y,
    quota,
    points_hbm,
    w1_hbm,
    w2_hbm,
    w3_hbm,
    counts_hbm,
    order_hbm,
    feat_ref,
    index_ref,
    counts_s,
    off_ref,
    index_s,
    wide_ref,
    xa_ref,
    xb_ref,
    points_ref,
    w1_ref,
    w2_ref,
    w3_ref,
    order_ref,
    sems,
):
    tx, zh, zl = place()
    own = tx * along_y + zh * (along_y // 2) + zl
    sources = (counts_hbm.at[own], order_hbm, points_hbm, w1_hbm, w2_hbm, w3_hbm)
    targets = (counts_s, order_ref, points_ref, w1_ref, w2_ref, w3_ref)
    copies = [
        pltpu.make_async_copy(a, b, sems.at[k]) for k, (a, b) in enumerate(zip(sources, targets))
    ]
    for copy in copies:
        copy.start()
    tiles = counts_s.shape[0]
    order_rows = order_ref.shape[0]
    rows_total = points_ref.shape[0]
    copies[0].wait()

    def add_up(g, total):
        off_ref[g] = total
        return total + counts_s[g]

    lax.fori_loop(0, tiles, add_up, jnp.int32(0), unroll=8)
    copies[1].wait()
    lane = lax.broadcasted_iota(jnp.int32, (1, LANES), 1)

    def run_of(start):
        line = start >> 7
        shift = start & (LANES - 1)
        first = order_ref[pl.ds(jnp.clip(line, 0, order_rows - 1), 1), :]
        second = order_ref[pl.ds(jnp.clip(line + 1, 0, order_rows - 1), 1), :]
        merged = jnp.where(lane < shift, second, first)
        return pltpu.roll(merged, (LANES - shift) & (LANES - 1), 1)

    per_line = LANES // quota

    def index_line(line, carry):
        value = jnp.zeros((1, LANES), jnp.int32)
        for k in range(per_line):
            d = line * per_line + k
            g1 = (d // along_y) * (TLX * grid_y) + (d % along_y) * TLY
            n1 = counts_s[g1] + counts_s[g1 + 1]
            run1 = run_of(off_ref[g1] - k * quota)
            run2 = run_of(off_ref[g1 + grid_y] - n1 - k * quota)
            both = jnp.where(lane < k * quota + n1, run1, run2)
            value = both if k == 0 else jnp.where(lane >= k * quota, both, value)
        index_ref[pl.ds(line, 1), :] = value
        return carry

    lax.fori_loop(0, rows_total // LANES, index_line, 0, unroll=8)
    copy = pltpu.make_async_copy(index_ref, index_s, sems.at[6])
    copy.start()
    copies[2].wait()
    copy.wait()

    def weights_ready():
        for k in (3, 4, 5):
            copies[k].wait()

    encode_rows(
        0, quota, xa_ref.shape[0], points_ref, weights_ready, w1_ref, w2_ref, w3_ref, index_s,
        feat_ref, wide_ref, (xa_ref, xb_ref),
    )


def encode_second_kernel(
    quota, points_ref, w1_ref, w2_ref, w3_ref, index_ref, feat_ref, wide_ref, xa_ref, xb_ref
):
    encode_rows(
        1, quota, xa_ref.shape[0], points_ref, lambda: None, w1_ref, w2_ref, w3_ref, index_ref,
        feat_ref, wide_ref, (xa_ref, xb_ref),
    )


def tile_of(position, counts_ref, pieces, piece_id, grid_y):
    bounds = [None, None, None]
    for k, (s, base) in enumerate(pieces):
        n0 = counts_ref[s, base]
        n1 = counts_ref[s, base + 1]
        n2 = counts_ref[s, base + grid_y]
        for i, found in enumerate((n0, n0 + n1, n0 + n1 + n2)):
            if k == 0:
                bounds[i] = jnp.full(position.shape, found, jnp.int32)
            else:
                bounds[i] = jnp.where(piece_id >= k, found, bounds[i])
    return sum((position >= b).astype(jnp.int32) for b in bounds)


def pieces_of(first, group, half_id, along_y):
    tx, zh, zl = place()
    lows = along_y // 2
    block = zl * 2 + block_of(half_id, zl)
    base = tx * (TLX * along_y * TLY) + block * TLY
    found = []
    for k in range(group):
        member = first + k
        found.append(((member // lows) * along_y + zh * lows + member % lows, base))
    return found


def partial_kernel(half_id, along_y, rows_ref, counts_ref, inducing_ref, proj_ref, *rest):
    own_ref, send_ref = rest[:2]
    num_ref = rest[-1]
    members, quota, width = rows_ref.shape
    grid_y = along_y * TLY
    half = LANES // HEADS
    group = min(512 // quota, members)
    chunk = group * quota
    ones = head_ones()
    lane = lax.broadcasted_iota(jnp.int32, (1, LANES), 1)
    left = lane < half
    queries = unit(dot(inducing_ref[...], proj_ref[0]), ones)
    queries = jnp.concatenate(
        [jnp.where(left, queries, 0.0), jnp.where(left, 0.0, queries)], axis=0
    ).astype(BF)
    wv_t = proj_ref[2].astype(F32).T.astype(BF)
    spot = lax.broadcasted_iota(jnp.int32, (16, chunk), 1)
    tile_row = lax.broadcasted_iota(jnp.int32, (16, chunk), 0)
    for c in range(members // group):
        x = jnp.concatenate([rows_ref[c * group + k] for k in range(group)], axis=0)
        keys = unit(dot(x, proj_ref[1]), ones).astype(BF)
        weights = jnp.exp2(dot_t(keys, queries) * (sharpness * math.log2(math.e))).astype(BF)
        values = dot_t(wv_t, x).astype(BF)
        pieces = pieces_of(c * group, group, half_id, along_y)
        tile = tile_of(spot % quota, counts_ref, pieces, spot // quota, grid_y)
        stacked = []
        for t in range(4):
            mask = jnp.where(tile == t, 1.0, 0.0).astype(BF)
            stacked += [values[k : k + 16] * mask for k in range(0, LANES, 16)]
        stacked.append(jnp.where(tile_row == tile, 1.0, 0.0).astype(BF))
        sums = dot(jnp.concatenate(stacked, axis=0), weights)
        if c == 0:
            num_ref[...] = sums
        else:
            num_ref[...] += sums
    last = 4 * LANES
    for t in range(4):
        rows = slice(t * LANES, (t + 1) * LANES)
        value = jnp.concatenate(
            [
                num_ref[t * LANES : t * LANES + half, :LANES],
                num_ref[t * LANES + half : (t + 1) * LANES, LANES:],
            ],
            axis=0,
        )
        own_ref[rows, :] = value
        send_ref[rows, :] = value.astype(BF)
    totals = jnp.concatenate(
        [num_ref[last : last + 4, h * LANES : (h + 1) * LANES] for h in range(HEADS)]
        + [jnp.zeros((8, LANES), F32)],
        axis=0,
    )
    own_ref[last:, :] = totals
    send_ref[last:, :] = totals.astype(BF)
    if half_id == 0:
        edge_ref = rest[2]
        zl = lax.axis_index("zl")
        for x in range(TLX):
            rows = slice(x * LANES, (x + 1) * LANES)
            high = send_ref[(2 * x + 1) * LANES : (2 * x + 2) * LANES, :]
            low = send_ref[2 * x * LANES : (2 * x + 1) * LANES, :]
            edge_ref[rows, :] = jnp.where(zl == 0, high, low)
        edge_ref[TLX * LANES :, :] = send_ref[last:, :]


def queries_kernel(rows0_ref, rows1_ref, proj_ref, out_ref):
    ones = head_ones()
    for half_id, rows_ref in enumerate((rows0_ref, rows1_ref)):
        members, quota, width = rows_ref.shape
        group = min(512 // quota, members)
        for c in range(members // group):
            x = jnp.concatenate([rows_ref[c * group + k] for k in range(group)], axis=0)
            query = unit(dot(x, proj_ref[0]), ones).astype(BF)
            for k in range(group):
                out_ref[half_id, c * group + k] = query[k * quota : (k + 1) * quota]


def combine_kernel(
    own0_ref,
    own1_ref,
    other0_ref,
    other1_ref,
    near_ref,
    far_ref,
    inducing_ref,
    proj_ref,
    query_any,
    out0_ref,
    out1_ref,
):
    half = LANES // HEADS
    last = 4 * LANES
    outs = (out0_ref, out1_ref)
    zl = lax.axis_index("zl")

    def summarize(value, total0, total1):
        attended = jnp.concatenate([value[:half] / total0, value[half:] / total1], axis=0)
        attended = attended.T.astype(BF)
        out = inducing_ref[...].astype(F32) + dot(attended, proj_ref[3])
        return out.astype(BF)

    for half_id, (own_ref, other_ref) in enumerate(((own0_ref, other0_ref), (own1_ref, other1_ref))):
        b = block_of(half_id, zl)
        totals = own_ref[last:, :] + other_ref[last:, :].astype(F32)
        for t in range(4):
            rows = slice(t * LANES, (t + 1) * LANES)
            value = own_ref[rows, :] + other_ref[rows, :].astype(F32)
            outs[t // 2][b * TLY + t % 2] = summarize(
                value, totals[t : t + 1], totals[t + 4 : t + 5]
            )
    totals = near_ref[TLX * LANES :, :].astype(F32) + far_ref[TLX * LANES :, :].astype(F32)
    for x in range(TLX):
        rows = slice(x * LANES, (x + 1) * LANES)
        value = near_ref[rows, :].astype(F32) + far_ref[rows, :].astype(F32)
        lines = [
            jnp.where(zl == 1, totals[k + 1 : k + 2], totals[k : k + 1])
            for k in (2 * x, 2 * x + 4)
        ]
        outs[x][2 * TLY] = summarize(value, *lines)


def mixture_kernel(
    own0_ref,
    own1_ref,
    below_ref,
    above_ref,
    proj_ref,
    mixing_ref,
    key_ref,
    value_ref,
    mid_ref,
    side_ref,
):
    half = LANES // HEADS
    blocks = key_ref.shape[0]
    tall = blocks * TLY
    low = lax.axis_index("zl")

    row = lax.broadcasted_iota(jnp.int32, (LANES, LANES), 0)
    col = lax.broadcasted_iota(jnp.int32, (LANES, LANES), 1)
    eye = jnp.where(row == col, 1.0, 0.0).astype(BF)
    blank = jnp.zeros((LANES, LANES), BF)

    def mix(a, b):
        return eye if (a, b) == (0, 0) else mixing_ref[neighbour_steps.index((a, b))]

    for k, a in enumerate((-1, 0, 1)):
        rows = slice(k * 2 * LANES, (k + 1) * 2 * LANES)
        mid_ref[rows, :] = jnp.concatenate(
            [
                jnp.concatenate([mix(a, 0), mix(a, -1)], axis=1),
                jnp.concatenate([mix(a, 1), mix(a, 0)], axis=1),
            ],
            axis=0,
        )
    for k, b in enumerate((-1, 1)):
        side_ref[k] = jnp.concatenate(
            [
                jnp.concatenate([mix(0, b), mix(-1, b)], axis=1),
                jnp.concatenate([mix(1, b), mix(0, b)], axis=1),
                jnp.concatenate([mix(-1, b), blank], axis=1),
                jnp.concatenate([blank, mix(1, b)], axis=1),
            ],
            axis=0,
        )
    ones = head_ones()
    lane = lax.broadcasted_iota(jnp.int32, (1, LANES), 1)
    left = lane < half
    grid = (below_ref, own0_ref, own1_ref, above_ref)

    def tile(i, j):
        if 0 <= j < tall:
            return grid[i][j]
        return jnp.where(low == (1 if j < 0 else 0), grid[i][tall], blank)

    mids, lefts, rights = [], [], []
    for i in range(2):
        for b in range(blocks):
            mids.append(
                jnp.concatenate(
                    [tile(i + r, 2 * b + s) for r in range(3) for s in range(2)], axis=1
                )
            )
    for b in range(blocks):
        lefts.append(jnp.concatenate([tile(i, 2 * b - 1) for i in (1, 2, 0, 3)], axis=1))
        rights.append(jnp.concatenate([tile(i, 2 * b + 2) for i in (1, 2, 0, 3)], axis=1))
    middle = dot(jnp.concatenate(mids, axis=0), mid_ref[...])
    from_left = dot(jnp.concatenate(lefts, axis=0), side_ref[0])
    from_right = dot(jnp.concatenate(rights, axis=0), side_ref[1])
    mixtures = []
    for b in range(blocks):
        span = slice(b * LANES, (b + 1) * LANES)
        for i in range(2):
            m = middle[(i * blocks + b) * LANES : (i * blocks + b + 1) * LANES]
            cols = slice(i * LANES, (i + 1) * LANES)
            mixtures.append((m[:, :LANES] + from_left[span, cols]).astype(BF))
            mixtures.append((m[:, LANES:] + from_right[span, cols]).astype(BF))
    mixtures = jnp.concatenate(mixtures, axis=0)
    keys = unit(dot(mixtures, proj_ref[1]), ones)
    values = dot(mixtures, proj_ref[2])
    for b in range(blocks):
        spans = [slice((b * 4 + t) * LANES, (b * 4 + t + 1) * LANES) for t in range(4)]
        for h in range(HEADS):
            mine = left if h == 0 else ~left
            key_ref[b, h * LANES : (h + 1) * LANES, :] = jnp.concatenate(
                [jnp.where(mine, keys[s], 0.0) for s in spans], axis=1
            ).astype(BF)
            flags = jnp.broadcast_to(jnp.where(mine, 1.0, 0.0), (LANES, LANES))
            for t, s in enumerate(spans):
                rows = slice((t * HEADS + h) * LANES, (t * HEADS + h + 1) * LANES)
                value_ref[b, rows, :] = jnp.concatenate(
                    [jnp.where(mine, values[s], 0.0), flags], axis=1
                ).astype(BF)


def attend_kernel(
    along_y, rows0_ref, rows1_ref, query_ref, counts_ref, key_ref, value_ref, proj_ref, out_ref
):
    members, quota, width = rows0_ref.shape
    grid_y = along_y * TLY
    group = min(512 // quota, members)
    chunk = group * quota
    spot = lax.broadcasted_iota(jnp.int32, (chunk, LANES), 0)
    for half_id, rows_ref in enumerate((rows0_ref, rows1_ref)):
        block = block_of(half_id, lax.axis_index("zl"))
        for c in range(members // group):
            x = jnp.concatenate([rows_ref[c * group + k] for k in range(group)], axis=0)
            query = jnp.concatenate(
                [query_ref[half_id, c * group + k] for k in range(group)], axis=0
            )
            pieces = pieces_of(c * group, group, half_id, along_y)
            which = tile_of(spot % quota, counts_ref, pieces, spot // quota, grid_y)
            masks = [jnp.where(which == t, 1.0, 0.0).astype(BF) for t in range(4)]
            expanded = jnp.concatenate([query * m for m in masks], axis=1)
            scores = dot_t(expanded, key_ref[block])
            weights = jnp.exp2(scores * (sharpness * math.log2(math.e))).astype(BF)
            spread = jnp.concatenate(
                [
                    weights[:, h * LANES : (h + 1) * LANES] * m
                    for m in masks
                    for h in range(HEADS)
                ],
                axis=1,
            )
            both = dot(spread, value_ref[block])
            attended = (both[:, :LANES] / both[:, LANES:]).astype(BF)
            result = (x.astype(F32) + dot(attended, proj_ref[3])).astype(BF)
            for k in range(group):
                out_ref[c * group + k, half_id] = result[k * quota : (k + 1) * quota]


def scatter_kernel(rows_ref, index_ref, out_ref, wide_ref, part_ref):
    chunk = part_ref.shape[0]
    members, halves, quota, width = rows_ref.shape
    group = chunk // (halves * quota)

    def step(c, carry):
        for k in range(group):
            for half_id in range(halves):
                row = (k * halves + block_of(half_id, k % 2)) * quota
                part_ref[row : row + quota, :] = rows_ref[c * group + k, half_id].astype(F32)
        for r in range(chunk):
            i = index_ref[c * (chunk // LANES) + r // LANES, r % LANES]
            wide_ref[pl.ds(i, 1), :] = part_ref[pl.ds(r, 1), :]
        return carry

    lax.fori_loop(0, members // group, step, 0)
    out_ref[...] = wide_ref[...].astype(BF)


def call(kernel, name, out_shape, in_specs, scratch, micros, operands, megabytes=20, **more):
    spaces = {"v": pltpu.VMEM, "s": pltpu.SMEM, "a": pl.ANY}
    many = isinstance(out_shape, tuple)
    whole = pl.BlockSpec(memory_space=pltpu.VMEM)
    return pl.pallas_call(
        kernel,
        out_shape=out_shape,
        in_specs=[pl.BlockSpec(memory_space=spaces[c]) for c in in_specs],
        out_specs=(whole,) * len(out_shape) if many else whole,
        scratch_shapes=scratch,
        compiler_params=pltpu.CompilerParams(vmem_limit_bytes=megabytes * 1024 * 1024),
        cost_estimate=pl.CostEstimate(
            flops=int(micros * 5e8), bytes_accessed=int(micros * 1e6), transcendentals=0
        ),
        name=name,
        **more,
    )(*operands)


def body(
    points,
    embed_weight,
    inner_weights,
    output_weight,
    counts,
    point_order,
    inducing,
    first_proj,
    second_proj,
    mixing,
):
    along_x = lax.axis_size("tx")
    highs = lax.axis_size("zh")
    lows = lax.axis_size("zl")
    along_y = highs * lows
    point_count, width = points.shape
    quota = point_count // (along_x * along_y)
    grid_y = along_y * TLY
    blocks = 2
    members = along_x * lows
    tall = blocks * TLY
    lines = point_count // LANES
    chunk = 512
    half_rows = (members, quota, width)

    def shape(sizes, dtype=BF):
        return jax.ShapeDtypeStruct(sizes, dtype)

    weights = (embed_weight, inner_weights, output_weight)
    buffers = [
        VMEM((point_count, width), F32),
        VMEM((chunk, width), F32),
        VMEM((chunk, width), F32),
    ]
    first, index = call(
        functools.partial(encode_first_kernel, grid_y, along_y, quota),
        "encode_first",
        (shape(half_rows), shape((lines, LANES), jnp.int32)),
        "aaaaaa",
        [
            SMEM((counts.shape[1],), jnp.int32),
            SMEM((counts.shape[1],), jnp.int32),
            SMEM((lines, LANES), jnp.int32),
        ]
        + buffers
        + [VMEM(a.shape, BF) for a in (points, *weights)]
        + [VMEM((lines, LANES), jnp.int32), pltpu.SemaphoreType.DMA((7,))],
        8,
        (points, *weights, counts, point_order.reshape(lines, LANES)),
        megabytes=56,
    )
    second = call(
        functools.partial(encode_second_kernel, quota),
        "encode_second",
        shape(half_rows),
        "vvvvs",
        buffers,
        6,
        (points, *weights, index),
    )

    def exchange(rows):
        return lax.all_to_all(rows, ("tx", "zl"), split_axis=0, concat_axis=0, tiled=True)

    rows0 = exchange(first)
    rows1 = exchange(second)

    part_rows = 4 * LANES + 16
    edge_rows = TLX * LANES + 16
    parts = (shape((part_rows, LANES), F32), shape((part_rows, LANES)))
    sums = [VMEM((part_rows, HEADS * LANES), F32)]
    own0, send0, edge = call(
        functools.partial(partial_kernel, 0, along_y),
        "partial_first",
        parts + (shape((edge_rows, LANES)),),
        "vsvv",
        sums,
        3,
        (rows0, counts, inducing, first_proj),
    )
    own1, send1 = call(
        functools.partial(partial_kernel, 1, along_y),
        "partial_second",
        parts,
        "vsvv",
        sums,
        3,
        (rows1, counts, inducing, first_proj),
    )
    pairs = [(h, l) for h in range(highs) for l in range(lows)]

    def swap(value, flip_high, flip_low):
        steps = []
        for h, l in pairs:
            other_h = highs - 1 - h if flip_high else h
            other_l = lows - 1 - l if flip_low else l
            steps.append((h * lows + l, other_h * lows + other_l))
        return lax.ppermute(value, ("zh", "zl"), steps)

    other0 = swap(send0, True, False)
    far = swap(edge, True, True)
    near = swap(edge, False, True)
    other1 = swap(send1, True, False)

    queries = call(
        queries_kernel,
        "point_queries",
        shape((2,) + half_rows),
        "vvv",
        [],
        2,
        (rows0, rows1, second_proj),
    )

    line = shape((tall + 1, LANES, width))
    summary0, summary1 = call(
        combine_kernel,
        "combine_partials",
        (line, line),
        "v" * 8 + "a",
        [],
        1,
        (own0, own1, other0, other1, near, far, inducing, first_proj, queries),
    )
    forward = [(i, i + 1) for i in range(along_x - 1)]
    backward = [(i + 1, i) for i in range(along_x - 1)]
    below = lax.ppermute(summary1, "tx", forward)
    above = lax.ppermute(summary0, "tx", backward)

    keys, values = call(
        mixture_kernel,
        "mix_tiles",
        (shape((blocks, HEADS * LANES, 4 * LANES)), shape((blocks, 4 * HEADS * LANES, 2 * LANES))),
        "v" * 6,
        [VMEM((6 * LANES, 2 * LANES), BF), VMEM((2, 4 * LANES, 2 * LANES), BF)],
        4,
        (summary0, summary1, below, above, second_proj, mixing),
    )

    result = call(
        functools.partial(attend_kernel, along_y),
        "attend_points",
        shape((members, 2, quota, width)),
        "vvvsvvv",
        [],
        7,
        (rows0, rows1, queries, counts, keys, values, second_proj),
    )
    return call(
        scatter_kernel,
        "scatter_rows",
        shape((point_count, width)),
        "vs",
        [VMEM((point_count, width), F32), VMEM((chunk, width), F32)],
        5,
        (exchange(result), index),
    )


def solution(mesh):
    along_x, along_y = mesh.devices.shape
    split = jax.sharding.Mesh(mesh.devices.reshape(along_x, 2, along_y // 2), ("tx", "zh", "zl"))
    rows = P(("tx", "zh", "zl"), None)
    placed = (rows, P(), P(), P(), P(), rows, P(), P(), P(), P())
    return jax.shard_map(body, mesh=split, in_specs=placed, out_specs=rows, check_vma=False)
```

```python
import functools
import math

import jax
import jax.numpy as jnp
from jax import lax
from jax.experimental import pallas as pl
from jax.experimental.pallas import tpu as pltpu
from jax.sharding import PartitionSpec as P

HEADS = 2
TLX = 2
TLY = 2
LANES = 128
BF = jnp.bfloat16
F32 = jnp.float32

sharpness = 32.0
epsilon = 1e-06
neighbour_steps = ((-1, -1), (-1, 0), (-1, 1), (0, -1), (0, 1), (1, -1), (1, 0), (1, 1))
VMEM = pltpu.VMEM
SMEM = pltpu.SMEM


def dot(a, b):
    return jnp.dot(a, b, preferred_element_type=F32)


def dot_t(a, b):
    return lax.dot_general(a, b, (((1,), (1,)), ((), ())), preferred_element_type=F32)


def head_ones():
    row = lax.broadcasted_iota(jnp.int32, (2 * LANES, LANES), 0)
    col = lax.broadcasted_iota(jnp.int32, (2 * LANES, LANES), 1)
    half = LANES // HEADS
    same = ((row % LANES) // half) == (col // half)
    return jnp.where(same, 1.0, 0.0).astype(BF)


def unit(v, ones):
    square = v * v
    high = square.astype(BF)
    low = (square - high.astype(F32)).astype(BF)
    total = dot(jnp.concatenate([high, low], axis=1), ones)
    return v * lax.rsqrt(total + epsilon)


def silu(v):
    half = 0.5 * v
    return half + half * jnp.tanh(half)


def place():
    return lax.axis_index("tx"), lax.axis_index("zh"), lax.axis_index("zl")


def block_of(half_id, low):
    return low if half_id else 1 - low


def encode_rows(half_id, quota, chunk, points, weights_ready, w1_ref, w2_ref, w3_ref, index_s, feat_ref, wide_ref, xs):
    rows_total = points.shape[0] // 2
    group = chunk // quota
    wide_ref[...] = points[...].astype(F32)

    def gather(c, buffer, first, last):
        for r in range(first, last):
            member = r // quota
            spot = (member * 2 + block_of(half_id, member % 2)) * quota + r % quota
            i = index_s[c * (2 * chunk // LANES) + spot // LANES, spot % LANES]
            buffer[pl.ds(r, 1), :] = wide_ref[pl.ds(i, 1), :]

    def layer(x, w, ahead, cuts):
        parts = []
        step = w.shape[1] // 2
        for k in range(2):
            ahead(cuts[k], cuts[k + 1])
            parts.append(silu(dot(x, w[:, k * step : (k + 1) * step])).astype(BF))
        return jnp.concatenate(parts, axis=1)

    def apply(c, buffer, ahead):
        cuts = [chunk * k // 5 for k in range(6)]
        hidden = layer(buffer[...].astype(BF), w1_ref, ahead, cuts[:3])
        hidden = layer(hidden, w2_ref.at[0], ahead, cuts[2:5])
        ahead(cuts[4], cuts[5])
        out = dot(hidden, w3_ref[...]).astype(BF)
        for k in range(group):
            feat_ref[c * group + k] = out[k * quota : (k + 1) * quota]

    chunks = rows_total // chunk
    if half_id:
        weights_ready()
    gather(0, xs[0], 0, chunk)
    if not half_id:
        weights_ready()

    def step(k, carry):
        c = 2 * k
        apply(c, xs[0], lambda a, b: gather(c + 1, xs[1], a, b))
        apply(c + 1, xs[1], lambda a, b: gather(jnp.minimum(c + 2, chunks - 1), xs[0], a, b))
        return carry

    lax.fori_loop(0, chunks // 2, step, 0)


def encode_first_kernel(
    grid_y,
    along_y,
    quota,
    points_hbm,
    w1_hbm,
    w2_hbm,
    w3_hbm,
    counts_hbm,
    order_hbm,
    feat_ref,
    index_ref,
    counts_s,
    off_ref,
    index_s,
    wide_ref,
    xa_ref,
    xb_ref,
    points_ref,
    w1_ref,
    w2_ref,
    w3_ref,
    order_ref,
    sems,
):
    tx, zh, zl = place()
    own = tx * along_y + zh * (along_y // 2) + zl
    sources = (counts_hbm.at[own], order_hbm, points_hbm, w1_hbm, w2_hbm, w3_hbm)
    targets = (counts_s, order_ref, points_ref, w1_ref, w2_ref, w3_ref)
    copies = [
        pltpu.make_async_copy(a, b, sems.at[k]) for k, (a, b) in enumerate(zip(sources, targets))
    ]
    for copy in copies:
        copy.start()
    tiles = counts_s.shape[0]
    order_rows = order_ref.shape[0]
    rows_total = points_ref.shape[0]
    copies[0].wait()

    def add_up(g, total):
        off_ref[g] = total
        return total + counts_s[g]

    lax.fori_loop(0, tiles, add_up, jnp.int32(0), unroll=8)
    copies[1].wait()
    lane = lax.broadcasted_iota(jnp.int32, (1, LANES), 1)

    def run_of(start):
        line = start >> 7
        shift = start & (LANES - 1)
        first = order_ref[pl.ds(jnp.clip(line, 0, order_rows - 1), 1), :]
        second = order_ref[pl.ds(jnp.clip(line + 1, 0, order_rows - 1), 1), :]
        merged = jnp.where(lane < shift, second, first)
        return pltpu.roll(merged, (LANES - shift) & (LANES - 1), 1)

    per_line = LANES // quota

    def index_line(line, carry):
        value = jnp.zeros((1, LANES), jnp.int32)
        for k in range(per_line):
            d = line * per_line + k
            g1 = (d // along_y) * (TLX * grid_y) + (d % along_y) * TLY
            n1 = counts_s[g1] + counts_s[g1 + 1]
            run1 = run_of(off_ref[g1] - k * quota)
            run2 = run_of(off_ref[g1 + grid_y] - n1 - k * quota)
            both = jnp.where(lane < k * quota + n1, run1, run2)
            value = both if k == 0 else jnp.where(lane >= k * quota, both, value)
        index_ref[pl.ds(line, 1), :] = value
        return carry

    lax.fori_loop(0, rows_total // LANES, index_line, 0, unroll=8)
    copy = pltpu.make_async_copy(index_ref, index_s, sems.at[6])
    copy.start()
    copies[2].wait()
    copy.wait()

    def weights_ready():
        for k in (3, 4, 5):
            copies[k].wait()

    encode_rows(
        0, quota, xa_ref.shape[0], points_ref, weights_ready, w1_ref, w2_ref, w3_ref, index_s,
        feat_ref, wide_ref, (xa_ref, xb_ref),
    )


def encode_second_kernel(
    quota, points_ref, w1_ref, w2_ref, w3_ref, index_any, feat_ref, index_s, wide_ref, xa_ref, xb_ref, sem
):
    copy = pltpu.make_async_copy(index_any, index_s, sem)
    copy.start()
    encode_rows(
        1, quota, xa_ref.shape[0], points_ref, copy.wait, w1_ref, w2_ref, w3_ref, index_s,
        feat_ref, wide_ref, (xa_ref, xb_ref),
    )


def tile_of(position, counts_ref, pieces, piece_id, grid_y):
    bounds = [None, None, None]
    for k, (s, base) in enumerate(pieces):
        n0 = counts_ref[s, base]
        n1 = counts_ref[s, base + 1]
        n2 = counts_ref[s, base + grid_y]
        for i, found in enumerate((n0, n0 + n1, n0 + n1 + n2)):
            if k == 0:
                bounds[i] = jnp.full(position.shape, found, jnp.int32)
            else:
                bounds[i] = jnp.where(piece_id >= k, found, bounds[i])
    return sum((position >= b).astype(jnp.int32) for b in bounds)


def pieces_of(first, group, half_id, along_y):
    tx, zh, zl = place()
    lows = along_y // 2
    block = zl * 2 + block_of(half_id, zl)
    base = tx * (TLX * along_y * TLY) + block * TLY
    found = []
    for k in range(group):
        member = first + k
        found.append(((member // lows) * along_y + zh * lows + member % lows, base))
    return found


def partial_kernel(half_id, along_y, rows_ref, counts_ref, *rest):
    num_ref = rest[-1]
    if half_id:
        query_ref, wv_ref, proj_ref, near_any, far_any, own_ref, send_ref = rest[:-1]
    else:
        inducing_ref, proj_ref, own_ref, send_ref, edge_ref, query_ref, wv_ref = rest[:-1]
    members, quota, width = rows_ref.shape
    grid_y = along_y * TLY
    half = LANES // HEADS
    group = min(512 // quota, members)
    chunk = group * quota
    ones = head_ones()
    lane = lax.broadcasted_iota(jnp.int32, (1, LANES), 1)
    left = lane < half
    if half_id:
        queries = query_ref[...]
        wv_t = wv_ref[...]
    else:
        queries = unit(dot(inducing_ref[...], proj_ref[0]), ones)
        queries = jnp.concatenate(
            [jnp.where(left, queries, 0.0), jnp.where(left, 0.0, queries)], axis=0
        ).astype(BF)
        wv_t = proj_ref[2].astype(F32).T.astype(BF)
        query_ref[...] = queries
        wv_ref[...] = wv_t
    spot = lax.broadcasted_iota(jnp.int32, (16, chunk), 1)
    tile_row = lax.broadcasted_iota(jnp.int32, (16, chunk), 0)
    for c in range(members // group):
        x = jnp.concatenate([rows_ref[c * group + k] for k in range(group)], axis=0)
        keys = unit(dot(x, proj_ref[1]), ones).astype(BF)
        weights = jnp.exp2(dot_t(keys, queries) * (sharpness * math.log2(math.e))).astype(BF)
        values = dot_t(wv_t, x).astype(BF)
        pieces = pieces_of(c * group, group, half_id, along_y)
        tile = tile_of(spot % quota, counts_ref, pieces, spot // quota, grid_y)
        stacked = []
        for t in range(4):
            mask = jnp.where(tile == t, 1.0, 0.0).astype(BF)
            stacked += [values[k : k + 16] * mask for k in range(0, LANES, 16)]
        stacked.append(jnp.where(tile_row == tile, 1.0, 0.0).astype(BF))
        sums = dot(jnp.concatenate(stacked, axis=0), weights)
        if c == 0:
            num_ref[...] = sums
        else:
            num_ref[...] += sums
    last = 4 * LANES
    for t in range(4):
        rows = slice(t * LANES, (t + 1) * LANES)
        value = jnp.concatenate(
            [
                num_ref[t * LANES : t * LANES + half, :LANES],
                num_ref[t * LANES + half : (t + 1) * LANES, LANES:],
            ],
            axis=0,
        )
        own_ref[rows, :] = value
        send_ref[rows, :] = value.astype(BF)
    totals = jnp.concatenate(
        [num_ref[last : last + 4, h * LANES : (h + 1) * LANES] for h in range(HEADS)]
        + [jnp.zeros((8, LANES), F32)],
        axis=0,
    )
    own_ref[last:, :] = totals
    send_ref[last:, :] = totals.astype(BF)
    if half_id == 0:
        zl = lax.axis_index("zl")
        for x in range(TLX):
            rows = slice(x * LANES, (x + 1) * LANES)
            high = send_ref[(2 * x + 1) * LANES : (2 * x + 2) * LANES, :]
            low = send_ref[2 * x * LANES : (2 * x + 1) * LANES, :]
            edge_ref[rows, :] = jnp.where(zl == 0, high, low)
        edge_ref[TLX * LANES :, :] = send_ref[last:, :]


def row_bounds(piece, counts_ref, grid_y):
    s, base = piece
    n0 = counts_ref[s, base]
    n1 = n0 + counts_ref[s, base + 1]
    return n0, n1, n1 + counts_ref[s, base + grid_y]


def queries_kernel(along_y, rows0_ref, rows1_ref, counts_ref, proj_ref, out_ref):
    ones = head_ones()
    for half_id, rows_ref in enumerate((rows0_ref, rows1_ref)):
        members, quota, width = rows_ref.shape
        group = min(512 // quota, members)
        row = lax.broadcasted_iota(jnp.int32, (quota, LANES), 0)
        for c in range(members // group):
            x = jnp.concatenate([rows_ref[c * group + k] for k in range(group)], axis=0)
            query = unit(dot(x, proj_ref[0]), ones)
            pieces = pieces_of(c * group, group, half_id, along_y)
            for k in range(group):
                bounds = row_bounds(pieces[k], counts_ref, along_y * TLY)
                past = [row >= b for b in bounds]
                mine = query[k * quota : (k + 1) * quota]
                masks = (~past[0], past[0] & ~past[1], past[1] & ~past[2], past[2])
                out_ref[half_id, c * group + k] = jnp.concatenate(
                    [jnp.where(m, mine, 0.0).astype(BF) for m in masks], axis=1
                )


def combine_kernel(
    own0_ref,
    own1_ref,
    other0_ref,
    other1_ref,
    near_ref,
    far_ref,
    inducing_ref,
    proj_ref,
    query_any,
    out0_ref,
    out1_ref,
    near_pair_ref,
    far_pair_ref,
):
    half = LANES // HEADS
    last = 4 * LANES
    outs = (out0_ref, out1_ref)
    zl = lax.axis_index("zl")

    def summarize(value, total0, total1):
        attended = jnp.concatenate([value[:half] / total0, value[half:] / total1], axis=0)
        attended = attended.T.astype(BF)
        out = inducing_ref[...].astype(F32) + dot(attended, proj_ref[3])
        return out.astype(BF)

    for half_id, (own_ref, other_ref) in enumerate(((own0_ref, other0_ref), (own1_ref, other1_ref))):
        b = block_of(half_id, zl)
        totals = own_ref[last:, :] + other_ref[last:, :].astype(F32)
        for t in range(4):
            rows = slice(t * LANES, (t + 1) * LANES)
            value = own_ref[rows, :] + other_ref[rows, :].astype(F32)
            outs[t // 2][b * TLY + t % 2] = summarize(
                value, totals[t : t + 1], totals[t + 4 : t + 5]
            )
    totals = near_ref[TLX * LANES :, :].astype(F32) + far_ref[TLX * LANES :, :].astype(F32)
    for x in range(TLX):
        rows = slice(x * LANES, (x + 1) * LANES)
        value = near_ref[rows, :].astype(F32) + far_ref[rows, :].astype(F32)
        lines = [
            jnp.where(zl == 1, totals[k + 1 : k + 2], totals[k : k + 1])
            for k in (2 * x, 2 * x + 4)
        ]
        outs[x][2 * TLY] = summarize(value, *lines)
    even = lax.axis_index("tx") % 2 == 0
    for j in range(out0_ref.shape[0]):
        near_pair_ref[j] = jnp.where(even, out1_ref[j], out0_ref[j])
        far_pair_ref[j] = jnp.where(even, out0_ref[j], out1_ref[j])


def mixture_kernel(
    own0_ref,
    own1_ref,
    near_pair_ref,
    far_pair_ref,
    proj_ref,
    mixing_ref,
    key_ref,
    value_ref,
    mid_ref,
    side_ref,
):
    half = LANES // HEADS
    blocks = key_ref.shape[0]
    tall = blocks * TLY
    low = lax.axis_index("zl")

    row = lax.broadcasted_iota(jnp.int32, (LANES, LANES), 0)
    col = lax.broadcasted_iota(jnp.int32, (LANES, LANES), 1)
    eye = jnp.where(row == col, 1.0, 0.0).astype(BF)
    blank = jnp.zeros((LANES, LANES), BF)

    def mix(a, b):
        return eye if (a, b) == (0, 0) else mixing_ref[neighbour_steps.index((a, b))]

    for k, a in enumerate((-1, 0, 1)):
        rows = slice(k * 2 * LANES, (k + 1) * 2 * LANES)
        mid_ref[rows, :] = jnp.concatenate(
            [
                jnp.concatenate([mix(a, 0), mix(a, -1)], axis=1),
                jnp.concatenate([mix(a, 1), mix(a, 0)], axis=1),
            ],
            axis=0,
        )
    for k, b in enumerate((-1, 1)):
        side_ref[k] = jnp.concatenate(
            [
                jnp.concatenate([mix(0, b), mix(-1, b)], axis=1),
                jnp.concatenate([mix(1, b), mix(0, b)], axis=1),
                jnp.concatenate([mix(-1, b), blank], axis=1),
                jnp.concatenate([blank, mix(1, b)], axis=1),
            ],
            axis=0,
        )
    ones = head_ones()
    lane = lax.broadcasted_iota(jnp.int32, (1, LANES), 1)
    left = lane < half
    even = lax.axis_index("tx") % 2 == 0

    def held(i, j):
        if i in (1, 2):
            return (own0_ref, own1_ref)[i - 1][j]
        near, far = near_pair_ref[j], far_pair_ref[j]
        return jnp.where(even, far, near) if i == 0 else jnp.where(even, near, far)

    grid = [[held(i, j) for j in range(tall + 1)] for i in range(4)]

    def tile(i, j):
        if 0 <= j < tall:
            return grid[i][j]
        return jnp.where(low == (1 if j < 0 else 0), grid[i][tall], blank)

    mids, lefts, rights = [], [], []
    for i in range(2):
        for b in range(blocks):
            mids.append(
                jnp.concatenate(
                    [tile(i + r, 2 * b + s) for r in range(3) for s in range(2)], axis=1
                )
            )
    for b in range(blocks):
        lefts.append(jnp.concatenate([tile(i, 2 * b - 1) for i in (1, 2, 0, 3)], axis=1))
        rights.append(jnp.concatenate([tile(i, 2 * b + 2) for i in (1, 2, 0, 3)], axis=1))
    middle = dot(jnp.concatenate(mids, axis=0), mid_ref[...])
    from_left = dot(jnp.concatenate(lefts, axis=0), side_ref[0])
    from_right = dot(jnp.concatenate(rights, axis=0), side_ref[1])
    mixtures = []
    for b in range(blocks):
        span = slice(b * LANES, (b + 1) * LANES)
        for i in range(2):
            m = middle[(i * blocks + b) * LANES : (i * blocks + b + 1) * LANES]
            cols = slice(i * LANES, (i + 1) * LANES)
            mixtures.append((m[:, :LANES] + from_left[span, cols]).astype(BF))
            mixtures.append((m[:, LANES:] + from_right[span, cols]).astype(BF))
    mixtures = jnp.concatenate(mixtures, axis=0)
    keys = unit(dot(mixtures, proj_ref[1]), ones)
    values = dot(mixtures, proj_ref[2])
    for b in range(blocks):
        spans = [slice((b * 4 + t) * LANES, (b * 4 + t + 1) * LANES) for t in range(4)]
        for h in range(HEADS):
            mine = left if h == 0 else ~left
            key_ref[b, h * LANES : (h + 1) * LANES, :] = jnp.concatenate(
                [jnp.where(mine, keys[s], 0.0) for s in spans], axis=1
            ).astype(BF)
            flags = jnp.broadcast_to(jnp.where(mine, 1.0, 0.0), (LANES, LANES))
            value_ref[b, h * LANES : (h + 1) * LANES, :] = jnp.concatenate(
                [jnp.where(mine, values[s], 0.0) for s in spans] + [flags], axis=1
            ).astype(BF)


def attend_kernel(
    along_y, rows0_ref, rows1_ref, query_ref, counts_ref, key_ref, value_ref, proj_ref, out_ref
):
    members, quota, width = rows0_ref.shape
    group = min(512 // quota, members)
    row = lax.broadcasted_iota(jnp.int32, (quota, LANES), 0)
    for half_id, rows_ref in enumerate((rows0_ref, rows1_ref)):
        block = block_of(half_id, lax.axis_index("zl"))
        for c in range(members // group):
            expanded = jnp.concatenate(
                [query_ref[half_id, c * group + k] for k in range(group)], axis=0
            )
            scores = dot_t(expanded, key_ref[block])
            weights = jnp.exp2(scores * (sharpness * math.log2(math.e))).astype(BF)
            every = dot(weights, value_ref[block])
            pieces = pieces_of(c * group, group, half_id, along_y)
            attended = []
            for k in range(group):
                bounds = row_bounds(pieces[k], counts_ref, along_y * TLY)
                part = every[k * quota : (k + 1) * quota]
                picked = part[:, :LANES]
                for t, bound in enumerate(bounds):
                    tile = part[:, (t + 1) * LANES : (t + 2) * LANES]
                    picked = jnp.where(row >= bound, tile, picked)
                attended.append((picked / part[:, 4 * LANES :]).astype(BF))
            x = jnp.concatenate([rows_ref[c * group + k] for k in range(group)], axis=0)
            added = dot(jnp.concatenate(attended, axis=0), proj_ref[3])
            result = (x.astype(F32) + added).astype(BF)
            for k in range(group):
                out_ref[c * group + k, half_id] = result[k * quota : (k + 1) * quota]


def scatter_kernel(rows_ref, index_ref, out_ref, wide_ref, part_ref):
    chunk = part_ref.shape[0]
    members, halves, quota, width = rows_ref.shape
    group = chunk // (halves * quota)

    def step(c, carry):
        for k in range(group):
            for half_id in range(halves):
                row = (k * halves + block_of(half_id, k % 2)) * quota
                part_ref[row : row + quota, :] = rows_ref[c * group + k, half_id].astype(F32)
        for r in range(chunk):
            i = index_ref[c * (chunk // LANES) + r // LANES, r % LANES]
            wide_ref[pl.ds(i, 1), :] = part_ref[pl.ds(r, 1), :]
        return carry

    lax.fori_loop(0, members // group, step, 0)
    out_ref[...] = wide_ref[...].astype(BF)


def call(kernel, name, out_shape, in_specs, scratch, micros, operands, megabytes=20, **more):
    spaces = {"v": pltpu.VMEM, "s": pltpu.SMEM, "a": pl.ANY}
    many = isinstance(out_shape, tuple)
    whole = pl.BlockSpec(memory_space=pltpu.VMEM)
    return pl.pallas_call(
        kernel,
        out_shape=out_shape,
        in_specs=[pl.BlockSpec(memory_space=spaces[c]) for c in in_specs],
        out_specs=(whole,) * len(out_shape) if many else whole,
        scratch_shapes=scratch,
        compiler_params=pltpu.CompilerParams(vmem_limit_bytes=megabytes * 1024 * 1024),
        cost_estimate=pl.CostEstimate(
            flops=int(micros * 5e8), bytes_accessed=int(micros * 1e6), transcendentals=0
        ),
        name=name,
        **more,
    )(*operands)


def body(
    points,
    embed_weight,
    inner_weights,
    output_weight,
    counts,
    point_order,
    inducing,
    first_proj,
    second_proj,
    mixing,
):
    along_x = lax.axis_size("tx")
    highs = lax.axis_size("zh")
    lows = lax.axis_size("zl")
    along_y = highs * lows
    point_count, width = points.shape
    quota = point_count // (along_x * along_y)
    grid_y = along_y * TLY
    blocks = 2
    members = along_x * lows
    tall = blocks * TLY
    lines = point_count // LANES
    chunk = 512
    half_rows = (members, quota, width)

    def shape(sizes, dtype=BF):
        return jax.ShapeDtypeStruct(sizes, dtype)

    weights = (embed_weight, inner_weights, output_weight)
    buffers = [
        VMEM((point_count, width), F32),
        VMEM((chunk, width), F32),
        VMEM((chunk, width), F32),
    ]
    first, index = call(
        functools.partial(encode_first_kernel, grid_y, along_y, quota),
        "encode_first",
        (shape(half_rows), shape((lines, LANES), jnp.int32)),
        "aaaaaa",
        [
            SMEM((counts.shape[1],), jnp.int32),
            SMEM((counts.shape[1],), jnp.int32),
            SMEM((lines, LANES), jnp.int32),
        ]
        + buffers
        + [VMEM(a.shape, BF) for a in (points, *weights)]
        + [VMEM((lines, LANES), jnp.int32), pltpu.SemaphoreType.DMA((7,))],
        8,
        (points, *weights, counts, point_order.reshape(lines, LANES)),
        megabytes=56,
    )
    second = call(
        functools.partial(encode_second_kernel, quota),
        "encode_second",
        shape(half_rows),
        "vvvva",
        [SMEM((lines, LANES), jnp.int32)] + buffers + [pltpu.SemaphoreType.DMA],
        6,
        (points, *weights, index),
    )

    def exchange(rows):
        return lax.all_to_all(rows, ("tx", "zl"), split_axis=0, concat_axis=0, tiled=True)

    rows0 = exchange(first)
    rows1 = exchange(second)

    part_rows = 4 * LANES + 16
    edge_rows = TLX * LANES + 16
    parts = (shape((part_rows, LANES), F32), shape((part_rows, LANES)))
    sums = [VMEM((part_rows, HEADS * LANES), F32)]
    own0, send0, edge, first_queries, value_weight = call(
        functools.partial(partial_kernel, 0, along_y),
        "partial_first",
        parts
        + (shape((edge_rows, LANES)), shape((HEADS * LANES, width)), shape((LANES, width))),
        "vsvv",
        sums,
        3,
        (rows0, counts, inducing, first_proj),
    )
    pairs = [(h, l) for h in range(highs) for l in range(lows)]

    def swap(value, flip_high, flip_low):
        steps = []
        for h, l in pairs:
            other_h = highs - 1 - h if flip_high else h
            other_l = lows - 1 - l if flip_low else l
            steps.append((h * lows + l, other_h * lows + other_l))
        return lax.ppermute(value, ("zh", "zl"), steps)

    far = swap(edge, True, True)
    near = swap(edge, False, True)
    other0 = swap(send0, True, False)
    own1, send1 = call(
        functools.partial(partial_kernel, 1, along_y),
        "partial_second",
        parts,
        "vsvvvaa",
        sums,
        3,
        (rows1, counts, first_queries, value_weight, first_proj, near, far),
    )
    other1 = swap(send1, True, False)

    queries = call(
        functools.partial(queries_kernel, along_y),
        "point_queries",
        shape((2, members, quota, 4 * width)),
        "vvsv",
        [],
        3,
        (rows0, rows1, counts, second_proj),
    )

    line = shape((tall + 1, LANES, width))
    summary0, summary1, near_line, far_line = call(
        combine_kernel,
        "combine_partials",
        (line,) * 4,
        "v" * 8 + "a",
        [],
        1,
        (own0, own1, other0, other1, near, far, inducing, first_proj, queries),
    )
    near_pairs = [(i, i ^ 1) for i in range(along_x)]
    far_pairs = [(i, ((i + 1) ^ 1) - 1) for i in range(1, along_x - 1)]
    near_line = lax.ppermute(near_line, "tx", near_pairs)
    far_line = lax.ppermute(far_line, "tx", far_pairs)

    keys, values = call(
        mixture_kernel,
        "mix_tiles",
        (shape((blocks, HEADS * LANES, 4 * LANES)), shape((blocks, HEADS * LANES, 5 * LANES))),
        "v" * 6,
        [VMEM((6 * LANES, 2 * LANES), BF), VMEM((2, 4 * LANES, 2 * LANES), BF)],
        4,
        (summary0, summary1, near_line, far_line, second_proj, mixing),
    )

    result = call(
        functools.partial(attend_kernel, along_y),
        "attend_points",
        shape((members, 2, quota, width)),
        "vvvsvvv",
        [],
        7,
        (rows0, rows1, queries, counts, keys, values, second_proj),
    )
    return call(
        scatter_kernel,
        "scatter_rows",
        shape((point_count, width)),
        "vs",
        [VMEM((point_count, width), F32), VMEM((chunk, width), F32)],
        5,
        (exchange(result), index),
    )


def solution(mesh):
    along_x, along_y = mesh.devices.shape
    split = jax.sharding.Mesh(mesh.devices.reshape(along_x, 2, along_y // 2), ("tx", "zh", "zl"))
    rows = P(("tx", "zh", "zl"), None)
    placed = (rows, P(), P(), P(), P(), rows, P(), P(), P(), P())
    return jax.shard_map(body, mesh=split, in_specs=placed, out_specs=rows, check_vma=False)
```

```python
import functools
import math

import jax
import jax.numpy as jnp
from jax import lax
from jax.experimental import pallas as pl
from jax.experimental.pallas import tpu as pltpu
from jax.sharding import PartitionSpec as P

HEADS = 2
TLX = 2
TLY = 2
LANES = 128
BF = jnp.bfloat16
F32 = jnp.float32

sharpness = 32.0
epsilon = 1e-06
neighbour_steps = ((-1, -1), (-1, 0), (-1, 1), (0, -1), (0, 1), (1, -1), (1, 0), (1, 1))
VMEM = pltpu.VMEM
SMEM = pltpu.SMEM


def dot(a, b):
    return jnp.dot(a, b, preferred_element_type=F32)


def dot_t(a, b):
    return lax.dot_general(a, b, (((1,), (1,)), ((), ())), preferred_element_type=F32)


def head_ones():
    row = lax.broadcasted_iota(jnp.int32, (LANES, LANES), 0)
    col = lax.broadcasted_iota(jnp.int32, (LANES, LANES), 1)
    half = LANES // HEADS
    return jnp.where((row // half) == (col // half), 1.0, 0.0).astype(BF)


def unit(v, ones):
    return v * lax.rsqrt(dot((v * v).astype(BF), ones) + epsilon)


def silu(v):
    half = (0.5 * v).astype(BF)
    return half + half * jnp.tanh(half)


def quotient(a, b):
    guess = pl.reciprocal(b, approx=True)
    return a * (guess * (2.0 - b * guess))


def place():
    return lax.axis_index("tx"), lax.axis_index("zh"), lax.axis_index("zl")


def block_of(half_id, low):
    return low if half_id else 1 - low


def encode_rows(half_id, quota, chunk, points, index_ready, weights_ready, w1_ref, w2_ref, w3_ref, index_s, feat_ref, wide_ref, xs):
    rows_total = points.shape[0] // 2
    group = chunk // quota
    wide_ref[...] = points[...].astype(F32)
    index_ready()

    def gather(c, buffer, first, last):
        for r in range(first, last):
            member = r // quota
            spot = (member * 2 + block_of(half_id, member % 2)) * quota + r % quota
            i = index_s[c * (2 * chunk // LANES) + spot // LANES, spot % LANES]
            buffer[pl.ds(r, 1), :] = wide_ref[pl.ds(i, 1), :]

    def layer(x, w, ahead, cuts):
        parts = []
        step = w.shape[1] // 2
        for k in range(2):
            ahead(cuts[k], cuts[k + 1])
            parts.append(silu(dot(x, w[:, k * step : (k + 1) * step])))
        return jnp.concatenate(parts, axis=1)

    def apply(c, buffer, ahead):
        cuts = [chunk * k // 5 for k in range(6)]
        hidden = layer(buffer[...].astype(BF), w1_ref, ahead, cuts[:3])
        hidden = layer(hidden, w2_ref.at[0], ahead, cuts[2:5])
        ahead(cuts[4], cuts[5])
        out = dot(hidden, w3_ref[...]).astype(BF)
        for k in range(group):
            feat_ref[c * group + k] = out[k * quota : (k + 1) * quota]

    chunks = rows_total // chunk
    gather(0, xs[0], 0, chunk)
    weights_ready()

    def step(k, carry):
        c = 2 * k
        apply(c, xs[0], lambda a, b: gather(c + 1, xs[1], a, b))
        apply(c + 1, xs[1], lambda a, b: gather(jnp.minimum(c + 2, chunks - 1), xs[0], a, b))
        return carry

    lax.fori_loop(0, chunks // 2, step, 0)


def encode_first_kernel(
    grid_y,
    along_y,
    quota,
    points_hbm,
    w1_hbm,
    w2_hbm,
    w3_hbm,
    counts_hbm,
    order_hbm,
    feat_ref,
    index_ref,
    counts_s,
    off_ref,
    index_s,
    wide_ref,
    xa_ref,
    xb_ref,
    points_ref,
    w1_ref,
    w2_ref,
    w3_ref,
    order_ref,
    sems,
):
    tx, zh, zl = place()
    own = tx * along_y + zh * (along_y // 2) + zl
    sources = (counts_hbm.at[own], order_hbm, points_hbm, w1_hbm, w2_hbm, w3_hbm)
    targets = (counts_s, order_ref, points_ref, w1_ref, w2_ref, w3_ref)
    copies = [
        pltpu.make_async_copy(a, b, sems.at[k]) for k, (a, b) in enumerate(zip(sources, targets))
    ]
    for copy in copies:
        copy.start()
    tiles = counts_s.shape[0]
    order_rows = order_ref.shape[0]
    rows_total = points_ref.shape[0]
    copies[0].wait()

    def add_up(g, total):
        off_ref[g] = total
        return total + counts_s[g]

    lax.fori_loop(0, tiles, add_up, jnp.int32(0), unroll=8)
    copies[1].wait()
    lane = lax.broadcasted_iota(jnp.int32, (1, LANES), 1)

    def run_of(start):
        line = start >> 7
        shift = start & (LANES - 1)
        first = order_ref[pl.ds(jnp.clip(line, 0, order_rows - 1), 1), :]
        second = order_ref[pl.ds(jnp.clip(line + 1, 0, order_rows - 1), 1), :]
        merged = jnp.where(lane < shift, second, first)
        return pltpu.roll(merged, (LANES - shift) & (LANES - 1), 1)

    per_line = LANES // quota

    def index_line(line, carry):
        value = jnp.zeros((1, LANES), jnp.int32)
        for k in range(per_line):
            d = line * per_line + k
            g1 = (d // along_y) * (TLX * grid_y) + (d % along_y) * TLY
            n1 = counts_s[g1] + counts_s[g1 + 1]
            run1 = run_of(off_ref[g1] - k * quota)
            run2 = run_of(off_ref[g1 + grid_y] - n1 - k * quota)
            both = jnp.where(lane < k * quota + n1, run1, run2)
            value = both if k == 0 else jnp.where(lane >= k * quota, both, value)
        index_ref[pl.ds(line, 1), :] = value
        return carry

    lax.fori_loop(0, rows_total // LANES, index_line, 0, unroll=8)
    copy = pltpu.make_async_copy(index_ref, index_s, sems.at[6])
    copy.start()
    copies[2].wait()

    def weights_ready():
        for k in (3, 4, 5):
            copies[k].wait()

    encode_rows(
        0, quota, xa_ref.shape[0], points_ref, copy.wait, weights_ready, w1_ref, w2_ref, w3_ref, index_s,
        feat_ref, wide_ref, (xa_ref, xb_ref),
    )


def encode_second_kernel(
    quota, points_ref, w1_ref, w2_ref, w3_ref, index_any, feat_ref, index_s, wide_ref, xa_ref, xb_ref, sem
):
    copy = pltpu.make_async_copy(index_any, index_s, sem)
    copy.start()
    encode_rows(
        1, quota, xa_ref.shape[0], points_ref, copy.wait, lambda: None, w1_ref, w2_ref, w3_ref, index_s,
        feat_ref, wide_ref, (xa_ref, xb_ref),
    )


def tile_of(position, counts_ref, pieces, piece_id, grid_y):
    bounds = [None, None, None]
    for k, (s, base) in enumerate(pieces):
        n0 = counts_ref[s, base]
        n1 = counts_ref[s, base + 1]
        n2 = counts_ref[s, base + grid_y]
        for i, found in enumerate((n0, n0 + n1, n0 + n1 + n2)):
            if k == 0:
                bounds[i] = jnp.full(position.shape, found, jnp.int32)
            else:
                bounds[i] = jnp.where(piece_id >= k, found, bounds[i])
    return sum((position >= b).astype(jnp.int32) for b in bounds)


def pieces_of(first, group, half_id, along_y):
    tx, zh, zl = place()
    lows = along_y // 2
    block = zl * 2 + block_of(half_id, zl)
    base = tx * (TLX * along_y * TLY) + block * TLY
    found = []
    for k in range(group):
        member = first + k
        found.append(((member // lows) * along_y + zh * lows + member % lows, base))
    return found


def partial_kernel(half_id, along_y, rows_ref, counts_ref, *rest):
    num_ref = rest[-1]
    if half_id:
        query_ref, wv_ref, proj_ref, before_any, own_ref, send_ref = rest[:-1]
    else:
        inducing_ref, proj_ref, own_ref, send_ref, query_ref, wv_ref = rest[:-1]
    members, quota, width = rows_ref.shape
    grid_y = along_y * TLY
    half = LANES // HEADS
    group = min(512 // quota, members)
    chunk = group * quota
    ones = head_ones()
    lane = lax.broadcasted_iota(jnp.int32, (1, LANES), 1)
    left = lane < half
    if half_id:
        queries = query_ref[...]
        wv_t = wv_ref[...]
    else:
        queries = unit(dot(inducing_ref[...], proj_ref[0]), ones)
        queries = jnp.concatenate(
            [jnp.where(left, queries, 0.0), jnp.where(left, 0.0, queries)], axis=0
        ).astype(BF)
        wv_t = proj_ref[2].astype(F32).T.astype(BF)
        query_ref[...] = queries
        wv_ref[...] = wv_t
    spot = lax.broadcasted_iota(jnp.int32, (16, chunk), 1)
    tile_row = lax.broadcasted_iota(jnp.int32, (16, chunk), 0)
    for c in range(members // group):
        x = jnp.concatenate([rows_ref[c * group + k] for k in range(group)], axis=0)
        keys = unit(dot(x, proj_ref[1]), ones).astype(BF)
        weights = jnp.exp2(dot_t(keys, queries) * (sharpness * math.log2(math.e))).astype(BF)
        values = dot_t(wv_t, x).astype(BF)
        pieces = pieces_of(c * group, group, half_id, along_y)
        tile = tile_of(spot % quota, counts_ref, pieces, spot // quota, grid_y)
        stacked = []
        for t in range(4):
            mask = jnp.where(tile == t, 1.0, 0.0).astype(BF)
            stacked += [values[k : k + 16] * mask for k in range(0, LANES, 16)]
        stacked.append(jnp.where(tile_row == tile, 1.0, 0.0).astype(BF))
        sums = dot(jnp.concatenate(stacked, axis=0), weights)
        if c == 0:
            num_ref[...] = sums
        else:
            num_ref[...] += sums
    last = 4 * LANES
    for t in range(4):
        rows = slice(t * LANES, (t + 1) * LANES)
        value = jnp.concatenate(
            [
                num_ref[t * LANES : t * LANES + half, :LANES],
                num_ref[t * LANES + half : (t + 1) * LANES, LANES:],
            ],
            axis=0,
        )
        own_ref[rows, :] = value
        send_ref[rows, :] = value.astype(BF)
    totals = jnp.concatenate(
        [num_ref[last : last + 4, h * LANES : (h + 1) * LANES] for h in range(HEADS)]
        + [jnp.zeros((8, LANES), F32)],
        axis=0,
    )
    own_ref[last:, :] = totals
    send_ref[last:, :] = totals.astype(BF)

def row_bounds(piece, counts_ref, grid_y):
    s, base = piece
    n0 = counts_ref[s, base]
    n1 = n0 + counts_ref[s, base + 1]
    return n0, n1, n1 + counts_ref[s, base + grid_y]


def queries_kernel(along_y, rows0_ref, rows1_ref, counts_ref, proj_ref, column_any, out_ref):
    ones = head_ones()
    for half_id, rows_ref in enumerate((rows0_ref, rows1_ref)):
        members, quota, width = rows_ref.shape
        group = min(512 // quota, members)
        row = lax.broadcasted_iota(jnp.int32, (quota, LANES), 0)
        for c in range(members // group):
            x = jnp.concatenate([rows_ref[c * group + k] for k in range(group)], axis=0)
            query = unit(dot(x, proj_ref[0]), ones)
            pieces = pieces_of(c * group, group, half_id, along_y)
            for k in range(group):
                bounds = row_bounds(pieces[k], counts_ref, along_y * TLY)
                past = [row >= b for b in bounds]
                mine = query[k * quota : (k + 1) * quota]
                masks = (~past[0], past[0] & ~past[1], past[1] & ~past[2], past[2])
                out_ref[half_id, c * group + k] = jnp.concatenate(
                    [jnp.where(m, mine, 0.0).astype(BF) for m in masks], axis=1
                )


def summarize(half_id, own_ref, other_ref, inducing_ref, proj_ref, store):
    half = LANES // HEADS
    last = 4 * LANES
    totals = own_ref[last:, :] + other_ref[last:, :].astype(F32)
    for t in range(4):
        rows = slice(t * LANES, (t + 1) * LANES)
        value = own_ref[rows, :] + other_ref[rows, :].astype(F32)
        attended = jnp.concatenate(
            [value[:half] / totals[t : t + 1], value[half:] / totals[t + 4 : t + 5]], axis=0
        )
        out = inducing_ref[...].astype(F32) + dot(attended.T.astype(BF), proj_ref[3])
        store(t // TLY, t % TLY, out.astype(BF))


def combine_first_kernel(own_ref, other_ref, inducing_ref, proj_ref, out_ref, column_ref):
    def store(x, y, value):
        out_ref[x, y] = value

    summarize(0, own_ref, other_ref, inducing_ref, proj_ref, store)
    for x in range(TLX):
        column_ref[x] = jnp.where(lax.axis_index("zl") == 0, out_ref[x, TLY - 1], out_ref[x, 0])


def combine_second_kernel(
    own_ref,
    other_ref,
    inducing_ref,
    proj_ref,
    first_ref,
    column_ref,
    query_any,
    out0_ref,
    out1_ref,
    near_pair_ref,
    far_pair_ref,
):
    outs = (out0_ref, out1_ref)
    zl = lax.axis_index("zl")

    def store(x, y, value):
        outs[x][block_of(1, zl) * TLY + y] = value

    for x in range(TLX):
        for y in range(TLY):
            outs[x][block_of(0, zl) * TLY + y] = first_ref[x, y]
        outs[x][2 * TLY] = column_ref[x]
    summarize(1, own_ref, other_ref, inducing_ref, proj_ref, store)
    even = lax.axis_index("tx") % 2 == 0
    for j in range(out0_ref.shape[0]):
        near_pair_ref[j] = jnp.where(even, out1_ref[j], out0_ref[j])
        far_pair_ref[j] = jnp.where(even, out0_ref[j], out1_ref[j])


def mixture_kernel(
    own0_ref,
    own1_ref,
    near_pair_ref,
    far_pair_ref,
    proj_ref,
    mixing_ref,
    key_ref,
    value_ref,
    mid_ref,
    side_ref,
):
    half = LANES // HEADS
    blocks = key_ref.shape[0]
    tall = blocks * TLY
    low = lax.axis_index("zl")

    row = lax.broadcasted_iota(jnp.int32, (LANES, LANES), 0)
    col = lax.broadcasted_iota(jnp.int32, (LANES, LANES), 1)
    eye = jnp.where(row == col, 1.0, 0.0).astype(BF)
    blank = jnp.zeros((LANES, LANES), BF)

    def mix(a, b):
        return eye if (a, b) == (0, 0) else mixing_ref[neighbour_steps.index((a, b))]

    for k, a in enumerate((-1, 0, 1)):
        rows = slice(k * 2 * LANES, (k + 1) * 2 * LANES)
        mid_ref[rows, :] = jnp.concatenate(
            [
                jnp.concatenate([mix(a, 0), mix(a, -1)], axis=1),
                jnp.concatenate([mix(a, 1), mix(a, 0)], axis=1),
            ],
            axis=0,
        )
    for k, b in enumerate((-1, 1)):
        side_ref[k] = jnp.concatenate(
            [
                jnp.concatenate([mix(0, b), mix(-1, b)], axis=1),
                jnp.concatenate([mix(1, b), mix(0, b)], axis=1),
                jnp.concatenate([mix(-1, b), blank], axis=1),
                jnp.concatenate([blank, mix(1, b)], axis=1),
            ],
            axis=0,
        )
    ones = head_ones()
    lane = lax.broadcasted_iota(jnp.int32, (1, LANES), 1)
    left = lane < half
    even = lax.axis_index("tx") % 2 == 0

    def held(i, j):
        if i in (1, 2):
            return (own0_ref, own1_ref)[i - 1][j]
        near, far = near_pair_ref[j], far_pair_ref[j]
        return jnp.where(even, far, near) if i == 0 else jnp.where(even, near, far)

    grid = [[held(i, j) for j in range(tall + 1)] for i in range(4)]

    def tile(i, j):
        if 0 <= j < tall:
            return grid[i][j]
        return jnp.where(low == (1 if j < 0 else 0), grid[i][tall], blank)

    mids, lefts, rights = [], [], []
    for i in range(2):
        for b in range(blocks):
            mids.append(
                jnp.concatenate(
                    [tile(i + r, 2 * b + s) for r in range(3) for s in range(2)], axis=1
                )
            )
    for b in range(blocks):
        lefts.append(jnp.concatenate([tile(i, 2 * b - 1) for i in (1, 2, 0, 3)], axis=1))
        rights.append(jnp.concatenate([tile(i, 2 * b + 2) for i in (1, 2, 0, 3)], axis=1))
    middle = dot(jnp.concatenate(mids, axis=0), mid_ref[...])
    from_left = dot(jnp.concatenate(lefts, axis=0), side_ref[0])
    from_right = dot(jnp.concatenate(rights, axis=0), side_ref[1])
    mixtures = []
    for b in range(blocks):
        span = slice(b * LANES, (b + 1) * LANES)
        for i in range(2):
            m = middle[(i * blocks + b) * LANES : (i * blocks + b + 1) * LANES]
            cols = slice(i * LANES, (i + 1) * LANES)
            mixtures.append((m[:, :LANES] + from_left[span, cols]).astype(BF))
            mixtures.append((m[:, LANES:] + from_right[span, cols]).astype(BF))
    mixtures = jnp.concatenate(mixtures, axis=0)
    keys = unit(dot(mixtures, proj_ref[1]), ones)
    values = dot(mixtures, proj_ref[2])
    for b in range(blocks):
        spans = [slice((b * 4 + t) * LANES, (b * 4 + t + 1) * LANES) for t in range(4)]
        for h in range(HEADS):
            mine = left if h == 0 else ~left
            key_ref[b, h * LANES : (h + 1) * LANES, :] = jnp.concatenate(
                [jnp.where(mine, keys[s], 0.0) for s in spans], axis=1
            ).astype(BF)
            flags = jnp.broadcast_to(jnp.where(mine, 1.0, 0.0), (LANES, LANES))
            value_ref[b, h * LANES : (h + 1) * LANES, :] = jnp.concatenate(
                [jnp.where(mine, values[s], 0.0) for s in spans] + [flags], axis=1
            ).astype(BF)


def attend_kernel(
    along_y, rows0_ref, rows1_ref, query_ref, counts_ref, key_ref, value_ref, proj_ref, out_ref
):
    members, quota, width = rows0_ref.shape
    group = min(512 // quota, members)
    row = lax.broadcasted_iota(jnp.int32, (quota, LANES), 0)
    for half_id, rows_ref in enumerate((rows0_ref, rows1_ref)):
        block = block_of(half_id, lax.axis_index("zl"))
        for c in range(members // group):
            expanded = jnp.concatenate(
                [query_ref[half_id, c * group + k] for k in range(group)], axis=0
            )
            scores = dot_t(expanded, key_ref[block])
            weights = jnp.exp2(scores * (sharpness * math.log2(math.e))).astype(BF)
            every = dot(weights, value_ref[block])
            pieces = pieces_of(c * group, group, half_id, along_y)
            attended = []
            for k in range(group):
                bounds = row_bounds(pieces[k], counts_ref, along_y * TLY)
                part = every[k * quota : (k + 1) * quota]
                picked = part[:, :LANES]
                for t, bound in enumerate(bounds):
                    tile = part[:, (t + 1) * LANES : (t + 2) * LANES]
                    picked = jnp.where(row >= bound, tile, picked)
                attended.append(quotient(picked, part[:, 4 * LANES :]).astype(BF))
            x = jnp.concatenate([rows_ref[c * group + k] for k in range(group)], axis=0)
            added = dot(jnp.concatenate(attended, axis=0), proj_ref[3])
            result = (x.astype(F32) + added).astype(BF)
            for k in range(group):
                out_ref[c * group + k, half_id] = result[k * quota : (k + 1) * quota]


def scatter_kernel(rows_ref, index_ref, out_ref, wide_ref, part_ref):
    chunk = part_ref.shape[0]
    members, halves, quota, width = rows_ref.shape
    group = chunk // (halves * quota)

    def step(c, carry):
        for k in range(group):
            for half_id in range(halves):
                row = (k * halves + block_of(half_id, k % 2)) * quota
                part_ref[row : row + quota, :] = rows_ref[c * group + k, half_id].astype(F32)
        for r in range(chunk):
            i = index_ref[c * (chunk // LANES) + r // LANES, r % LANES]
            wide_ref[pl.ds(i, 1), :] = part_ref[pl.ds(r, 1), :]
        return carry

    lax.fori_loop(0, members // group, step, 0)
    out_ref[...] = wide_ref[...].astype(BF)


def call(kernel, name, out_shape, in_specs, scratch, micros, operands, megabytes=20, **more):
    spaces = {"v": pltpu.VMEM, "s": pltpu.SMEM, "a": pl.ANY}
    many = isinstance(out_shape, tuple)
    whole = pl.BlockSpec(memory_space=pltpu.VMEM)
    return pl.pallas_call(
        kernel,
        out_shape=out_shape,
        in_specs=[pl.BlockSpec(memory_space=spaces[c]) for c in in_specs],
        out_specs=(whole,) * len(out_shape) if many else whole,
        scratch_shapes=scratch,
        compiler_params=pltpu.CompilerParams(vmem_limit_bytes=megabytes * 1024 * 1024),
        cost_estimate=pl.CostEstimate(
            flops=int(micros * 5e8), bytes_accessed=int(micros * 1e6), transcendentals=0
        ),
        name=name,
        **more,
    )(*operands)


def body(
    points,
    embed_weight,
    inner_weights,
    output_weight,
    counts,
    point_order,
    inducing,
    first_proj,
    second_proj,
    mixing,
):
    along_x = lax.axis_size("tx")
    highs = lax.axis_size("zh")
    lows = lax.axis_size("zl")
    along_y = highs * lows
    point_count, width = points.shape
    quota = point_count // (along_x * along_y)
    grid_y = along_y * TLY
    blocks = 2
    members = along_x * lows
    tall = blocks * TLY
    lines = point_count // LANES
    chunk = 512
    half_rows = (members, quota, width)

    def shape(sizes, dtype=BF):
        return jax.ShapeDtypeStruct(sizes, dtype)

    weights = (embed_weight, inner_weights, output_weight)
    buffers = [
        VMEM((point_count, width), F32),
        VMEM((chunk, width), F32),
        VMEM((chunk, width), F32),
    ]
    first, index = call(
        functools.partial(encode_first_kernel, grid_y, along_y, quota),
        "encode_first",
        (shape(half_rows), shape((lines, LANES), jnp.int32)),
        "aaaaaa",
        [
            SMEM((counts.shape[1],), jnp.int32),
            SMEM((counts.shape[1],), jnp.int32),
            SMEM((lines, LANES), jnp.int32),
        ]
        + buffers
        + [VMEM(a.shape, BF) for a in (points, *weights)]
        + [VMEM((lines, LANES), jnp.int32), pltpu.SemaphoreType.DMA((7,))],
        8,
        (points, *weights, counts, point_order.reshape(lines, LANES)),
        megabytes=56,
    )
    second = call(
        functools.partial(encode_second_kernel, quota),
        "encode_second",
        shape(half_rows),
        "vvvva",
        [SMEM((lines, LANES), jnp.int32)] + buffers + [pltpu.SemaphoreType.DMA],
        6,
        (points, *weights, index),
    )

    def exchange(rows):
        return lax.all_to_all(rows, ("tx", "zl"), split_axis=0, concat_axis=0, tiled=True)

    rows0 = exchange(first)
    rows1 = exchange(second)

    part_rows = 4 * LANES + 16
    parts = (shape((part_rows, LANES), F32), shape((part_rows, LANES)))
    sums = [VMEM((part_rows, HEADS * LANES), F32)]
    own0, send0, first_queries, value_weight = call(
        functools.partial(partial_kernel, 0, along_y),
        "partial_first",
        parts
        + (shape((HEADS * LANES, width)), shape((LANES, width))),
        "vsvv",
        sums,
        3,
        (rows0, counts, inducing, first_proj),
    )
    pairs = [(h, l) for h in range(highs) for l in range(lows)]

    def swap(value, flip_high, flip_low):
        steps = []
        for h, l in pairs:
            other_h = highs - 1 - h if flip_high else h
            other_l = lows - 1 - l if flip_low else l
            steps.append((h * lows + l, other_h * lows + other_l))
        return lax.ppermute(value, ("zh", "zl"), steps)

    other0 = swap(send0, True, False)
    first_half, border = call(
        combine_first_kernel,
        "combine_first",
        (shape((TLX, TLY, LANES, width)), shape((TLX, LANES, width))),
        "vvvv",
        [],
        0.3,
        (own0, other0, inducing, first_proj),
    )
    column = swap(border, False, True)
    own1, send1 = call(
        functools.partial(partial_kernel, 1, along_y),
        "partial_second",
        parts,
        "vsvvva",
        sums,
        3,
        (rows1, counts, first_queries, value_weight, first_proj, border),
    )
    other1 = swap(send1, True, False)
    queries = call(
        functools.partial(queries_kernel, along_y),
        "point_queries",
        shape((2, members, quota, 4 * width)),
        "vvsva",
        [],
        3,
        (rows0, rows1, counts, second_proj, column),
    )
    line = shape((tall + 1, LANES, width))
    summary0, summary1, near_line, far_line = call(
        combine_second_kernel,
        "combine_second",
        (line,) * 4,
        "vvvvvva",
        [],
        0.3,
        (own1, other1, inducing, first_proj, first_half, column, queries),
    )
    near_pairs = [(i, i ^ 1) for i in range(along_x)]
    far_pairs = [(i, ((i + 1) ^ 1) - 1) for i in range(1, along_x - 1)]
    near_line = lax.ppermute(near_line, "tx", near_pairs)
    far_line = lax.ppermute(far_line, "tx", far_pairs)

    keys, values = call(
        mixture_kernel,
        "mix_tiles",
        (shape((blocks, HEADS * LANES, 4 * LANES)), shape((blocks, HEADS * LANES, 5 * LANES))),
        "v" * 6,
        [VMEM((6 * LANES, 2 * LANES), BF), VMEM((2, 4 * LANES, 2 * LANES), BF)],
        4,
        (summary0, summary1, near_line, far_line, second_proj, mixing),
    )

    result = call(
        functools.partial(attend_kernel, along_y),
        "attend_points",
        shape((members, 2, quota, width)),
        "vvvsvvv",
        [],
        7,
        (rows0, rows1, queries, counts, keys, values, second_proj),
    )
    return call(
        scatter_kernel,
        "scatter_rows",
        shape((point_count, width)),
        "vs",
        [VMEM((point_count, width), F32), VMEM((chunk, width), F32)],
        5,
        (exchange(result), index),
    )


def solution(mesh):
    along_x, along_y = mesh.devices.shape
    split = jax.sharding.Mesh(mesh.devices.reshape(along_x, 2, along_y // 2), ("tx", "zh", "zl"))
    rows = P(("tx", "zh", "zl"), None)
    placed = (rows, P(), P(), P(), P(), rows, P(), P(), P(), P())
    return jax.shard_map(body, mesh=split, in_specs=placed, out_specs=rows, check_vma=False)
```

```python
import functools
import math

import jax
import jax.numpy as jnp
from jax import lax
from jax.experimental import pallas as pl
from jax.experimental.pallas import tpu as pltpu
from jax.sharding import PartitionSpec as P

HEADS = 2
TLX = 2
TLY = 2
LANES = 128
GROUP_ROWS = 2048
BF = jnp.bfloat16
F32 = jnp.float32

sharpness = 32.0
epsilon = 1e-06
neighbour_steps = ((-1, -1), (-1, 0), (-1, 1), (0, -1), (0, 1), (1, -1), (1, 0), (1, 1))
VMEM = pltpu.VMEM
SMEM = pltpu.SMEM


def dot(a, b):
    return jnp.dot(a, b, preferred_element_type=F32)


def dot_t(a, b):
    return lax.dot_general(a, b, (((1,), (1,)), ((), ())), preferred_element_type=F32)


def head_ones():
    row = lax.broadcasted_iota(jnp.int32, (LANES, LANES), 0)
    col = lax.broadcasted_iota(jnp.int32, (LANES, LANES), 1)
    half = LANES // HEADS
    return jnp.where((row // half) == (col // half), 1.0, 0.0).astype(BF)


def unit(v, ones):
    return v * lax.rsqrt(dot((v * v).astype(BF), ones) + epsilon)


def silu(v):
    half = 0.5 * v
    return (half + half * jnp.tanh(half)).astype(BF)


def quotient(a, b):
    guess = pl.reciprocal(b, approx=True)
    return a * (guess * (2.0 - b * guess))


def place():
    return lax.axis_index("tx"), lax.axis_index("zh"), lax.axis_index("zl")


def block_of(half_id, low):
    return low if half_id else 1 - low


def encode_rows(half_id, quota, chunk, points, index_ready, weights_ready, w1_ref, w2_ref, w3_ref, index_s, feat_ref, wide_ref, xs):
    rows_total = points.shape[0] // 2
    group = chunk // quota
    wide_ref[...] = points[...].astype(F32)
    index_ready()

    def gather(c, buffer, first, last):
        for r in range(first, last):
            member = r // quota
            spot = (member * 2 + block_of(half_id, member % 2)) * quota + r % quota
            i = index_s[c * (2 * chunk // LANES) + spot // LANES, spot % LANES]
            buffer[pl.ds(r, 1), :] = wide_ref[pl.ds(i, 1), :]

    def layer(x, w, ahead, cuts):
        parts = []
        step = w.shape[1] // 2
        for k in range(2):
            ahead(cuts[k], cuts[k + 1])
            parts.append(silu(dot(x, w[:, k * step : (k + 1) * step])))
        return jnp.concatenate(parts, axis=1)

    def apply(c, buffer, ahead):
        cuts = [chunk * k // 5 for k in range(6)]
        hidden = layer(buffer[...].astype(BF), w1_ref, ahead, cuts[:3])
        hidden = layer(hidden, w2_ref.at[0], ahead, cuts[2:5])
        ahead(cuts[4], cuts[5])
        out = dot(hidden, w3_ref[...]).astype(BF)
        for k in range(group):
            feat_ref[c * group + k] = out[k * quota : (k + 1) * quota]

    chunks = rows_total // chunk
    gather(0, xs[0], 0, chunk)
    weights_ready()
    for c in range(chunks):

        def ahead(a, b):
            if c + 1 < chunks:
                gather(c + 1, xs[(c + 1) % 2], a, b)

        apply(c, xs[c % 2], ahead)


def encode_first_kernel(
    grid_y,
    along_y,
    quota,
    points_hbm,
    w1_hbm,
    w2_hbm,
    w3_hbm,
    counts_hbm,
    order_hbm,
    feat_ref,
    index_ref,
    counts_s,
    off_ref,
    index_s,
    wide_ref,
    xa_ref,
    xb_ref,
    points_ref,
    w1_ref,
    w2_ref,
    w3_ref,
    order_ref,
    sems,
):
    tx, zh, zl = place()
    own = tx * along_y + zh * (along_y // 2) + zl
    sources = (counts_hbm.at[own], order_hbm, points_hbm, w1_hbm, w2_hbm, w3_hbm)
    targets = (counts_s, order_ref, points_ref, w1_ref, w2_ref, w3_ref)
    copies = [
        pltpu.make_async_copy(a, b, sems.at[k]) for k, (a, b) in enumerate(zip(sources, targets))
    ]
    for copy in copies:
        copy.start()
    tiles = counts_s.shape[0]
    order_rows = order_ref.shape[0]
    rows_total = points_ref.shape[0]
    copies[0].wait()

    def add_up(g, total):
        off_ref[g] = total
        return total + counts_s[g]

    lax.fori_loop(0, tiles, add_up, jnp.int32(0), unroll=8)
    copies[1].wait()
    lane = lax.broadcasted_iota(jnp.int32, (1, LANES), 1)

    def run_of(start):
        line = start >> 7
        shift = start & (LANES - 1)
        first = order_ref[pl.ds(jnp.clip(line, 0, order_rows - 1), 1), :]
        second = order_ref[pl.ds(jnp.clip(line + 1, 0, order_rows - 1), 1), :]
        merged = jnp.where(lane < shift, second, first)
        return pltpu.roll(merged, (LANES - shift) & (LANES - 1), 1)

    per_line = LANES // quota

    def index_line(line, carry):
        value = jnp.zeros((1, LANES), jnp.int32)
        for k in range(per_line):
            d = line * per_line + k
            g1 = (d // along_y) * (TLX * grid_y) + (d % along_y) * TLY
            n1 = counts_s[g1] + counts_s[g1 + 1]
            run1 = run_of(off_ref[g1] - k * quota)
            run2 = run_of(off_ref[g1 + grid_y] - n1 - k * quota)
            both = jnp.where(lane < k * quota + n1, run1, run2)
            value = both if k == 0 else jnp.where(lane >= k * quota, both, value)
        index_ref[pl.ds(line, 1), :] = value
        return carry

    lax.fori_loop(0, rows_total // LANES, index_line, 0, unroll=8)
    copy = pltpu.make_async_copy(index_ref, index_s, sems.at[6])
    copy.start()
    copies[2].wait()

    def weights_ready():
        for k in (3, 4, 5):
            copies[k].wait()

    encode_rows(
        0, quota, xa_ref.shape[0], points_ref, copy.wait, weights_ready, w1_ref, w2_ref, w3_ref, index_s,
        feat_ref, wide_ref, (xa_ref, xb_ref),
    )


def encode_second_kernel(
    quota, points_ref, w1_ref, w2_ref, w3_ref, index_any, feat_ref, index_s, wide_ref, xa_ref, xb_ref, sem
):
    copy = pltpu.make_async_copy(index_any, index_s, sem)
    copy.start()
    encode_rows(
        1, quota, xa_ref.shape[0], points_ref, copy.wait, lambda: None, w1_ref, w2_ref, w3_ref, index_s,
        feat_ref, wide_ref, (xa_ref, xb_ref),
    )


def tile_of(position, counts_ref, pieces, piece_id, grid_y):
    bounds = [None, None, None]
    for k, (s, base) in enumerate(pieces):
        n0 = counts_ref[s, base]
        n1 = counts_ref[s, base + 1]
        n2 = counts_ref[s, base + grid_y]
        for i, found in enumerate((n0, n0 + n1, n0 + n1 + n2)):
            if k == 0:
                bounds[i] = jnp.full(position.shape, found, jnp.int32)
            else:
                bounds[i] = jnp.where(piece_id >= k, found, bounds[i])
    return sum((position >= b).astype(jnp.int32) for b in bounds)


def pieces_of(first, group, half_id, along_y):
    tx, zh, zl = place()
    lows = along_y // 2
    block = zl * 2 + block_of(half_id, zl)
    base = tx * (TLX * along_y * TLY) + block * TLY
    found = []
    for k in range(group):
        member = first + k
        found.append(((member // lows) * along_y + zh * lows + member % lows, base))
    return found


def partial_kernel(half_id, along_y, rows_ref, counts_ref, *rest):
    num_ref = rest[-1]
    if half_id:
        query_ref, wv_ref, proj_ref, own_ref, send_ref = rest[:-1]
    else:
        inducing_ref, proj_ref, own_ref, send_ref, query_ref, wv_ref = rest[:-1]
    members, quota, width = rows_ref.shape
    grid_y = along_y * TLY
    half = LANES // HEADS
    group = min(GROUP_ROWS // quota, members)
    chunk = group * quota
    ones = head_ones()
    lane = lax.broadcasted_iota(jnp.int32, (1, LANES), 1)
    left = lane < half
    if half_id:
        queries = query_ref[...]
        wv_t = wv_ref[...]
    else:
        queries = unit(dot(inducing_ref[...], proj_ref[0]), ones)
        queries = jnp.concatenate(
            [jnp.where(left, queries, 0.0), jnp.where(left, 0.0, queries)], axis=0
        ).astype(BF)
        wv_t = proj_ref[2].astype(F32).T.astype(BF)
        query_ref[...] = queries
        wv_ref[...] = wv_t
    spot = lax.broadcasted_iota(jnp.int32, (16, chunk), 1)
    tile_row = lax.broadcasted_iota(jnp.int32, (16, chunk), 0)
    for c in range(members // group):
        x = jnp.concatenate([rows_ref[c * group + k] for k in range(group)], axis=0)
        keys = unit(dot(x, proj_ref[1]), ones).astype(BF)
        weights = jnp.exp2(dot_t(keys, queries) * (sharpness * math.log2(math.e))).astype(BF)
        values = dot_t(wv_t, x).astype(BF)
        pieces = pieces_of(c * group, group, half_id, along_y)
        tile = tile_of(spot % quota, counts_ref, pieces, spot // quota, grid_y)
        stacked = []
        for t in range(4):
            mask = jnp.where(tile == t, 1.0, 0.0).astype(BF)
            stacked += [values[k : k + 16] * mask for k in range(0, LANES, 16)]
        stacked.append(jnp.where(tile_row == tile, 1.0, 0.0).astype(BF))
        sums = dot(jnp.concatenate(stacked, axis=0), weights)
        if c == 0:
            num_ref[...] = sums
        else:
            num_ref[...] += sums
    last = 4 * LANES
    for t in range(4):
        rows = slice(t * LANES, (t + 1) * LANES)
        value = jnp.concatenate(
            [
                num_ref[t * LANES : t * LANES + half, :LANES],
                num_ref[t * LANES + half : (t + 1) * LANES, LANES:],
            ],
            axis=0,
        )
        own_ref[rows, :] = value
        send_ref[rows, :] = value.astype(BF)
    totals = jnp.concatenate(
        [num_ref[last : last + 4, h * LANES : (h + 1) * LANES] for h in range(HEADS)]
        + [jnp.zeros((8, LANES), F32)],
        axis=0,
    )
    own_ref[last:, :] = totals
    send_ref[last:, :] = totals.astype(BF)

def row_bounds(piece, counts_ref, grid_y):
    s, base = piece
    n0 = counts_ref[s, base]
    n1 = n0 + counts_ref[s, base + 1]
    return n0, n1, n1 + counts_ref[s, base + grid_y]


def queries_kernel(along_y, rows0_ref, rows1_ref, counts_ref, proj_ref, column_any, out_ref):
    ones = head_ones()
    for half_id, rows_ref in enumerate((rows0_ref, rows1_ref)):
        members, quota, width = rows_ref.shape
        group = min(GROUP_ROWS // quota, members)
        row = lax.broadcasted_iota(jnp.int32, (quota, LANES), 0)
        for c in range(members // group):
            x = jnp.concatenate([rows_ref[c * group + k] for k in range(group)], axis=0)
            query = unit(dot(x, proj_ref[0]), ones)
            pieces = pieces_of(c * group, group, half_id, along_y)
            for k in range(group):
                bounds = row_bounds(pieces[k], counts_ref, along_y * TLY)
                past = [row >= b for b in bounds]
                mine = query[k * quota : (k + 1) * quota]
                masks = (~past[0], past[0] & ~past[1], past[1] & ~past[2], past[2])
                out_ref[half_id, c * group + k] = jnp.concatenate(
                    [jnp.where(m, mine, 0.0).astype(BF) for m in masks], axis=1
                )


def summarize(half_id, own_ref, other_ref, inducing_ref, proj_ref, store):
    half = LANES // HEADS
    last = 4 * LANES
    totals = own_ref[last:, :] + other_ref[last:, :].astype(F32)
    for t in range(4):
        rows = slice(t * LANES, (t + 1) * LANES)
        value = own_ref[rows, :] + other_ref[rows, :].astype(F32)
        attended = jnp.concatenate(
            [value[:half] / totals[t : t + 1], value[half:] / totals[t + 4 : t + 5]], axis=0
        )
        out = inducing_ref[...].astype(F32) + dot(attended.T.astype(BF), proj_ref[3])
        store(t // TLY, t % TLY, out.astype(BF))


def combine_first_kernel(
    own_ref, other_ref, inducing_ref, proj_ref, after_any, out_ref, column_ref
):
    def store(x, y, value):
        out_ref[x, y] = value

    summarize(0, own_ref, other_ref, inducing_ref, proj_ref, store)
    for x in range(TLX):
        column_ref[x] = jnp.where(lax.axis_index("zl") == 0, out_ref[x, TLY - 1], out_ref[x, 0])


def pair_lines(rows, near_ref, far_ref):
    even = lax.axis_index("tx") % 2 == 0
    for y, (low, high) in enumerate(zip(*rows)):
        near_ref[y] = jnp.where(even, high, low)
        far_ref[y] = jnp.where(even, low, high)


def early_lines_kernel(first_ref, column_ref, query_any, near_ref, far_ref):
    rows = [[first_ref[x, y] for y in range(TLY)] + [column_ref[x]] for x in range(TLX)]
    pair_lines(rows, near_ref, far_ref)


def combine_second_kernel(
    own_ref, other_ref, inducing_ref, proj_ref, query_any, out_ref, near_ref, far_ref
):
    def store(x, y, value):
        out_ref[x, y] = value

    summarize(1, own_ref, other_ref, inducing_ref, proj_ref, store)
    pair_lines([[out_ref[x, y] for y in range(TLY)] for x in range(TLX)], near_ref, far_ref)


def mixture_kernel(
    first_ref,
    column_ref,
    second_ref,
    near0_ref,
    far0_ref,
    near1_ref,
    far1_ref,
    proj_ref,
    mixing_ref,
    key_ref,
    value_ref,
    grid_ref,
    mid_ref,
    side_ref,
):
    half = LANES // HEADS
    blocks = key_ref.shape[0]
    tall = blocks * TLY
    low = lax.axis_index("zl")

    row = lax.broadcasted_iota(jnp.int32, (LANES, LANES), 0)
    col = lax.broadcasted_iota(jnp.int32, (LANES, LANES), 1)
    eye = jnp.where(row == col, 1.0, 0.0).astype(BF)
    blank = jnp.zeros((LANES, LANES), BF)

    def mix(a, b):
        return eye if (a, b) == (0, 0) else mixing_ref[neighbour_steps.index((a, b))]

    for k, a in enumerate((-1, 0, 1)):
        rows = slice(k * 2 * LANES, (k + 1) * 2 * LANES)
        mid_ref[rows, :] = jnp.concatenate(
            [
                jnp.concatenate([mix(a, 0), mix(a, -1)], axis=1),
                jnp.concatenate([mix(a, 1), mix(a, 0)], axis=1),
            ],
            axis=0,
        )
    for k, b in enumerate((-1, 1)):
        side_ref[k] = jnp.concatenate(
            [
                jnp.concatenate([mix(0, b), mix(-1, b)], axis=1),
                jnp.concatenate([mix(1, b), mix(0, b)], axis=1),
                jnp.concatenate([mix(-1, b), blank], axis=1),
                jnp.concatenate([blank, mix(1, b)], axis=1),
            ],
            axis=0,
        )
    ones = head_ones()
    lane = lax.broadcasted_iota(jnp.int32, (1, LANES), 1)
    left = lane < half
    even = lax.axis_index("tx") % 2
    near_row = (1 - even) * (TLX + 1)
    far_row = even * (TLX + 1)
    border = (1 - low) * (tall + 1)
    outside = low * (tall + 1)
    for x in range(TLX):
        for y in range(TLY):
            grid_ref[1 + x, 1 + block_of(0, low) * TLY + y] = first_ref[x, y]
            grid_ref[1 + x, 1 + block_of(1, low) * TLY + y] = second_ref[x, y]
        grid_ref[1 + x, border] = column_ref[x]
    for line, early_ref, late_ref in ((near_row, near0_ref, near1_ref), (far_row, far0_ref, far1_ref)):
        for y in range(TLY):
            grid_ref[line, 1 + block_of(0, low) * TLY + y] = early_ref[y]
            grid_ref[line, 1 + block_of(1, low) * TLY + y] = late_ref[y]
        grid_ref[line, border] = early_ref[TLY]
    for x in range(TLX + 2):
        grid_ref[x, outside] = blank

    def tile(i, j):
        return grid_ref[i, j + 1]

    mids, lefts, rights = [], [], []
    for i in range(2):
        for b in range(blocks):
            mids.append(
                jnp.concatenate(
                    [tile(i + r, 2 * b + s) for r in range(3) for s in range(2)], axis=1
                )
            )
    for b in range(blocks):
        lefts.append(jnp.concatenate([tile(i, 2 * b - 1) for i in (1, 2, 0, 3)], axis=1))
        rights.append(jnp.concatenate([tile(i, 2 * b + 2) for i in (1, 2, 0, 3)], axis=1))
    middle = dot(jnp.concatenate(mids, axis=0), mid_ref[...])
    from_left = dot(jnp.concatenate(lefts, axis=0), side_ref[0])
    from_right = dot(jnp.concatenate(rights, axis=0), side_ref[1])
    mixtures = []
    for b in range(blocks):
        span = slice(b * LANES, (b + 1) * LANES)
        for i in range(2):
            m = middle[(i * blocks + b) * LANES : (i * blocks + b + 1) * LANES]
            cols = slice(i * LANES, (i + 1) * LANES)
            mixtures.append((m[:, :LANES] + from_left[span, cols]).astype(BF))
            mixtures.append((m[:, LANES:] + from_right[span, cols]).astype(BF))
    mixtures = jnp.concatenate(mixtures, axis=0)
    keys = unit(dot(mixtures, proj_ref[1]), ones)
    values = dot(mixtures, proj_ref[2])
    for b in range(blocks):
        spans = [slice((b * 4 + t) * LANES, (b * 4 + t + 1) * LANES) for t in range(4)]
        for h in range(HEADS):
            mine = left if h == 0 else ~left
            key_ref[b, h * LANES : (h + 1) * LANES, :] = jnp.concatenate(
                [jnp.where(mine, keys[s], 0.0) for s in spans], axis=1
            ).astype(BF)
            flags = jnp.broadcast_to(jnp.where(mine, 1.0, 0.0), (LANES, LANES))
            value_ref[b, h * LANES : (h + 1) * LANES, :] = jnp.concatenate(
                [jnp.where(mine, values[s], 0.0) for s in spans] + [flags], axis=1
            ).astype(BF)


def attend_kernel(
    along_y, rows0_ref, rows1_ref, query_ref, counts_ref, key_ref, value_ref, proj_ref, out_ref
):
    members, quota, width = rows0_ref.shape
    group = min(GROUP_ROWS // quota, members)
    row = lax.broadcasted_iota(jnp.int32, (quota, LANES), 0)
    for half_id, rows_ref in enumerate((rows0_ref, rows1_ref)):
        block = block_of(half_id, lax.axis_index("zl"))
        for c in range(members // group):
            expanded = jnp.concatenate(
                [query_ref[half_id, c * group + k] for k in range(group)], axis=0
            )
            scores = dot_t(expanded, key_ref[block])
            weights = jnp.exp2(scores * (sharpness * math.log2(math.e))).astype(BF)
            every = dot(weights, value_ref[block])
            pieces = pieces_of(c * group, group, half_id, along_y)
            attended = []
            for k in range(group):
                bounds = row_bounds(pieces[k], counts_ref, along_y * TLY)
                part = every[k * quota : (k + 1) * quota]
                picked = part[:, :LANES]
                for t, bound in enumerate(bounds):
                    tile = part[:, (t + 1) * LANES : (t + 2) * LANES]
                    picked = jnp.where(row >= bound, tile, picked)
                attended.append(quotient(picked, part[:, 4 * LANES :]).astype(BF))
            x = jnp.concatenate([rows_ref[c * group + k] for k in range(group)], axis=0)
            added = dot(jnp.concatenate(attended, axis=0), proj_ref[3])
            result = (x.astype(F32) + added).astype(BF)
            for k in range(group):
                out_ref[c * group + k, half_id] = result[k * quota : (k + 1) * quota]


def scatter_kernel(rows_ref, index_ref, out_ref, wide_ref, part_ref):
    chunk = part_ref.shape[0]
    members, halves, quota, width = rows_ref.shape
    group = chunk // (halves * quota)

    def step(c, carry):
        for k in range(group):
            for half_id in range(halves):
                row = (k * halves + block_of(half_id, k % 2)) * quota
                part_ref[row : row + quota, :] = rows_ref[c * group + k, half_id].astype(F32)
        for r in range(chunk):
            i = index_ref[c * (chunk // LANES) + r // LANES, r % LANES]
            wide_ref[pl.ds(i, 1), :] = part_ref[pl.ds(r, 1), :]
        return carry

    lax.fori_loop(0, members // group, step, 0)
    out_ref[...] = wide_ref[...].astype(BF)


def call(kernel, name, out_shape, in_specs, scratch, micros, operands, megabytes=20, **more):
    spaces = {"v": pltpu.VMEM, "s": pltpu.SMEM, "a": pl.ANY}
    many = isinstance(out_shape, tuple)
    whole = pl.BlockSpec(memory_space=pltpu.VMEM)
    return pl.pallas_call(
        kernel,
        out_shape=out_shape,
        in_specs=[pl.BlockSpec(memory_space=spaces[c]) for c in in_specs],
        out_specs=(whole,) * len(out_shape) if many else whole,
        scratch_shapes=scratch,
        compiler_params=pltpu.CompilerParams(vmem_limit_bytes=megabytes * 1024 * 1024),
        cost_estimate=pl.CostEstimate(
            flops=int(micros * 5e8), bytes_accessed=int(micros * 1e6), transcendentals=0
        ),
        name=name,
        **more,
    )(*operands)


def body(
    points,
    embed_weight,
    inner_weights,
    output_weight,
    counts,
    point_order,
    inducing,
    first_proj,
    second_proj,
    mixing,
):
    along_x = lax.axis_size("tx")
    highs = lax.axis_size("zh")
    lows = lax.axis_size("zl")
    along_y = highs * lows
    point_count, width = points.shape
    quota = point_count // (along_x * along_y)
    grid_y = along_y * TLY
    blocks = 2
    members = along_x * lows
    tall = blocks * TLY
    lines = point_count // LANES
    chunk = 1024
    half_rows = (members, quota, width)

    def shape(sizes, dtype=BF):
        return jax.ShapeDtypeStruct(sizes, dtype)

    weights = (embed_weight, inner_weights, output_weight)
    buffers = [
        VMEM((point_count, width), F32),
        VMEM((chunk, width), F32),
        VMEM((chunk, width), F32),
    ]
    first, index = call(
        functools.partial(encode_first_kernel, grid_y, along_y, quota),
        "encode_first",
        (shape(half_rows), shape((lines, LANES), jnp.int32)),
        "aaaaaa",
        [
            SMEM((counts.shape[1],), jnp.int32),
            SMEM((counts.shape[1],), jnp.int32),
            SMEM((lines, LANES), jnp.int32),
        ]
        + buffers
        + [VMEM(a.shape, BF) for a in (points, *weights)]
        + [VMEM((lines, LANES), jnp.int32), pltpu.SemaphoreType.DMA((7,))],
        8,
        (points, *weights, counts, point_order.reshape(lines, LANES)),
        megabytes=56,
    )
    second = call(
        functools.partial(encode_second_kernel, quota),
        "encode_second",
        shape(half_rows),
        "vvvva",
        [SMEM((lines, LANES), jnp.int32)] + buffers + [pltpu.SemaphoreType.DMA],
        6,
        (points, *weights, index),
    )

    def exchange(rows):
        return lax.all_to_all(rows, ("tx", "zl"), split_axis=0, concat_axis=0, tiled=True)

    rows0 = exchange(first)
    rows1 = exchange(second)

    part_rows = 4 * LANES + 16
    parts = (shape((part_rows, LANES), F32), shape((part_rows, LANES)))
    sums = [VMEM((part_rows, HEADS * LANES), F32)]
    own0, send0, first_queries, value_weight = call(
        functools.partial(partial_kernel, 0, along_y),
        "partial_first",
        parts
        + (shape((HEADS * LANES, width)), shape((LANES, width))),
        "vsvv",
        sums,
        3,
        (rows0, counts, inducing, first_proj),
    )
    pairs = [(h, l) for h in range(highs) for l in range(lows)]

    def swap(value, flip_high, flip_low):
        steps = []
        for h, l in pairs:
            other_h = highs - 1 - h if flip_high else h
            other_l = lows - 1 - l if flip_low else l
            steps.append((h * lows + l, other_h * lows + other_l))
        return lax.ppermute(value, ("zh", "zl"), steps)

    other0 = swap(send0, True, False)
    own1, send1 = call(
        functools.partial(partial_kernel, 1, along_y),
        "partial_second",
        parts,
        "vsvvv",
        sums,
        3,
        (rows1, counts, first_queries, value_weight, first_proj),
    )
    other1 = swap(send1, True, False)
    first_half, border = call(
        combine_first_kernel,
        "combine_first",
        (shape((TLX, TLY, LANES, width)), shape((TLX, LANES, width))),
        "vvvva",
        [],
        0.01,
        (own0, other0, inducing, first_proj, send1),
    )
    column = swap(border, False, True)
    queries = call(
        functools.partial(queries_kernel, along_y),
        "point_queries",
        shape((2, members, quota, 4 * width)),
        "vvsva",
        [],
        0.01,
        (rows0, rows1, counts, second_proj, border),
    )
    near_pairs = [(i, i ^ 1) for i in range(along_x)]
    far_pairs = [(i, ((i + 1) ^ 1) - 1) for i in range(1, along_x - 1)]

    def halo(near, far):
        far = lax.ppermute(far, "tx", far_pairs)
        return lax.ppermute(near, "tx", near_pairs), far

    early = shape((TLY + 1, LANES, width))
    near0, far0 = halo(
        *call(
            early_lines_kernel,
            "early_lines",
            (early,) * 2,
            "vva",
            [],
            0.01,
            (first_half, column, queries),
        )
    )
    late = shape((TLY, LANES, width))
    second_half, near1, far1 = call(
        combine_second_kernel,
        "combine_second",
        (shape((TLX, TLY, LANES, width)), late, late),
        "vvvva",
        [],
        0.01,
        (own1, other1, inducing, first_proj, queries),
    )
    near1, far1 = halo(near1, far1)

    keys, values = call(
        mixture_kernel,
        "mix_tiles",
        (shape((blocks, HEADS * LANES, 4 * LANES)), shape((blocks, HEADS * LANES, 5 * LANES))),
        "v" * 9,
        [
            VMEM((TLX + 2, tall + 2, LANES, width), BF),
            VMEM((6 * LANES, 2 * LANES), BF),
            VMEM((2, 4 * LANES, 2 * LANES), BF),
        ],
        1,
        (first_half, column, second_half, near0, far0, near1, far1, second_proj, mixing),
    )

    result = call(
        functools.partial(attend_kernel, along_y),
        "attend_points",
        shape((members, 2, quota, width)),
        "vvvsvvv",
        [],
        7,
        (rows0, rows1, queries, counts, keys, values, second_proj),
    )
    return call(
        scatter_kernel,
        "scatter_rows",
        shape((point_count, width)),
        "vs",
        [VMEM((point_count, width), F32), VMEM((512, width), F32)],
        5,
        (exchange(result), index),
    )


def solution(mesh):
    along_x, along_y = mesh.devices.shape
    split = jax.sharding.Mesh(mesh.devices.reshape(along_x, 2, along_y // 2), ("tx", "zh", "zl"))
    rows = P(("tx", "zh", "zl"), None)
    placed = (rows, P(), P(), P(), P(), rows, P(), P(), P(), P())
    return jax.shard_map(body, mesh=split, in_specs=placed, out_specs=rows, check_vma=False)
```

```python
import functools
import math

import jax
import jax.numpy as jnp
from jax import lax
from jax.experimental import pallas as pl
from jax.experimental.pallas import tpu as pltpu
from jax.sharding import PartitionSpec as P

HEADS = 2
TLX = 2
TLY = 2
LANES = 128
GROUP_ROWS = 2048
BF = jnp.bfloat16
F32 = jnp.float32

sharpness = 32.0
epsilon = 1e-06
neighbour_steps = ((-1, -1), (-1, 0), (-1, 1), (0, -1), (0, 1), (1, -1), (1, 0), (1, 1))
VMEM = pltpu.VMEM
SMEM = pltpu.SMEM


def dot(a, b):
    return jnp.dot(a, b, preferred_element_type=F32)


def dot_t(a, b):
    return lax.dot_general(a, b, (((1,), (1,)), ((), ())), preferred_element_type=F32)


def head_ones():
    row = lax.broadcasted_iota(jnp.int32, (LANES, LANES), 0)
    col = lax.broadcasted_iota(jnp.int32, (LANES, LANES), 1)
    half = LANES // HEADS
    return jnp.where((row // half) == (col // half), 1.0, 0.0).astype(BF)


def doubled(w):
    blank = jnp.zeros_like(w)
    return jnp.concatenate(
        [jnp.concatenate([w, blank], axis=1), jnp.concatenate([blank, w], axis=1)], axis=0
    )


def beside(x):
    half = x.shape[0] // 2
    return jnp.concatenate([x[:half], x[half:]], axis=1)


def stacked_back(x):
    return jnp.concatenate([x[:, :LANES], x[:, LANES:]], axis=0)


def unit(v, ones):
    return v * lax.rsqrt(dot((v * v).astype(BF), ones) + epsilon)


def unit_pair(x, w, ones):
    return stacked_back(unit(dot(beside(x), doubled(w)), doubled(ones)))


def silu(v):
    half = 0.5 * v
    return (half + half * jnp.tanh(half)).astype(BF)


def quotient(a, b):
    guess = pl.reciprocal(b, approx=True)
    return a * (guess * (2.0 - b * guess))


def place():
    return lax.axis_index("tx"), lax.axis_index("zh"), lax.axis_index("zl")


def block_of(half_id, low):
    return low if half_id else 1 - low


def encode_rows(
    quota, points, index_ready, weights_ready, w1_ref, w2_ref, w3_ref, index_s, feat_ref, wide_ref, xs
):
    rows_total = points.shape[0]
    wide_ref[...] = points[...].astype(F32)
    index_ready()
    longest = xs[0].shape[0]
    sizes = [longest // 4, 3 * longest // 4] + [longest] * (rows_total // longest - 1)
    starts = [sum(sizes[:k]) for k in range(len(sizes))]

    def gather(c, first, last):
        for r in range(first, last):
            row = starts[c] + r
            member, rest = row // (2 * quota), row % (2 * quota)
            half_id, spot = rest // quota, rest % quota
            spot += (member * 2 + block_of(half_id, member % 2)) * quota
            i = index_s[spot // LANES, spot % LANES]
            xs[c % 2][pl.ds(r, 1), :] = wide_ref[pl.ds(i, 1), :]

    def layer(x, w, ahead, cuts):
        parts = []
        step = w.shape[1] // 2
        for k in range(2):
            ahead(cuts[k], cuts[k + 1])
            parts.append(silu(dot(x, w[:, k * step : (k + 1) * step])))
        return jnp.concatenate(parts, axis=1)

    gather(0, 0, sizes[0])
    weights_ready()
    for c, size in enumerate(sizes):
        coming = sizes[c + 1] if c + 1 < len(sizes) else 0

        def ahead(a, b):
            gather(c + 1, a, b)

        cuts = [coming * k // 5 for k in range(6)]
        hidden = layer(xs[c % 2][:size].astype(BF), w1_ref, ahead, cuts[:3])
        hidden = layer(hidden, w2_ref.at[0], ahead, cuts[2:5])
        ahead(cuts[4], cuts[5])
        out = dot(hidden, w3_ref[...]).astype(BF)
        for k in range(size // quota):
            row = starts[c] + k * quota
            feat_ref[row // (2 * quota), (row // quota) % 2] = out[k * quota : (k + 1) * quota]


def encode_kernel(
    grid_y,
    along_y,
    quota,
    points_hbm,
    w1_hbm,
    w2_hbm,
    w3_hbm,
    counts_hbm,
    order_hbm,
    feat_ref,
    index_ref,
    counts_s,
    off_ref,
    index_s,
    wide_ref,
    xa_ref,
    xb_ref,
    points_ref,
    w1_ref,
    w2_ref,
    w3_ref,
    order_ref,
    sems,
):
    tx, zh, zl = place()
    own = tx * along_y + zh * (along_y // 2) + zl
    sources = (counts_hbm.at[own], order_hbm, points_hbm, w1_hbm, w2_hbm, w3_hbm)
    targets = (counts_s, order_ref, points_ref, w1_ref, w2_ref, w3_ref)
    copies = [
        pltpu.make_async_copy(a, b, sems.at[k]) for k, (a, b) in enumerate(zip(sources, targets))
    ]
    for copy in copies:
        copy.start()
    tiles = counts_s.shape[0]
    order_rows = order_ref.shape[0]
    rows_total = points_ref.shape[0]
    copies[0].wait()

    def add_up(g, total):
        off_ref[g] = total
        return total + counts_s[g]

    lax.fori_loop(0, tiles, add_up, jnp.int32(0), unroll=8)
    copies[1].wait()
    lane = lax.broadcasted_iota(jnp.int32, (1, LANES), 1)

    def run_of(start):
        line = start >> 7
        shift = start & (LANES - 1)
        first = order_ref[pl.ds(jnp.clip(line, 0, order_rows - 1), 1), :]
        second = order_ref[pl.ds(jnp.clip(line + 1, 0, order_rows - 1), 1), :]
        merged = jnp.where(lane < shift, second, first)
        return pltpu.roll(merged, (LANES - shift) & (LANES - 1), 1)

    per_line = LANES // quota

    def index_line(line, carry):
        value = jnp.zeros((1, LANES), jnp.int32)
        for k in range(per_line):
            d = line * per_line + k
            g1 = (d // along_y) * (TLX * grid_y) + (d % along_y) * TLY
            n1 = counts_s[g1] + counts_s[g1 + 1]
            run1 = run_of(off_ref[g1] - k * quota)
            run2 = run_of(off_ref[g1 + grid_y] - n1 - k * quota)
            both = jnp.where(lane < k * quota + n1, run1, run2)
            value = both if k == 0 else jnp.where(lane >= k * quota, both, value)
        index_ref[pl.ds(line, 1), :] = value
        return carry

    lax.fori_loop(0, rows_total // LANES, index_line, 0, unroll=8)
    copy = pltpu.make_async_copy(index_ref, index_s, sems.at[6])
    copy.start()
    copies[2].wait()

    def weights_ready():
        for k in (3, 4, 5):
            copies[k].wait()

    encode_rows(
        quota, points_ref, copy.wait, weights_ready, w1_ref, w2_ref, w3_ref, index_s, feat_ref,
        wide_ref, (xa_ref, xb_ref),
    )


def tile_of(position, counts_ref, pieces, piece_id, grid_y):
    bounds = [None, None, None]
    for k, (s, base) in enumerate(pieces):
        n0 = counts_ref[s, base]
        n1 = counts_ref[s, base + 1]
        n2 = counts_ref[s, base + grid_y]
        for i, found in enumerate((n0, n0 + n1, n0 + n1 + n2)):
            if k == 0:
                bounds[i] = jnp.full(position.shape, found, jnp.int32)
            else:
                bounds[i] = jnp.where(piece_id >= k, found, bounds[i])
    return sum((position >= b).astype(jnp.int32) for b in bounds)


def pieces_of(first, group, half_id, along_y):
    tx, zh, zl = place()
    lows = along_y // 2
    block = zl * 2 + block_of(half_id, zl)
    base = tx * (TLX * along_y * TLY) + block * TLY
    found = []
    for k in range(group):
        member = first + k
        found.append(((member // lows) * along_y + zh * lows + member % lows, base))
    return found


def partial_kernel(half_id, along_y, rows_ref, counts_ref, *rest):
    num_ref = rest[-1]
    if half_id:
        query_ref, wv_ref, proj_ref, own_ref, send_ref = rest[:-1]
    else:
        inducing_ref, proj_ref, own_ref, send_ref, query_ref, wv_ref = rest[:-1]
    members, halves, quota, width = rows_ref.shape
    grid_y = along_y * TLY
    half = LANES // HEADS
    group = min(GROUP_ROWS // quota, members)
    chunk = group * quota
    ones = head_ones()
    lane = lax.broadcasted_iota(jnp.int32, (1, LANES), 1)
    left = lane < half
    if half_id:
        queries = query_ref[...]
        wv_t = wv_ref[...]
    else:
        queries = unit(dot(inducing_ref[...], proj_ref[0]), ones)
        queries = jnp.concatenate(
            [jnp.where(left, queries, 0.0), jnp.where(left, 0.0, queries)], axis=0
        ).astype(BF)
        wv_t = proj_ref[2].astype(F32).T.astype(BF)
        query_ref[...] = queries
        wv_ref[...] = wv_t
    spot = lax.broadcasted_iota(jnp.int32, (16, chunk), 1)
    tile_row = lax.broadcasted_iota(jnp.int32, (16, chunk), 0)
    for c in range(members // group):
        x = jnp.concatenate([rows_ref[c * group + k, half_id] for k in range(group)], axis=0)
        keys = unit_pair(x, proj_ref[1], ones).astype(BF)
        weights = jnp.exp2(dot_t(keys, queries) * (sharpness * math.log2(math.e))).astype(BF)
        values = dot_t(wv_t, x).astype(BF)
        pieces = pieces_of(c * group, group, half_id, along_y)
        tile = tile_of(spot % quota, counts_ref, pieces, spot // quota, grid_y)
        stacked = []
        for t in range(4):
            mask = jnp.where(tile == t, 1.0, 0.0).astype(BF)
            stacked += [values[k : k + 16] * mask for k in range(0, LANES, 16)]
        stacked.append(jnp.where(tile_row == tile, 1.0, 0.0).astype(BF))
        sums = dot(jnp.concatenate(stacked, axis=0), weights)
        if c == 0:
            num_ref[...] = sums
        else:
            num_ref[...] += sums
    last = 4 * LANES
    for t in range(4):
        rows = slice(t * LANES, (t + 1) * LANES)
        value = jnp.concatenate(
            [
                num_ref[t * LANES : t * LANES + half, :LANES],
                num_ref[t * LANES + half : (t + 1) * LANES, LANES:],
            ],
            axis=0,
        )
        own_ref[rows, :] = value
        send_ref[rows, :] = value.astype(BF)
    totals = jnp.concatenate(
        [num_ref[last : last + 4, h * LANES : (h + 1) * LANES] for h in range(HEADS)]
        + [jnp.zeros((8, LANES), F32)],
        axis=0,
    )
    own_ref[last:, :] = totals
    send_ref[last:, :] = totals.astype(BF)

def row_bounds(piece, counts_ref, grid_y):
    s, base = piece
    n0 = counts_ref[s, base]
    n1 = n0 + counts_ref[s, base + 1]
    return n0, n1, n1 + counts_ref[s, base + grid_y]


def queries_kernel(along_y, rows_ref, counts_ref, proj_ref, border_any, out_ref):
    ones = head_ones()
    members, halves, quota, width = rows_ref.shape
    group = min(GROUP_ROWS // quota, members)
    row = lax.broadcasted_iota(jnp.int32, (quota, LANES), 0)
    for half_id in range(halves):
        for c in range(members // group):
            x = jnp.concatenate([rows_ref[c * group + k, half_id] for k in range(group)], axis=0)
            query = unit_pair(x, proj_ref[0], ones)
            pieces = pieces_of(c * group, group, half_id, along_y)
            for k in range(group):
                bounds = row_bounds(pieces[k], counts_ref, along_y * TLY)
                past = [row >= b for b in bounds]
                mine = query[k * quota : (k + 1) * quota]
                masks = (~past[0], past[0] & ~past[1], past[1] & ~past[2], past[2])
                out_ref[half_id, c * group + k] = jnp.concatenate(
                    [jnp.where(m, mine, 0.0).astype(BF) for m in masks], axis=1
                )


def summarize(half_id, own_ref, other_ref, inducing_ref, proj_ref, store):
    half = LANES // HEADS
    last = 4 * LANES
    totals = own_ref[last:, :] + other_ref[last:, :].astype(F32)
    for t in range(4):
        rows = slice(t * LANES, (t + 1) * LANES)
        value = own_ref[rows, :] + other_ref[rows, :].astype(F32)
        attended = jnp.concatenate(
            [value[:half] / totals[t : t + 1], value[half:] / totals[t + 4 : t + 5]], axis=0
        )
        out = inducing_ref[...].astype(F32) + dot(attended.T.astype(BF), proj_ref[3])
        store(t // TLY, t % TLY, out.astype(BF))


def combine_first_kernel(
    own_ref, other_ref, inducing_ref, proj_ref, after_any, out_ref, column_ref
):
    def store(x, y, value):
        out_ref[x, y] = value

    summarize(0, own_ref, other_ref, inducing_ref, proj_ref, store)
    for x in range(TLX):
        column_ref[x] = jnp.where(lax.axis_index("zl") == 0, out_ref[x, TLY - 1], out_ref[x, 0])


def pair_lines(rows, near_ref, far_ref):
    even = lax.axis_index("tx") % 2 == 0
    for y, (low, high) in enumerate(zip(*rows)):
        near_ref[y] = jnp.where(even, high, low)
        far_ref[y] = jnp.where(even, low, high)


def early_lines_kernel(first_ref, column_ref, query_any, near_ref, far_ref):
    rows = [[first_ref[x, y] for y in range(TLY)] + [column_ref[x]] for x in range(TLX)]
    pair_lines(rows, near_ref, far_ref)


def combine_second_kernel(
    own_ref, other_ref, inducing_ref, proj_ref, query_any, out_ref, near_ref, far_ref
):
    def store(x, y, value):
        out_ref[x, y] = value

    summarize(1, own_ref, other_ref, inducing_ref, proj_ref, store)
    pair_lines([[out_ref[x, y] for y in range(TLY)] for x in range(TLX)], near_ref, far_ref)


def mixture_kernel(
    first_ref,
    column_ref,
    second_ref,
    near0_ref,
    far0_ref,
    near1_ref,
    far1_ref,
    proj_ref,
    mixing_ref,
    key_ref,
    value_ref,
    grid_ref,
    mid_ref,
    side_ref,
):
    half = LANES // HEADS
    blocks = key_ref.shape[0]
    tall = blocks * TLY
    low = lax.axis_index("zl")

    row = lax.broadcasted_iota(jnp.int32, (LANES, LANES), 0)
    col = lax.broadcasted_iota(jnp.int32, (LANES, LANES), 1)
    eye = jnp.where(row == col, 1.0, 0.0).astype(BF)
    blank = jnp.zeros((LANES, LANES), BF)

    def mix(a, b):
        return eye if (a, b) == (0, 0) else mixing_ref[neighbour_steps.index((a, b))]

    for k, a in enumerate((-1, 0, 1)):
        rows = slice(k * 2 * LANES, (k + 1) * 2 * LANES)
        mid_ref[rows, :] = jnp.concatenate(
            [
                jnp.concatenate([mix(a, 0), mix(a, -1)], axis=1),
                jnp.concatenate([mix(a, 1), mix(a, 0)], axis=1),
            ],
            axis=0,
        )
    for k, b in enumerate((-1, 1)):
        side_ref[k] = jnp.concatenate(
            [
                jnp.concatenate([mix(0, b), mix(-1, b)], axis=1),
                jnp.concatenate([mix(1, b), mix(0, b)], axis=1),
                jnp.concatenate([mix(-1, b), blank], axis=1),
                jnp.concatenate([blank, mix(1, b)], axis=1),
            ],
            axis=0,
        )
    ones = head_ones()
    lane = lax.broadcasted_iota(jnp.int32, (1, LANES), 1)
    left = lane < half
    even = lax.axis_index("tx") % 2
    near_row = (1 - even) * (TLX + 1)
    far_row = even * (TLX + 1)
    border = (1 - low) * (tall + 1)
    outside = low * (tall + 1)
    for x in range(TLX):
        for y in range(TLY):
            grid_ref[1 + x, 1 + block_of(0, low) * TLY + y] = first_ref[x, y]
            grid_ref[1 + x, 1 + block_of(1, low) * TLY + y] = second_ref[x, y]
        grid_ref[1 + x, border] = column_ref[x]
    for line, early_ref, late_ref in ((near_row, near0_ref, near1_ref), (far_row, far0_ref, far1_ref)):
        for y in range(TLY):
            grid_ref[line, 1 + block_of(0, low) * TLY + y] = early_ref[y]
            grid_ref[line, 1 + block_of(1, low) * TLY + y] = late_ref[y]
        grid_ref[line, border] = early_ref[TLY]
    for x in range(TLX + 2):
        grid_ref[x, outside] = blank

    def tile(i, j):
        return grid_ref[i, j + 1]

    mids, lefts, rights = [], [], []
    for i in range(2):
        for b in range(blocks):
            mids.append(
                jnp.concatenate(
                    [tile(i + r, 2 * b + s) for r in range(3) for s in range(2)], axis=1
                )
            )
    for b in range(blocks):
        lefts.append(jnp.concatenate([tile(i, 2 * b - 1) for i in (1, 2, 0, 3)], axis=1))
        rights.append(jnp.concatenate([tile(i, 2 * b + 2) for i in (1, 2, 0, 3)], axis=1))
    middle = dot(jnp.concatenate(mids, axis=0), mid_ref[...])
    from_left = dot(jnp.concatenate(lefts, axis=0), side_ref[0])
    from_right = dot(jnp.concatenate(rights, axis=0), side_ref[1])
    mixtures = []
    for b in range(blocks):
        span = slice(b * LANES, (b + 1) * LANES)
        for i in range(2):
            m = middle[(i * blocks + b) * LANES : (i * blocks + b + 1) * LANES]
            cols = slice(i * LANES, (i + 1) * LANES)
            mixtures.append((m[:, :LANES] + from_left[span, cols]).astype(BF))
            mixtures.append((m[:, LANES:] + from_right[span, cols]).astype(BF))
    mixtures = jnp.concatenate(mixtures, axis=0)
    keys = unit(dot(mixtures, proj_ref[1]), ones)
    values = dot(mixtures, proj_ref[2])
    for b in range(blocks):
        spans = [slice((b * 4 + t) * LANES, (b * 4 + t + 1) * LANES) for t in range(4)]
        for h in range(HEADS):
            mine = left if h == 0 else ~left
            key_ref[b, h * LANES : (h + 1) * LANES, :] = jnp.concatenate(
                [jnp.where(mine, keys[s], 0.0) for s in spans], axis=1
            ).astype(BF)
            flags = jnp.broadcast_to(jnp.where(mine, 1.0, 0.0), (LANES, LANES))
            value_ref[b, h * LANES : (h + 1) * LANES, :] = jnp.concatenate(
                [jnp.where(mine, values[s], 0.0) for s in spans] + [flags], axis=1
            ).astype(BF)


def attend_kernel(
    along_y, rows_ref, query_ref, counts_ref, key_ref, value_ref, proj_ref, out_ref
):
    members, halves, quota, width = rows_ref.shape
    group = min(GROUP_ROWS // quota, members)
    row = lax.broadcasted_iota(jnp.int32, (quota, LANES), 0)
    output_weight = doubled(proj_ref[3])
    for half_id in range(halves):
        block = block_of(half_id, lax.axis_index("zl"))
        for c in range(members // group):
            expanded = jnp.concatenate(
                [query_ref[half_id, c * group + k] for k in range(group)], axis=0
            )
            scores = dot_t(expanded, key_ref[block])
            weights = jnp.exp2(scores * (sharpness * math.log2(math.e))).astype(BF)
            every = dot(weights, value_ref[block])
            pieces = pieces_of(c * group, group, half_id, along_y)
            attended = []
            for k in range(group):
                bounds = row_bounds(pieces[k], counts_ref, along_y * TLY)
                part = every[k * quota : (k + 1) * quota]
                picked = part[:, :LANES]
                for t, bound in enumerate(bounds):
                    tile = part[:, (t + 1) * LANES : (t + 2) * LANES]
                    picked = jnp.where(row >= bound, tile, picked)
                attended.append(quotient(picked, part[:, 4 * LANES :]).astype(BF))
            x = jnp.concatenate([rows_ref[c * group + k, half_id] for k in range(group)], axis=0)
            added = stacked_back(dot(beside(jnp.concatenate(attended, axis=0)), output_weight))
            result = (x.astype(F32) + added).astype(BF)
            for k in range(group):
                out_ref[c * group + k, half_id] = result[k * quota : (k + 1) * quota]


def scatter_kernel(rows_ref, index_ref, out_ref, wide_ref, part_ref):
    chunk = part_ref.shape[0]
    members, halves, quota, width = rows_ref.shape
    group = chunk // (halves * quota)

    def step(c, carry):
        for k in range(group):
            for half_id in range(halves):
                row = (k * halves + block_of(half_id, k % 2)) * quota
                part_ref[row : row + quota, :] = rows_ref[c * group + k, half_id].astype(F32)
        for r in range(chunk):
            i = index_ref[c * (chunk // LANES) + r // LANES, r % LANES]
            wide_ref[pl.ds(i, 1), :] = part_ref[pl.ds(r, 1), :]
        return carry

    lax.fori_loop(0, members // group, step, 0)
    out_ref[...] = wide_ref[...].astype(BF)


def call(kernel, name, out_shape, in_specs, scratch, micros, operands, megabytes=20, **more):
    spaces = {"v": pltpu.VMEM, "s": pltpu.SMEM, "a": pl.ANY}
    many = isinstance(out_shape, tuple)
    whole = pl.BlockSpec(memory_space=pltpu.VMEM)
    return pl.pallas_call(
        kernel,
        out_shape=out_shape,
        in_specs=[pl.BlockSpec(memory_space=spaces[c]) for c in in_specs],
        out_specs=(whole,) * len(out_shape) if many else whole,
        scratch_shapes=scratch,
        compiler_params=pltpu.CompilerParams(vmem_limit_bytes=megabytes * 1024 * 1024),
        cost_estimate=pl.CostEstimate(
            flops=int(micros * 5e8), bytes_accessed=int(micros * 1e6), transcendentals=0
        ),
        name=name,
        **more,
    )(*operands)


def body(
    points,
    embed_weight,
    inner_weights,
    output_weight,
    counts,
    point_order,
    inducing,
    first_proj,
    second_proj,
    mixing,
):
    along_x = lax.axis_size("tx")
    highs = lax.axis_size("zh")
    lows = lax.axis_size("zl")
    along_y = highs * lows
    point_count, width = points.shape
    quota = point_count // (along_x * along_y)
    grid_y = along_y * TLY
    blocks = 2
    members = along_x * lows
    tall = blocks * TLY
    lines = point_count // LANES
    chunk = 1024

    def shape(sizes, dtype=BF):
        return jax.ShapeDtypeStruct(sizes, dtype)

    weights = (embed_weight, inner_weights, output_weight)
    buffers = [
        VMEM((point_count, width), F32),
        VMEM((chunk, width), F32),
        VMEM((chunk, width), F32),
    ]
    both_halves = (members, 2, quota, width)
    features, index = call(
        functools.partial(encode_kernel, grid_y, along_y, quota),
        "encode_points",
        (shape(both_halves), shape((lines, LANES), jnp.int32)),
        "aaaaaa",
        [
            SMEM((counts.shape[1],), jnp.int32),
            SMEM((counts.shape[1],), jnp.int32),
            SMEM((lines, LANES), jnp.int32),
        ]
        + buffers
        + [VMEM(a.shape, BF) for a in (points, *weights)]
        + [VMEM((lines, LANES), jnp.int32), pltpu.SemaphoreType.DMA((7,))],
        12,
        (points, *weights, counts, point_order.reshape(lines, LANES)),
        megabytes=56,
    )

    def exchange(rows):
        return lax.all_to_all(rows, ("tx", "zl"), split_axis=0, concat_axis=0, tiled=True)

    rows = exchange(features)

    part_rows = 4 * LANES + 16
    parts = (shape((part_rows, LANES), F32), shape((part_rows, LANES)))
    sums = [VMEM((part_rows, HEADS * LANES), F32)]
    own0, send0, first_queries, value_weight = call(
        functools.partial(partial_kernel, 0, along_y),
        "partial_first",
        parts
        + (shape((HEADS * LANES, width)), shape((LANES, width))),
        "vsvv",
        sums,
        3,
        (rows, counts, inducing, first_proj),
    )
    pairs = [(h, l) for h in range(highs) for l in range(lows)]

    def swap(value, flip_high, flip_low):
        steps = []
        for h, l in pairs:
            other_h = highs - 1 - h if flip_high else h
            other_l = lows - 1 - l if flip_low else l
            steps.append((h * lows + l, other_h * lows + other_l))
        return lax.ppermute(value, ("zh", "zl"), steps)

    other0 = swap(send0, True, False)
    own1, send1 = call(
        functools.partial(partial_kernel, 1, along_y),
        "partial_second",
        parts,
        "vsvvv",
        sums,
        3,
        (rows, counts, first_queries, value_weight, first_proj),
    )
    other1 = swap(send1, True, False)
    first_half, border = call(
        combine_first_kernel,
        "combine_first",
        (shape((TLX, TLY, LANES, width)), shape((TLX, LANES, width))),
        "vvvva",
        [],
        0.01,
        (own0, other0, inducing, first_proj, send1),
    )
    column = swap(border, False, True)
    queries = call(
        functools.partial(queries_kernel, along_y),
        "point_queries",
        shape((2, members, quota, 4 * width)),
        "vsva",
        [],
        0.01,
        (rows, counts, second_proj, border),
    )
    near_pairs = [(i, i ^ 1) for i in range(along_x)]
    far_pairs = [(i, ((i + 1) ^ 1) - 1) for i in range(1, along_x - 1)]

    def halo(near, far):
        far = lax.ppermute(far, "tx", far_pairs)
        return lax.ppermute(near, "tx", near_pairs), far

    early = shape((TLY + 1, LANES, width))
    near0, far0 = halo(
        *call(
            early_lines_kernel,
            "early_lines",
            (early,) * 2,
            "vva",
            [],
            0.01,
            (first_half, column, queries),
        )
    )
    late = shape((TLY, LANES, width))
    second_half, near1, far1 = call(
        combine_second_kernel,
        "combine_second",
        (shape((TLX, TLY, LANES, width)), late, late),
        "vvvva",
        [],
        0.01,
        (own1, other1, inducing, first_proj, queries),
    )
    near1, far1 = halo(near1, far1)

    keys, values = call(
        mixture_kernel,
        "mix_tiles",
        (shape((blocks, HEADS * LANES, 4 * LANES)), shape((blocks, HEADS * LANES, 5 * LANES))),
        "v" * 9,
        [
            VMEM((TLX + 2, tall + 2, LANES, width), BF),
            VMEM((6 * LANES, 2 * LANES), BF),
            VMEM((2, 4 * LANES, 2 * LANES), BF),
        ],
        1,
        (first_half, column, second_half, near0, far0, near1, far1, second_proj, mixing),
    )

    result = call(
        functools.partial(attend_kernel, along_y),
        "attend_points",
        shape(both_halves),
        "vvsvvv",
        [],
        7,
        (rows, queries, counts, keys, values, second_proj),
    )
    return call(
        scatter_kernel,
        "scatter_rows",
        shape((point_count, width)),
        "vs",
        [VMEM((point_count, width), F32), VMEM((512, width), F32)],
        5,
        (exchange(result), index),
    )


def solution(mesh):
    along_x, along_y = mesh.devices.shape
    split = jax.sharding.Mesh(mesh.devices.reshape(along_x, 2, along_y // 2), ("tx", "zh", "zl"))
    rows = P(("tx", "zh", "zl"), None)
    placed = (rows, P(), P(), P(), P(), rows, P(), P(), P(), P())
    return jax.shard_map(body, mesh=split, in_specs=placed, out_specs=rows, check_vma=False)
```

```python
import functools
import math

import jax
import jax.numpy as jnp
from jax import lax
from jax.experimental import pallas as pl
from jax.experimental.pallas import tpu as pltpu
from jax.sharding import PartitionSpec as P

HEADS = 2
TLX = 2
TLY = 2
LANES = 128
GROUP_ROWS = 2048
BF = jnp.bfloat16
F32 = jnp.float32

sharpness = 32.0
epsilon = 1e-06
neighbour_steps = ((-1, -1), (-1, 0), (-1, 1), (0, -1), (0, 1), (1, -1), (1, 0), (1, 1))
VMEM = pltpu.VMEM
SMEM = pltpu.SMEM


def dot(a, b):
    return jnp.dot(a, b, preferred_element_type=F32)


def dot_t(a, b):
    return lax.dot_general(a, b, (((1,), (1,)), ((), ())), preferred_element_type=F32)


def head_ones():
    row = lax.broadcasted_iota(jnp.int32, (LANES, LANES), 0)
    col = lax.broadcasted_iota(jnp.int32, (LANES, LANES), 1)
    half = LANES // HEADS
    return jnp.where((row // half) == (col // half), 1.0, 0.0).astype(BF)


def unit(v, ones):
    return v * lax.rsqrt(dot((v * v).astype(BF), ones) + epsilon)


def silu(v):
    half = 0.5 * v
    return (half + half * jnp.tanh(half)).astype(BF)


def quotient(a, b):
    guess = pl.reciprocal(b, approx=True)
    return a * (guess * (2.0 - b * guess))


def place():
    return lax.axis_index("tx"), lax.axis_index("zh"), lax.axis_index("zl")


def block_of(half_id, low):
    return low if half_id else 1 - low


def move_rows(pairs, source_ref, target_ref):
    for k in range(0, len(pairs), 16):
        batch = [(t, source_ref[pl.ds(f, 1), :]) for f, t in pairs[k : k + 16]]
        for target, row in batch:
            target_ref[pl.ds(target, 1), :] = row


def encode_rows(
    half_id, quota, points, index_ready, weights_ready, w1_ref, w2_ref, w3_ref, index_s, feat_ref,
    wide_ref, xs,
):
    rows_total = points.shape[0] // 2
    wide_ref[...] = points[...].astype(F32)
    index_ready()
    longest = xs[0].shape[0]
    sizes = [longest // 4, 3 * longest // 4] + [longest] * (rows_total // longest - 1)
    starts = [sum(sizes[:k]) for k in range(len(sizes))]

    def gather(c, first, last):
        pairs = []
        for r in range(first, last):
            member, rest = divmod(starts[c] + r, quota)
            spot = (member * 2 + block_of(half_id, member % 2)) * quota + rest
            pairs.append((index_s[spot // LANES, spot % LANES], r))
        move_rows(pairs, wide_ref, xs[c % 2])

    def layer(x, w, ahead, cuts):
        parts = []
        step = w.shape[1] // 2
        for k in range(2):
            ahead(cuts[k], cuts[k + 1])
            parts.append(silu(dot(x, w[:, k * step : (k + 1) * step])))
        return jnp.concatenate(parts, axis=1)

    gather(0, 0, sizes[0])
    weights_ready()
    for c, size in enumerate(sizes):
        coming = sizes[c + 1] if c + 1 < len(sizes) else 0

        def ahead(a, b):
            gather(c + 1, a, b)

        cuts = [coming * k // 80 * 16 for k in range(6)]
        cuts[5] = coming
        hidden = layer(xs[c % 2][:size].astype(BF), w1_ref, ahead, cuts[:3])
        hidden = layer(hidden, w2_ref.at[0], ahead, cuts[2:5])
        ahead(cuts[4], cuts[5])
        out = dot(hidden, w3_ref[...]).astype(BF)
        for k in range(size // quota):
            feat_ref[starts[c] // quota + k] = out[k * quota : (k + 1) * quota]


def encode_first_kernel(
    grid_y,
    along_y,
    quota,
    points_hbm,
    w1_hbm,
    w2_hbm,
    w3_hbm,
    counts_hbm,
    order_hbm,
    feat_ref,
    index_ref,
    counts_s,
    off_ref,
    index_s,
    wide_ref,
    xa_ref,
    xb_ref,
    points_ref,
    w1_ref,
    w2_ref,
    w3_ref,
    order_ref,
    sems,
):
    tx, zh, zl = place()
    own = tx * along_y + zh * (along_y // 2) + zl
    sources = (counts_hbm.at[own], order_hbm, points_hbm, w1_hbm, w2_hbm, w3_hbm)
    targets = (counts_s, order_ref, points_ref, w1_ref, w2_ref, w3_ref)
    copies = [
        pltpu.make_async_copy(a, b, sems.at[k]) for k, (a, b) in enumerate(zip(sources, targets))
    ]
    for copy in copies:
        copy.start()
    tiles = counts_s.shape[0]
    order_rows = order_ref.shape[0]
    rows_total = points_ref.shape[0]
    copies[0].wait()

    def add_up(g, total):
        off_ref[g] = total
        return total + counts_s[g]

    lax.fori_loop(0, tiles, add_up, jnp.int32(0), unroll=8)
    copies[1].wait()
    lane = lax.broadcasted_iota(jnp.int32, (1, LANES), 1)

    def run_of(start):
        line = start >> 7
        shift = start & (LANES - 1)
        first = order_ref[pl.ds(jnp.clip(line, 0, order_rows - 1), 1), :]
        second = order_ref[pl.ds(jnp.clip(line + 1, 0, order_rows - 1), 1), :]
        merged = jnp.where(lane < shift, second, first)
        return pltpu.roll(merged, (LANES - shift) & (LANES - 1), 1)

    per_line = LANES // quota

    def index_line(line, carry):
        value = jnp.zeros((1, LANES), jnp.int32)
        for k in range(per_line):
            d = line * per_line + k
            g1 = (d // along_y) * (TLX * grid_y) + (d % along_y) * TLY
            n1 = counts_s[g1] + counts_s[g1 + 1]
            run1 = run_of(off_ref[g1] - k * quota)
            run2 = run_of(off_ref[g1 + grid_y] - n1 - k * quota)
            both = jnp.where(lane < k * quota + n1, run1, run2)
            value = both if k == 0 else jnp.where(lane >= k * quota, both, value)
        index_ref[pl.ds(line, 1), :] = value
        return carry

    lax.fori_loop(0, rows_total // LANES, index_line, 0, unroll=8)
    copy = pltpu.make_async_copy(index_ref, index_s, sems.at[6])
    copy.start()
    copies[2].wait()

    def weights_ready():
        for k in (3, 4, 5):
            copies[k].wait()

    encode_rows(
        0, quota, points_ref, copy.wait, weights_ready, w1_ref, w2_ref, w3_ref, index_s,
        feat_ref, wide_ref, (xa_ref, xb_ref),
    )


def encode_second_kernel(
    quota, points_ref, w1_ref, w2_ref, w3_ref, index_any, feat_ref, index_s, wide_ref, xa_ref, xb_ref, sem
):
    copy = pltpu.make_async_copy(index_any, index_s, sem)
    copy.start()
    encode_rows(
        1, quota, points_ref, copy.wait, lambda: None, w1_ref, w2_ref, w3_ref, index_s,
        feat_ref, wide_ref, (xa_ref, xb_ref),
    )


def tile_of(position, counts_ref, pieces, piece_id, grid_y):
    bounds = [None, None, None]
    for k, (s, base) in enumerate(pieces):
        n0 = counts_ref[s, base]
        n1 = counts_ref[s, base + 1]
        n2 = counts_ref[s, base + grid_y]
        for i, found in enumerate((n0, n0 + n1, n0 + n1 + n2)):
            if k == 0:
                bounds[i] = jnp.full(position.shape, found, jnp.int32)
            else:
                bounds[i] = jnp.where(piece_id >= k, found, bounds[i])
    return sum((position >= b).astype(jnp.int32) for b in bounds)


def pieces_of(first, group, half_id, along_y):
    tx, zh, zl = place()
    lows = along_y // 2
    block = zl * 2 + block_of(half_id, zl)
    base = tx * (TLX * along_y * TLY) + block * TLY
    found = []
    for k in range(group):
        member = first + k
        found.append(((member // lows) * along_y + zh * lows + member % lows, base))
    return found


def partial_kernel(half_id, along_y, rows_ref, counts_ref, *rest):
    num_ref = rest[-1]
    if half_id:
        query_ref, wv_ref, proj_ref, own_ref, send_ref = rest[:-1]
    else:
        inducing_ref, proj_ref, own_ref, send_ref, query_ref, wv_ref = rest[:-1]
    members, quota, width = rows_ref.shape
    grid_y = along_y * TLY
    half = LANES // HEADS
    group = min(GROUP_ROWS // quota, members)
    chunk = group * quota
    ones = head_ones()
    lane = lax.broadcasted_iota(jnp.int32, (1, LANES), 1)
    left = lane < half
    if half_id:
        queries = query_ref[...]
        wv_t = wv_ref[...]
    else:
        queries = unit(dot(inducing_ref[...], proj_ref[0]), ones)
        queries = jnp.concatenate(
            [jnp.where(left, queries, 0.0), jnp.where(left, 0.0, queries)], axis=0
        ).astype(BF)
        wv_t = proj_ref[2].astype(F32).T.astype(BF)
        query_ref[...] = queries
        wv_ref[...] = wv_t
    spot = lax.broadcasted_iota(jnp.int32, (16, chunk), 1)
    tile_row = lax.broadcasted_iota(jnp.int32, (16, chunk), 0)
    for c in range(members // group):
        x = jnp.concatenate([rows_ref[c * group + k] for k in range(group)], axis=0)
        keys = unit(dot(x, proj_ref[1]), ones).astype(BF)
        weights = jnp.exp2(dot_t(keys, queries) * (sharpness * math.log2(math.e))).astype(BF)
        values = dot_t(wv_t, x).astype(BF)
        pieces = pieces_of(c * group, group, half_id, along_y)
        tile = tile_of(spot % quota, counts_ref, pieces, spot // quota, grid_y)
        stacked = []
        for t in range(4):
            mask = jnp.where(tile == t, 1.0, 0.0).astype(BF)
            stacked += [values[k : k + 16] * mask for k in range(0, LANES, 16)]
        stacked.append(jnp.where(tile_row == tile, 1.0, 0.0).astype(BF))
        sums = dot(jnp.concatenate(stacked, axis=0), weights)
        if c == 0:
            num_ref[...] = sums
        else:
            num_ref[...] += sums
    last = 4 * LANES
    for t in range(4):
        rows = slice(t * LANES, (t + 1) * LANES)
        value = jnp.concatenate(
            [
                num_ref[t * LANES : t * LANES + half, :LANES],
                num_ref[t * LANES + half : (t + 1) * LANES, LANES:],
            ],
            axis=0,
        )
        own_ref[rows, :] = value
        send_ref[rows, :] = value.astype(BF)
    totals = jnp.concatenate(
        [num_ref[last : last + 4, h * LANES : (h + 1) * LANES] for h in range(HEADS)]
        + [jnp.zeros((8, LANES), F32)],
        axis=0,
    )
    own_ref[last:, :] = totals
    send_ref[last:, :] = totals.astype(BF)

def row_bounds(piece, counts_ref, grid_y):
    s, base = piece
    n0 = counts_ref[s, base]
    n1 = n0 + counts_ref[s, base + 1]
    return n0, n1, n1 + counts_ref[s, base + grid_y]


def queries_kernel(along_y, rows0_ref, rows1_ref, counts_ref, proj_ref, column_any, out_ref):
    ones = head_ones()
    for half_id, rows_ref in enumerate((rows0_ref, rows1_ref)):
        members, quota, width = rows_ref.shape
        group = min(GROUP_ROWS // quota, members)
        row = lax.broadcasted_iota(jnp.int32, (quota, LANES), 0)
        for c in range(members // group):
            x = jnp.concatenate([rows_ref[c * group + k] for k in range(group)], axis=0)
            query = unit(dot(x, proj_ref[0]), ones)
            pieces = pieces_of(c * group, group, half_id, along_y)
            for k in range(group):
                bounds = row_bounds(pieces[k], counts_ref, along_y * TLY)
                past = [row >= b for b in bounds]
                mine = query[k * quota : (k + 1) * quota]
                masks = (~past[0], past[0] & ~past[1], past[1] & ~past[2], past[2])
                out_ref[half_id, c * group + k] = jnp.concatenate(
                    [jnp.where(m, mine, 0.0).astype(BF) for m in masks], axis=1
                )


def summarize(half_id, own_ref, other_ref, inducing_ref, proj_ref, store):
    half = LANES // HEADS
    last = 4 * LANES
    totals = own_ref[last:, :] + other_ref[last:, :].astype(F32)
    for t in range(4):
        rows = slice(t * LANES, (t + 1) * LANES)
        value = own_ref[rows, :] + other_ref[rows, :].astype(F32)
        attended = jnp.concatenate(
            [value[:half] / totals[t : t + 1], value[half:] / totals[t + 4 : t + 5]], axis=0
        )
        out = inducing_ref[...].astype(F32) + dot(attended.T.astype(BF), proj_ref[3])
        store(t // TLY, t % TLY, out.astype(BF))


def combine_first_kernel(
    own_ref, other_ref, inducing_ref, proj_ref, after_any, out_ref, column_ref
):
    def store(x, y, value):
        out_ref[x, y] = value

    summarize(0, own_ref, other_ref, inducing_ref, proj_ref, store)
    for x in range(TLX):
        column_ref[x] = jnp.where(lax.axis_index("zl") == 0, out_ref[x, TLY - 1], out_ref[x, 0])


def line_to(near, rows, out_ref):
    upper = lax.axis_index("tx") % 2 == (0 if near else 1)
    for y, (low, high) in enumerate(zip(*rows)):
        out_ref[y] = jnp.where(upper, high, low)


def early_line_kernel(first_ref, column_ref, query_any, far_ref):
    rows = [[first_ref[x, y] for y in range(TLY)] + [column_ref[x]] for x in range(TLX)]
    line_to(False, rows, far_ref)


def combine_second_kernel(
    own_ref, other_ref, inducing_ref, proj_ref, first_ref, column_ref, query_any, out_ref, near_ref, far_ref
):
    def store(x, y, value):
        out_ref[x, y] = value

    summarize(1, own_ref, other_ref, inducing_ref, proj_ref, store)
    rows = [[out_ref[x, y] for y in range(TLY)] for x in range(TLX)]
    line_to(False, rows, far_ref)
    for x in range(TLX):
        rows[x] += [first_ref[x, y] for y in range(TLY)] + [column_ref[x]]
    line_to(True, rows, near_ref)


def mixture_kernel(
    first_ref,
    column_ref,
    second_ref,
    near_ref,
    far0_ref,
    far1_ref,
    proj_ref,
    mixing_ref,
    key_ref,
    value_ref,
    grid_ref,
    mid_ref,
    side_ref,
):
    half = LANES // HEADS
    blocks = key_ref.shape[0]
    tall = blocks * TLY
    low = lax.axis_index("zl")

    row = lax.broadcasted_iota(jnp.int32, (LANES, LANES), 0)
    col = lax.broadcasted_iota(jnp.int32, (LANES, LANES), 1)
    eye = jnp.where(row == col, 1.0, 0.0).astype(BF)
    blank = jnp.zeros((LANES, LANES), BF)

    def mix(a, b):
        return eye if (a, b) == (0, 0) else mixing_ref[neighbour_steps.index((a, b))]

    for k, a in enumerate((-1, 0, 1)):
        rows = slice(k * 2 * LANES, (k + 1) * 2 * LANES)
        mid_ref[rows, :] = jnp.concatenate(
            [
                jnp.concatenate([mix(a, 0), mix(a, -1)], axis=1),
                jnp.concatenate([mix(a, 1), mix(a, 0)], axis=1),
            ],
            axis=0,
        )
    for k, b in enumerate((-1, 1)):
        side_ref[k] = jnp.concatenate(
            [
                jnp.concatenate([mix(0, b), mix(-1, b)], axis=1),
                jnp.concatenate([mix(1, b), mix(0, b)], axis=1),
                jnp.concatenate([mix(-1, b), blank], axis=1),
                jnp.concatenate([blank, mix(1, b)], axis=1),
            ],
            axis=0,
        )
    ones = head_ones()
    lane = lax.broadcasted_iota(jnp.int32, (1, LANES), 1)
    left = lane < half
    even = lax.axis_index("tx") % 2
    near_row = (1 - even) * (TLX + 1)
    far_row = even * (TLX + 1)
    border = (1 - low) * (tall + 1)
    outside = low * (tall + 1)
    for x in range(TLX):
        for y in range(TLY):
            grid_ref[1 + x, 1 + block_of(0, low) * TLY + y] = first_ref[x, y]
            grid_ref[1 + x, 1 + block_of(1, low) * TLY + y] = second_ref[x, y]
        grid_ref[1 + x, border] = column_ref[x]
    for y in range(TLY):
        grid_ref[near_row, 1 + block_of(1, low) * TLY + y] = near_ref[y]
        grid_ref[near_row, 1 + block_of(0, low) * TLY + y] = near_ref[TLY + y]
        grid_ref[far_row, 1 + block_of(1, low) * TLY + y] = far1_ref[y]
        grid_ref[far_row, 1 + block_of(0, low) * TLY + y] = far0_ref[y]
    grid_ref[near_row, border] = near_ref[2 * TLY]
    grid_ref[far_row, border] = far0_ref[TLY]
    for x in range(TLX + 2):
        grid_ref[x, outside] = blank

    def tile(i, j):
        return grid_ref[i, j + 1]

    mids, lefts, rights = [], [], []
    for i in range(2):
        for b in range(blocks):
            mids.append(
                jnp.concatenate(
                    [tile(i + r, 2 * b + s) for r in range(3) for s in range(2)], axis=1
                )
            )
    for b in range(blocks):
        lefts.append(jnp.concatenate([tile(i, 2 * b - 1) for i in (1, 2, 0, 3)], axis=1))
        rights.append(jnp.concatenate([tile(i, 2 * b + 2) for i in (1, 2, 0, 3)], axis=1))
    middle = dot(jnp.concatenate(mids, axis=0), mid_ref[...])
    from_left = dot(jnp.concatenate(lefts, axis=0), side_ref[0])
    from_right = dot(jnp.concatenate(rights, axis=0), side_ref[1])
    mixtures = []
    for b in range(blocks):
        span = slice(b * LANES, (b + 1) * LANES)
        for i in range(2):
            m = middle[(i * blocks + b) * LANES : (i * blocks + b + 1) * LANES]
            cols = slice(i * LANES, (i + 1) * LANES)
            mixtures.append((m[:, :LANES] + from_left[span, cols]).astype(BF))
            mixtures.append((m[:, LANES:] + from_right[span, cols]).astype(BF))
    mixtures = jnp.concatenate(mixtures, axis=0)
    keys = unit(dot(mixtures, proj_ref[1]), ones)
    values = dot(mixtures, proj_ref[2])
    for b in range(blocks):
        spans = [slice((b * 4 + t) * LANES, (b * 4 + t + 1) * LANES) for t in range(4)]
        for h in range(HEADS):
            mine = left if h == 0 else ~left
            key_ref[b, h * LANES : (h + 1) * LANES, :] = jnp.concatenate(
                [jnp.where(mine, keys[s], 0.0) for s in spans], axis=1
            ).astype(BF)
            flags = jnp.broadcast_to(jnp.where(mine, 1.0, 0.0), (LANES, LANES))
            value_ref[b, h * LANES : (h + 1) * LANES, :] = jnp.concatenate(
                [jnp.where(mine, values[s], 0.0) for s in spans] + [flags], axis=1
            ).astype(BF)


def attend_kernel(
    along_y, rows0_ref, rows1_ref, query_ref, counts_ref, key_ref, value_ref, proj_ref, out_ref
):
    members, quota, width = rows0_ref.shape
    group = min(GROUP_ROWS // quota, members)
    row = lax.broadcasted_iota(jnp.int32, (quota, LANES), 0)
    for half_id, rows_ref in enumerate((rows0_ref, rows1_ref)):
        block = block_of(half_id, lax.axis_index("zl"))
        for c in range(members // group):
            expanded = jnp.concatenate(
                [query_ref[half_id, c * group + k] for k in range(group)], axis=0
            )
            scores = dot_t(expanded, key_ref[block])
            weights = jnp.exp2(scores * (sharpness * math.log2(math.e))).astype(BF)
            every = dot(weights, value_ref[block])
            pieces = pieces_of(c * group, group, half_id, along_y)
            attended = []
            for k in range(group):
                bounds = row_bounds(pieces[k], counts_ref, along_y * TLY)
                part = every[k * quota : (k + 1) * quota]
                picked = part[:, :LANES]
                for t, bound in enumerate(bounds):
                    tile = part[:, (t + 1) * LANES : (t + 2) * LANES]
                    picked = jnp.where(row >= bound, tile, picked)
                attended.append(quotient(picked, part[:, 4 * LANES :]).astype(BF))
            x = jnp.concatenate([rows_ref[c * group + k] for k in range(group)], axis=0)
            added = dot(jnp.concatenate(attended, axis=0), proj_ref[3])
            result = (x.astype(F32) + added).astype(BF)
            for k in range(group):
                out_ref[c * group + k, half_id] = result[k * quota : (k + 1) * quota]


def scatter_kernel(rows_ref, index_ref, out_ref, wide_ref, part_ref):
    chunk = part_ref.shape[0]
    members, halves, quota, width = rows_ref.shape
    group = chunk // (halves * quota)

    def step(c, carry):
        for k in range(group):
            for half_id in range(halves):
                row = (k * halves + block_of(half_id, k % 2)) * quota
                part_ref[row : row + quota, :] = rows_ref[c * group + k, half_id].astype(F32)
        pairs = []
        for r in range(chunk):
            pairs.append((r, index_ref[c * (chunk // LANES) + r // LANES, r % LANES]))
        move_rows(pairs, part_ref, wide_ref)
        return carry

    lax.fori_loop(0, members // group, step, 0)
    out_ref[...] = wide_ref[...].astype(BF)


def call(kernel, name, out_shape, in_specs, scratch, micros, operands, megabytes=20, **more):
    spaces = {"v": pltpu.VMEM, "s": pltpu.SMEM, "a": pl.ANY}
    many = isinstance(out_shape, tuple)
    whole = pl.BlockSpec(memory_space=pltpu.VMEM)
    return pl.pallas_call(
        kernel,
        out_shape=out_shape,
        in_specs=[pl.BlockSpec(memory_space=spaces[c]) for c in in_specs],
        out_specs=(whole,) * len(out_shape) if many else whole,
        scratch_shapes=scratch,
        compiler_params=pltpu.CompilerParams(vmem_limit_bytes=megabytes * 1024 * 1024),
        cost_estimate=pl.CostEstimate(
            flops=int(micros * 5e8), bytes_accessed=int(micros * 1e6), transcendentals=0
        ),
        name=name,
        **more,
    )(*operands)


def body(
    points,
    embed_weight,
    inner_weights,
    output_weight,
    counts,
    point_order,
    inducing,
    first_proj,
    second_proj,
    mixing,
):
    along_x = lax.axis_size("tx")
    highs = lax.axis_size("zh")
    lows = lax.axis_size("zl")
    along_y = highs * lows
    point_count, width = points.shape
    quota = point_count // (along_x * along_y)
    grid_y = along_y * TLY
    blocks = 2
    members = along_x * lows
    tall = blocks * TLY
    lines = point_count // LANES
    chunk = 1024
    half_rows = (members, quota, width)

    def shape(sizes, dtype=BF):
        return jax.ShapeDtypeStruct(sizes, dtype)

    weights = (embed_weight, inner_weights, output_weight)
    buffers = [
        VMEM((point_count, width), F32),
        VMEM((chunk, width), F32),
        VMEM((chunk, width), F32),
    ]
    first, index = call(
        functools.partial(encode_first_kernel, grid_y, along_y, quota),
        "encode_first",
        (shape(half_rows), shape((lines, LANES), jnp.int32)),
        "aaaaaa",
        [
            SMEM((counts.shape[1],), jnp.int32),
            SMEM((counts.shape[1],), jnp.int32),
            SMEM((lines, LANES), jnp.int32),
        ]
        + buffers
        + [VMEM(a.shape, BF) for a in (points, *weights)]
        + [VMEM((lines, LANES), jnp.int32), pltpu.SemaphoreType.DMA((7,))],
        8,
        (points, *weights, counts, point_order.reshape(lines, LANES)),
        megabytes=56,
    )
    second = call(
        functools.partial(encode_second_kernel, quota),
        "encode_second",
        shape(half_rows),
        "vvvva",
        [SMEM((lines, LANES), jnp.int32)] + buffers + [pltpu.SemaphoreType.DMA],
        6,
        (points, *weights, index),
    )

    def exchange(rows):
        return lax.all_to_all(rows, ("tx", "zl"), split_axis=0, concat_axis=0, tiled=True)

    rows0 = exchange(first)
    rows1 = exchange(second)

    part_rows = 4 * LANES + 16
    parts = (shape((part_rows, LANES), F32), shape((part_rows, LANES)))
    sums = [VMEM((part_rows, HEADS * LANES), F32)]
    own0, send0, first_queries, value_weight = call(
        functools.partial(partial_kernel, 0, along_y),
        "partial_first",
        parts
        + (shape((HEADS * LANES, width)), shape((LANES, width))),
        "vsvv",
        sums,
        3,
        (rows0, counts, inducing, first_proj),
    )
    pairs = [(h, l) for h in range(highs) for l in range(lows)]

    def swap(value, flip_high, flip_low):
        steps = []
        for h, l in pairs:
            other_h = highs - 1 - h if flip_high else h
            other_l = lows - 1 - l if flip_low else l
            steps.append((h * lows + l, other_h * lows + other_l))
        return lax.ppermute(value, ("zh", "zl"), steps)

    other0 = swap(send0, True, False)
    own1, send1 = call(
        functools.partial(partial_kernel, 1, along_y),
        "partial_second",
        parts,
        "vsvvv",
        sums,
        3,
        (rows1, counts, first_queries, value_weight, first_proj),
    )
    other1 = swap(send1, True, False)
    first_half, border = call(
        combine_first_kernel,
        "combine_first",
        (shape((TLX, TLY, LANES, width)), shape((TLX, LANES, width))),
        "vvvva",
        [],
        0.01,
        (own0, other0, inducing, first_proj, send1),
    )
    column = swap(border, False, True)
    queries = call(
        functools.partial(queries_kernel, along_y),
        "point_queries",
        shape((2, members, quota, 4 * width)),
        "vvsva",
        [],
        0.01,
        (rows0, rows1, counts, second_proj, border),
    )
    near_pairs = [(i, i ^ 1) for i in range(along_x)]
    far_pairs = [(i, ((i + 1) ^ 1) - 1) for i in range(1, along_x - 1)]

    def tiles(count):
        return shape((count, LANES, width))

    early = call(
        early_line_kernel,
        "early_line",
        tiles(TLY + 1),
        "vva",
        [],
        0.01,
        (first_half, column, queries),
    )
    far0 = lax.ppermute(early, "tx", far_pairs)
    second_half, near, far1 = call(
        combine_second_kernel,
        "combine_second",
        (shape((TLX, TLY, LANES, width)), tiles(2 * TLY + 1), tiles(TLY)),
        "vvvvvva",
        [],
        0.01,
        (own1, other1, inducing, first_proj, first_half, column, early),
    )
    near = lax.ppermute(near, "tx", near_pairs)
    far1 = lax.ppermute(far1, "tx", far_pairs)

    keys, values = call(
        mixture_kernel,
        "mix_tiles",
        (shape((blocks, HEADS * LANES, 4 * LANES)), shape((blocks, HEADS * LANES, 5 * LANES))),
        "v" * 8,
        [
            VMEM((TLX + 2, tall + 2, LANES, width), BF),
            VMEM((6 * LANES, 2 * LANES), BF),
            VMEM((2, 4 * LANES, 2 * LANES), BF),
        ],
        1,
        (first_half, column, second_half, near, far0, far1, second_proj, mixing),
    )

    result = call(
        functools.partial(attend_kernel, along_y),
        "attend_points",
        shape((members, 2, quota, width)),
        "vvvsvvv",
        [],
        7,
        (rows0, rows1, queries, counts, keys, values, second_proj),
    )
    return call(
        scatter_kernel,
        "scatter_rows",
        shape((point_count, width)),
        "vs",
        [VMEM((point_count, width), F32), VMEM((512, width), F32)],
        5,
        (exchange(result), index),
    )


def solution(mesh):
    along_x, along_y = mesh.devices.shape
    split = jax.sharding.Mesh(mesh.devices.reshape(along_x, 2, along_y // 2), ("tx", "zh", "zl"))
    rows = P(("tx", "zh", "zl"), None)
    placed = (rows, P(), P(), P(), P(), rows, P(), P(), P(), P())
    return jax.shard_map(body, mesh=split, in_specs=placed, out_specs=rows, check_vma=False)
```

```python
import functools
import math

import jax
import jax.numpy as jnp
from jax import lax
from jax.experimental import pallas as pl
from jax.experimental.pallas import tpu as pltpu
from jax.sharding import PartitionSpec as P

HEADS = 2
TLX = 2
TLY = 2
LANES = 128
GROUP_ROWS = 2048
BF = jnp.bfloat16
F32 = jnp.float32

sharpness = 32.0
epsilon = 1e-06
neighbour_steps = ((-1, -1), (-1, 0), (-1, 1), (0, -1), (0, 1), (1, -1), (1, 0), (1, 1))
VMEM = pltpu.VMEM
SMEM = pltpu.SMEM


def dot(a, b):
    return jnp.dot(a, b, preferred_element_type=F32)


def dot_t(a, b):
    return lax.dot_general(a, b, (((1,), (1,)), ((), ())), preferred_element_type=F32)


def head_ones():
    row = lax.broadcasted_iota(jnp.int32, (LANES, LANES), 0)
    col = lax.broadcasted_iota(jnp.int32, (LANES, LANES), 1)
    half = LANES // HEADS
    return jnp.where((row // half) == (col // half), 1.0, 0.0).astype(BF)


def unit(v, ones):
    return v * lax.rsqrt(dot((v * v).astype(BF), ones) + epsilon)


def silu(v):
    half = 0.5 * v
    return (half + half * jnp.tanh(half)).astype(BF)


def quotient(a, b):
    guess = pl.reciprocal(b, approx=True)
    return a * (guess * (2.0 - b * guess))


def place():
    return lax.axis_index("tx"), lax.axis_index("zh"), lax.axis_index("zl")


def block_of(half_id, low):
    return low if half_id else 1 - low


def encode_rows(half_id, quota, chunk, points, index_ready, weights_ready, w1_ref, w2_ref, w3_ref, index_s, feat_ref, wide_ref, xs):
    rows_total = points.shape[0] // 2
    group = chunk // quota
    wide_ref[...] = points[...].astype(F32)
    index_ready()

    def gather(c, buffer, first, last):
        for r in range(first, last):
            member = r // quota
            spot = (member * 2 + block_of(half_id, member % 2)) * quota + r % quota
            i = index_s[c * (2 * chunk // LANES) + spot // LANES, spot % LANES]
            buffer[pl.ds(r, 1), :] = wide_ref[pl.ds(i, 1), :]

    def layer(x, w, ahead, cuts):
        parts = []
        step = w.shape[1] // 2
        for k in range(2):
            ahead(cuts[k], cuts[k + 1])
            parts.append(silu(dot(x, w[:, k * step : (k + 1) * step])))
        return jnp.concatenate(parts, axis=1)

    def apply(c, buffer, ahead):
        cuts = [chunk * k // 5 for k in range(6)]
        hidden = layer(buffer[...].astype(BF), w1_ref, ahead, cuts[:3])
        hidden = layer(hidden, w2_ref.at[0], ahead, cuts[2:5])
        ahead(cuts[4], cuts[5])
        out = dot(hidden, w3_ref[...]).astype(BF)
        for k in range(group):
            feat_ref[c * group + k] = out[k * quota : (k + 1) * quota]

    chunks = rows_total // chunk
    gather(0, xs[0], 0, chunk)
    weights_ready()
    for c in range(chunks):

        def ahead(a, b):
            if c + 1 < chunks:
                gather(c + 1, xs[(c + 1) % 2], a, b)

        apply(c, xs[c % 2], ahead)


def encode_first_kernel(
    grid_y,
    along_y,
    quota,
    points_hbm,
    w1_hbm,
    w2_hbm,
    w3_hbm,
    counts_hbm,
    order_hbm,
    feat_ref,
    index_ref,
    counts_s,
    off_ref,
    index_s,
    wide_ref,
    xa_ref,
    xb_ref,
    points_ref,
    w1_ref,
    w2_ref,
    w3_ref,
    order_ref,
    sems,
):
    tx, zh, zl = place()
    own = tx * along_y + zh * (along_y // 2) + zl
    sources = (counts_hbm.at[own], order_hbm, points_hbm, w1_hbm, w2_hbm, w3_hbm)
    targets = (counts_s, order_ref, points_ref, w1_ref, w2_ref, w3_ref)
    copies = [
        pltpu.make_async_copy(a, b, sems.at[k]) for k, (a, b) in enumerate(zip(sources, targets))
    ]
    for copy in copies:
        copy.start()
    tiles = counts_s.shape[0]
    order_rows = order_ref.shape[0]
    rows_total = points_ref.shape[0]
    copies[0].wait()

    def add_up(g, total):
        off_ref[g] = total
        return total + counts_s[g]

    lax.fori_loop(0, tiles, add_up, jnp.int32(0), unroll=8)
    copies[1].wait()
    lane = lax.broadcasted_iota(jnp.int32, (1, LANES), 1)

    def run_of(start):
        line = start >> 7
        shift = start & (LANES - 1)
        first = order_ref[pl.ds(jnp.clip(line, 0, order_rows - 1), 1), :]
        second = order_ref[pl.ds(jnp.clip(line + 1, 0, order_rows - 1), 1), :]
        merged = jnp.where(lane < shift, second, first)
        return pltpu.roll(merged, (LANES - shift) & (LANES - 1), 1)

    per_line = LANES // quota

    def index_line(line, carry):
        value = jnp.zeros((1, LANES), jnp.int32)
        for k in range(per_line):
            d = line * per_line + k
            g1 = (d // along_y) * (TLX * grid_y) + (d % along_y) * TLY
            n1 = counts_s[g1] + counts_s[g1 + 1]
            run1 = run_of(off_ref[g1] - k * quota)
            run2 = run_of(off_ref[g1 + grid_y] - n1 - k * quota)
            both = jnp.where(lane < k * quota + n1, run1, run2)
            value = both if k == 0 else jnp.where(lane >= k * quota, both, value)
        index_ref[pl.ds(line, 1), :] = value
        return carry

    lax.fori_loop(0, rows_total // LANES, index_line, 0, unroll=8)
    copy = pltpu.make_async_copy(index_ref, index_s, sems.at[6])
    copy.start()
    copies[2].wait()

    def weights_ready():
        for k in (3, 4, 5):
            copies[k].wait()

    encode_rows(
        0, quota, xa_ref.shape[0], points_ref, copy.wait, weights_ready, w1_ref, w2_ref, w3_ref, index_s,
        feat_ref, wide_ref, (xa_ref, xb_ref),
    )


def encode_second_kernel(
    quota, points_ref, w1_ref, w2_ref, w3_ref, index_any, feat_ref, index_s, wide_ref, xa_ref, xb_ref, sem
):
    copy = pltpu.make_async_copy(index_any, index_s, sem)
    copy.start()
    encode_rows(
        1, quota, xa_ref.shape[0], points_ref, copy.wait, lambda: None, w1_ref, w2_ref, w3_ref, index_s,
        feat_ref, wide_ref, (xa_ref, xb_ref),
    )


def tile_of(position, counts_ref, pieces, piece_id, grid_y):
    bounds = [None, None, None]
    for k, (s, base) in enumerate(pieces):
        n0 = counts_ref[s, base]
        n1 = counts_ref[s, base + 1]
        n2 = counts_ref[s, base + grid_y]
        for i, found in enumerate((n0, n0 + n1, n0 + n1 + n2)):
            if k == 0:
                bounds[i] = jnp.full(position.shape, found, jnp.int32)
            else:
                bounds[i] = jnp.where(piece_id >= k, found, bounds[i])
    return sum((position >= b).astype(jnp.int32) for b in bounds)


def pieces_of(first, group, half_id, along_y):
    tx, zh, zl = place()
    lows = along_y // 2
    block = zl * 2 + block_of(half_id, zl)
    base = tx * (TLX * along_y * TLY) + block * TLY
    found = []
    for k in range(group):
        member = first + k
        found.append(((member // lows) * along_y + zh * lows + member % lows, base))
    return found


def partial_kernel(half_id, along_y, rows_ref, counts_ref, *rest):
    num_ref = rest[-1]
    if half_id:
        query_ref, wv_ref, proj_ref, before_any, own_ref, send_ref = rest[:-1]
    else:
        inducing_ref, proj_ref, own_ref, send_ref, query_ref, wv_ref = rest[:-1]
    members, quota, width = rows_ref.shape
    grid_y = along_y * TLY
    half = LANES // HEADS
    group = min(GROUP_ROWS // quota, members)
    chunk = group * quota
    ones = head_ones()
    lane = lax.broadcasted_iota(jnp.int32, (1, LANES), 1)
    left = lane < half
    if half_id:
        queries = query_ref[...]
        wv_t = wv_ref[...]
    else:
        queries = unit(dot(inducing_ref[...], proj_ref[0]), ones)
        queries = jnp.concatenate(
            [jnp.where(left, queries, 0.0), jnp.where(left, 0.0, queries)], axis=0
        ).astype(BF)
        wv_t = proj_ref[2].astype(F32).T.astype(BF)
        query_ref[...] = queries
        wv_ref[...] = wv_t
    spot = lax.broadcasted_iota(jnp.int32, (16, chunk), 1)
    tile_row = lax.broadcasted_iota(jnp.int32, (16, chunk), 0)
    for c in range(members // group):
        x = jnp.concatenate([rows_ref[c * group + k] for k in range(group)], axis=0)
        keys = unit(dot(x, proj_ref[1]), ones).astype(BF)
        weights = jnp.exp2(dot_t(keys, queries) * (sharpness * math.log2(math.e))).astype(BF)
        values = dot_t(wv_t, x).astype(BF)
        pieces = pieces_of(c * group, group, half_id, along_y)
        tile = tile_of(spot % quota, counts_ref, pieces, spot // quota, grid_y)
        stacked = []
        for t in range(4):
            mask = jnp.where(tile == t, 1.0, 0.0).astype(BF)
            stacked += [values[k : k + 16] * mask for k in range(0, LANES, 16)]
        stacked.append(jnp.where(tile_row == tile, 1.0, 0.0).astype(BF))
        sums = dot(jnp.concatenate(stacked, axis=0), weights)
        if c == 0:
            num_ref[...] = sums
        else:
            num_ref[...] += sums
    last = 4 * LANES
    for t in range(4):
        rows = slice(t * LANES, (t + 1) * LANES)
        value = jnp.concatenate(
            [
                num_ref[t * LANES : t * LANES + half, :LANES],
                num_ref[t * LANES + half : (t + 1) * LANES, LANES:],
            ],
            axis=0,
        )
        own_ref[rows, :] = value
        send_ref[rows, :] = value.astype(BF)
    totals = jnp.concatenate(
        [num_ref[last : last + 4, h * LANES : (h + 1) * LANES] for h in range(HEADS)]
        + [jnp.zeros((8, LANES), F32)],
        axis=0,
    )
    own_ref[last:, :] = totals
    send_ref[last:, :] = totals.astype(BF)

def row_bounds(piece, counts_ref, grid_y):
    s, base = piece
    n0 = counts_ref[s, base]
    n1 = n0 + counts_ref[s, base + 1]
    return n0, n1, n1 + counts_ref[s, base + grid_y]


def queries_kernel(half_id, along_y, rows_ref, counts_ref, proj_ref, *rest):
    out_ref = rest[-1]
    ones = head_ones()
    members, quota, width = rows_ref.shape
    group = min(GROUP_ROWS // quota, members)
    row = lax.broadcasted_iota(jnp.int32, (quota, LANES), 0)
    for c in range(members // group):
        x = jnp.concatenate([rows_ref[c * group + k] for k in range(group)], axis=0)
        query = unit(dot(x, proj_ref[0]), ones)
        pieces = pieces_of(c * group, group, half_id, along_y)
        for k in range(group):
            bounds = row_bounds(pieces[k], counts_ref, along_y * TLY)
            past = [row >= b for b in bounds]
            mine = query[k * quota : (k + 1) * quota]
            masks = (~past[0], past[0] & ~past[1], past[1] & ~past[2], past[2])
            out_ref[c * group + k] = jnp.concatenate(
                [jnp.where(m, mine, 0.0).astype(BF) for m in masks], axis=1
            )


def summarize(half_id, own_ref, other_ref, inducing_ref, proj_ref, store):
    half = LANES // HEADS
    last = 4 * LANES
    totals = own_ref[last:, :] + other_ref[last:, :].astype(F32)
    for t in range(4):
        rows = slice(t * LANES, (t + 1) * LANES)
        value = own_ref[rows, :] + other_ref[rows, :].astype(F32)
        attended = jnp.concatenate(
            [value[:half] / totals[t : t + 1], value[half:] / totals[t + 4 : t + 5]], axis=0
        )
        out = inducing_ref[...].astype(F32) + dot(attended.T.astype(BF), proj_ref[3])
        store(t // TLY, t % TLY, out.astype(BF))


def combine_first_kernel(
    own_ref, other_ref, inducing_ref, proj_ref, after_any, out_ref, column_ref
):
    def store(x, y, value):
        out_ref[x, y] = value

    summarize(0, own_ref, other_ref, inducing_ref, proj_ref, store)
    for x in range(TLX):
        column_ref[x] = jnp.where(lax.axis_index("zl") == 0, out_ref[x, TLY - 1], out_ref[x, 0])


def pair_lines(rows, near_ref, far_ref):
    even = lax.axis_index("tx") % 2 == 0
    for y, (low, high) in enumerate(zip(*rows)):
        near_ref[y] = jnp.where(even, high, low)
        far_ref[y] = jnp.where(even, low, high)


def early_lines_kernel(first_ref, column_ref, query_any, near_ref, far_ref):
    rows = [[first_ref[x, y] for y in range(TLY)] + [column_ref[x]] for x in range(TLX)]
    pair_lines(rows, near_ref, far_ref)


def combine_second_kernel(
    own_ref, other_ref, inducing_ref, proj_ref, query_any, out_ref, near_ref, far_ref
):
    def store(x, y, value):
        out_ref[x, y] = value

    summarize(1, own_ref, other_ref, inducing_ref, proj_ref, store)
    pair_lines([[out_ref[x, y] for y in range(TLY)] for x in range(TLX)], near_ref, far_ref)


def mixture_kernel(
    first_ref,
    column_ref,
    second_ref,
    near0_ref,
    far0_ref,
    near1_ref,
    far1_ref,
    proj_ref,
    mixing_ref,
    key_ref,
    value_ref,
    grid_ref,
    mid_ref,
    side_ref,
):
    half = LANES // HEADS
    blocks = key_ref.shape[0]
    tall = blocks * TLY
    low = lax.axis_index("zl")

    row = lax.broadcasted_iota(jnp.int32, (LANES, LANES), 0)
    col = lax.broadcasted_iota(jnp.int32, (LANES, LANES), 1)
    eye = jnp.where(row == col, 1.0, 0.0).astype(BF)
    blank = jnp.zeros((LANES, LANES), BF)

    def mix(a, b):
        return eye if (a, b) == (0, 0) else mixing_ref[neighbour_steps.index((a, b))]

    for k, a in enumerate((-1, 0, 1)):
        rows = slice(k * 2 * LANES, (k + 1) * 2 * LANES)
        mid_ref[rows, :] = jnp.concatenate(
            [
                jnp.concatenate([mix(a, 0), mix(a, -1)], axis=1),
                jnp.concatenate([mix(a, 1), mix(a, 0)], axis=1),
            ],
            axis=0,
        )
    for k, b in enumerate((-1, 1)):
        side_ref[k] = jnp.concatenate(
            [
                jnp.concatenate([mix(0, b), mix(-1, b)], axis=1),
                jnp.concatenate([mix(1, b), mix(0, b)], axis=1),
                jnp.concatenate([mix(-1, b), blank], axis=1),
                jnp.concatenate([blank, mix(1, b)], axis=1),
            ],
            axis=0,
        )
    ones = head_ones()
    lane = lax.broadcasted_iota(jnp.int32, (1, LANES), 1)
    left = lane < half
    even = lax.axis_index("tx") % 2
    near_row = (1 - even) * (TLX + 1)
    far_row = even * (TLX + 1)
    border = (1 - low) * (tall + 1)
    outside = low * (tall + 1)
    for x in range(TLX):
        for y in range(TLY):
            grid_ref[1 + x, 1 + block_of(0, low) * TLY + y] = first_ref[x, y]
            grid_ref[1 + x, 1 + block_of(1, low) * TLY + y] = second_ref[x, y]
        grid_ref[1 + x, border] = column_ref[x]
    for line, early_ref, late_ref in ((near_row, near0_ref, near1_ref), (far_row, far0_ref, far1_ref)):
        for y in range(TLY):
            grid_ref[line, 1 + block_of(0, low) * TLY + y] = early_ref[y]
            grid_ref[line, 1 + block_of(1, low) * TLY + y] = late_ref[y]
        grid_ref[line, border] = early_ref[TLY]
    for x in range(TLX + 2):
        grid_ref[x, outside] = blank

    def tile(i, j):
        return grid_ref[i, j + 1]

    mids, lefts, rights = [], [], []
    for i in range(2):
        for b in range(blocks):
            mids.append(
                jnp.concatenate(
                    [tile(i + r, 2 * b + s) for r in range(3) for s in range(2)], axis=1
                )
            )
    for b in range(blocks):
        lefts.append(jnp.concatenate([tile(i, 2 * b - 1) for i in (1, 2, 0, 3)], axis=1))
        rights.append(jnp.concatenate([tile(i, 2 * b + 2) for i in (1, 2, 0, 3)], axis=1))
    middle = dot(jnp.concatenate(mids, axis=0), mid_ref[...])
    from_left = dot(jnp.concatenate(lefts, axis=0), side_ref[0])
    from_right = dot(jnp.concatenate(rights, axis=0), side_ref[1])
    mixtures = []
    for b in range(blocks):
        span = slice(b * LANES, (b + 1) * LANES)
        for i in range(2):
            m = middle[(i * blocks + b) * LANES : (i * blocks + b + 1) * LANES]
            cols = slice(i * LANES, (i + 1) * LANES)
            mixtures.append((m[:, :LANES] + from_left[span, cols]).astype(BF))
            mixtures.append((m[:, LANES:] + from_right[span, cols]).astype(BF))
    mixtures = jnp.concatenate(mixtures, axis=0)
    keys = unit(dot(mixtures, proj_ref[1]), ones)
    values = dot(mixtures, proj_ref[2])
    for b in range(blocks):
        spans = [slice((b * 4 + t) * LANES, (b * 4 + t + 1) * LANES) for t in range(4)]
        for h in range(HEADS):
            mine = left if h == 0 else ~left
            key_ref[b, h * LANES : (h + 1) * LANES, :] = jnp.concatenate(
                [jnp.where(mine, keys[s], 0.0) for s in spans], axis=1
            ).astype(BF)
            value_ref[b, h * LANES : (h + 1) * LANES, :] = jnp.concatenate(
                [jnp.where(mine, values[s], 0.0) for s in spans], axis=1
            ).astype(BF)


def attend_kernel(
    along_y,
    rows0_ref,
    rows1_ref,
    query0_ref,
    query1_ref,
    counts_ref,
    key_ref,
    value_ref,
    proj_ref,
    out_ref,
):
    members, quota, width = rows0_ref.shape
    group = min(GROUP_ROWS // quota, members)
    row = lax.broadcasted_iota(jnp.int32, (quota, LANES), 0)
    left = lax.broadcasted_iota(jnp.int32, (1, LANES), 1) < LANES // HEADS
    for half_id, (rows_ref, query_ref) in enumerate(
        ((rows0_ref, query0_ref), (rows1_ref, query1_ref))
    ):
        block = block_of(half_id, lax.axis_index("zl"))
        for c in range(members // group):
            expanded = jnp.concatenate([query_ref[c * group + k] for k in range(group)], axis=0)
            scores = dot_t(expanded, key_ref[block])
            weights = jnp.exp2(scores * (sharpness * math.log2(math.e)))
            totals = [
                jnp.sum(weights[:, h * LANES : (h + 1) * LANES], axis=1, keepdims=True)
                for h in range(HEADS)
            ]
            every = dot(weights.astype(BF), value_ref[block])
            pieces = pieces_of(c * group, group, half_id, along_y)
            attended = []
            for k in range(group):
                bounds = row_bounds(pieces[k], counts_ref, along_y * TLY)
                span = slice(k * quota, (k + 1) * quota)
                part = every[span]
                picked = part[:, :LANES]
                for t, bound in enumerate(bounds):
                    tile = part[:, (t + 1) * LANES : (t + 2) * LANES]
                    picked = jnp.where(row >= bound, tile, picked)
                total = jnp.where(left, totals[0][span], totals[1][span])
                attended.append(quotient(picked, total).astype(BF))
            x = jnp.concatenate([rows_ref[c * group + k] for k in range(group)], axis=0)
            added = dot(jnp.concatenate(attended, axis=0), proj_ref[3])
            result = (x.astype(F32) + added).astype(BF)
            for k in range(group):
                out_ref[c * group + k, half_id] = result[k * quota : (k + 1) * quota]


def scatter_kernel(rows_ref, index_ref, out_hbm, wide_ref, part_ref, out_ref, sems):
    chunk = part_ref.shape[0]
    members, halves, quota, width = rows_ref.shape
    group = chunk // (halves * quota)

    def step(c, carry):
        for k in range(group):
            for half_id in range(halves):
                row = (k * halves + block_of(half_id, k % 2)) * quota
                part_ref[row : row + quota, :] = rows_ref[c * group + k, half_id].astype(F32)
        for r in range(chunk):
            i = index_ref[c * (chunk // LANES) + r // LANES, r % LANES]
            wide_ref[pl.ds(i, 1), :] = part_ref[pl.ds(r, 1), :]
        return carry

    lax.fori_loop(0, members // group, step, 0)
    count = sems.shape[0]
    size = wide_ref.shape[0] // count
    copies = []
    for k in range(count):
        span = pl.ds(k * size, size)
        out_ref[span, :] = wide_ref[span, :].astype(BF)
        copies.append(pltpu.make_async_copy(out_ref.at[span], out_hbm.at[span], sems.at[k]))
        copies[k].start()
    for copy in copies:
        copy.wait()


def call(kernel, name, out_shape, in_specs, scratch, micros, operands, megabytes=20, out_space=pltpu.VMEM):
    spaces = {"v": pltpu.VMEM, "s": pltpu.SMEM, "a": pl.ANY}
    many = isinstance(out_shape, tuple)
    whole = pl.BlockSpec(memory_space=out_space)
    return pl.pallas_call(
        kernel,
        out_shape=out_shape,
        in_specs=[pl.BlockSpec(memory_space=spaces[c]) for c in in_specs],
        out_specs=(whole,) * len(out_shape) if many else whole,
        scratch_shapes=scratch,
        compiler_params=pltpu.CompilerParams(vmem_limit_bytes=megabytes * 1024 * 1024),
        cost_estimate=pl.CostEstimate(
            flops=int(micros * 5e8), bytes_accessed=int(micros * 1e6), transcendentals=0
        ),
        name=name,
    )(*operands)


def body(
    points,
    embed_weight,
    inner_weights,
    output_weight,
    counts,
    point_order,
    inducing,
    first_proj,
    second_proj,
    mixing,
):
    along_x = lax.axis_size("tx")
    highs = lax.axis_size("zh")
    lows = lax.axis_size("zl")
    along_y = highs * lows
    point_count, width = points.shape
    quota = point_count // (along_x * along_y)
    grid_y = along_y * TLY
    blocks = 2
    members = along_x * lows
    tall = blocks * TLY
    lines = point_count // LANES
    chunk = 1024
    half_rows = (members, quota, width)

    def shape(sizes, dtype=BF):
        return jax.ShapeDtypeStruct(sizes, dtype)

    weights = (embed_weight, inner_weights, output_weight)
    buffers = [
        VMEM((point_count, width), F32),
        VMEM((chunk, width), F32),
        VMEM((chunk, width), F32),
    ]
    first, index = call(
        functools.partial(encode_first_kernel, grid_y, along_y, quota),
        "encode_first",
        (shape(half_rows), shape((lines, LANES), jnp.int32)),
        "aaaaaa",
        [
            SMEM((counts.shape[1],), jnp.int32),
            SMEM((counts.shape[1],), jnp.int32),
            SMEM((lines, LANES), jnp.int32),
        ]
        + buffers
        + [VMEM(a.shape, BF) for a in (points, *weights)]
        + [VMEM((lines, LANES), jnp.int32), pltpu.SemaphoreType.DMA((7,))],
        8,
        (points, *weights, counts, point_order.reshape(lines, LANES)),
        megabytes=56,
    )
    second = call(
        functools.partial(encode_second_kernel, quota),
        "encode_second",
        shape(half_rows),
        "vvvva",
        [SMEM((lines, LANES), jnp.int32)] + buffers + [pltpu.SemaphoreType.DMA],
        6,
        (points, *weights, index),
    )

    def exchange(rows):
        return lax.all_to_all(rows, ("tx", "zl"), split_axis=0, concat_axis=0, tiled=True)

    rows0 = exchange(first)
    rows1 = exchange(second)

    part_rows = 4 * LANES + 16
    parts = (shape((part_rows, LANES), F32), shape((part_rows, LANES)))
    sums = [VMEM((part_rows, HEADS * LANES), F32)]
    own0, send0, first_queries, value_weight = call(
        functools.partial(partial_kernel, 0, along_y),
        "partial_first",
        parts
        + (shape((HEADS * LANES, width)), shape((LANES, width))),
        "vsvv",
        sums,
        3,
        (rows0, counts, inducing, first_proj),
    )
    pairs = [(h, l) for h in range(highs) for l in range(lows)]

    def swap(value, flip_high, flip_low):
        steps = []
        for h, l in pairs:
            other_h = highs - 1 - h if flip_high else h
            other_l = lows - 1 - l if flip_low else l
            steps.append((h * lows + l, other_h * lows + other_l))
        return lax.ppermute(value, ("zh", "zl"), steps)

    other0 = swap(send0, True, False)
    query0 = call(
        functools.partial(queries_kernel, 0, along_y),
        "queries_first",
        shape((members, quota, 4 * width)),
        "vsva",
        [],
        1,
        (rows0, counts, second_proj, send0),
    )
    own1, send1 = call(
        functools.partial(partial_kernel, 1, along_y),
        "partial_second",
        parts,
        "vsvvva",
        sums,
        3,
        (rows1, counts, first_queries, value_weight, first_proj, query0),
    )
    other1 = swap(send1, True, False)
    first_half, border = call(
        combine_first_kernel,
        "combine_first",
        (shape((TLX, TLY, LANES, width)), shape((TLX, LANES, width))),
        "vvvva",
        [],
        0.01,
        (own0, other0, inducing, first_proj, send1),
    )
    column = swap(border, False, True)
    query1 = call(
        functools.partial(queries_kernel, 1, along_y),
        "queries_second",
        shape((members, quota, 4 * width)),
        "vsva",
        [],
        0.01,
        (rows1, counts, second_proj, border),
    )
    near_pairs = [(i, i ^ 1) for i in range(along_x)]
    far_pairs = [(i, ((i + 1) ^ 1) - 1) for i in range(1, along_x - 1)]

    def halo(near, far):
        far = lax.ppermute(far, "tx", far_pairs)
        return lax.ppermute(near, "tx", near_pairs), far

    early = shape((TLY + 1, LANES, width))
    near0, far0 = halo(
        *call(
            early_lines_kernel,
            "early_lines",
            (early,) * 2,
            "vva",
            [],
            0.01,
            (first_half, column, query1),
        )
    )
    late = shape((TLY, LANES, width))
    second_half, near1, far1 = call(
        combine_second_kernel,
        "combine_second",
        (shape((TLX, TLY, LANES, width)), late, late),
        "vvvva",
        [],
        0.01,
        (own1, other1, inducing, first_proj, query1),
    )
    near1, far1 = halo(near1, far1)

    keys, values = call(
        mixture_kernel,
        "mix_tiles",
        (shape((blocks, HEADS * LANES, 4 * LANES)), shape((blocks, HEADS * LANES, 4 * LANES))),
        "v" * 9,
        [
            VMEM((TLX + 2, tall + 2, LANES, width), BF),
            VMEM((6 * LANES, 2 * LANES), BF),
            VMEM((2, 4 * LANES, 2 * LANES), BF),
        ],
        1,
        (first_half, column, second_half, near0, far0, near1, far1, second_proj, mixing),
    )

    result = call(
        functools.partial(attend_kernel, along_y),
        "attend_points",
        shape((members, 2, quota, width)),
        "vvvvsvvv",
        [],
        7,
        (rows0, rows1, query0, query1, counts, keys, values, second_proj),
    )
    return call(
        scatter_kernel,
        "scatter_rows",
        shape((point_count, width)),
        "vs",
        [
            VMEM((point_count, width), F32),
            VMEM((512, width), F32),
            VMEM((point_count, width), BF),
            pltpu.SemaphoreType.DMA((4,)),
        ],
        5,
        (exchange(result), index),
        out_space=pl.ANY,
    )


def solution(mesh):
    along_x, along_y = mesh.devices.shape
    split = jax.sharding.Mesh(mesh.devices.reshape(along_x, 2, along_y // 2), ("tx", "zh", "zl"))
    rows = P(("tx", "zh", "zl"), None)
    placed = (rows, P(), P(), P(), P(), rows, P(), P(), P(), P())
    return jax.shard_map(body, mesh=split, in_specs=placed, out_specs=rows, check_vma=False)
```

```python
import functools
import math

import jax
import jax.numpy as jnp
from jax import lax
from jax.experimental import pallas as pl
from jax.experimental.pallas import tpu as pltpu
from jax.sharding import PartitionSpec as P

HEADS = 2
TLX = 2
TLY = 2
LANES = 128
GROUP_ROWS = 2048
BF = jnp.bfloat16
F32 = jnp.float32

sharpness = 32.0
epsilon = 1e-06
neighbour_steps = ((-1, -1), (-1, 0), (-1, 1), (0, -1), (0, 1), (1, -1), (1, 0), (1, 1))
VMEM = pltpu.VMEM
SMEM = pltpu.SMEM


def dot(a, b):
    return jnp.dot(a, b, preferred_element_type=F32)


def dot_t(a, b):
    return lax.dot_general(a, b, (((1,), (1,)), ((), ())), preferred_element_type=F32)


def head_ones():
    row = lax.broadcasted_iota(jnp.int32, (LANES, LANES), 0)
    col = lax.broadcasted_iota(jnp.int32, (LANES, LANES), 1)
    half = LANES // HEADS
    return jnp.where((row // half) == (col // half), 1.0, 0.0).astype(BF)


def unit(v, ones):
    return v * lax.rsqrt(dot((v * v).astype(BF), ones) + epsilon)


def silu(v):
    half = 0.5 * v
    return (half + half * jnp.tanh(half)).astype(BF)


def quotient(a, b):
    guess = pl.reciprocal(b, approx=True)
    return a * (guess * (2.0 - b * guess))


def place():
    return lax.axis_index("tx"), lax.axis_index("zh"), lax.axis_index("zl")


def block_of(half_id, low):
    return low if half_id else 1 - low


def encode_rows(half_id, quota, chunk, points, index_ready, weights_ready, w1_ref, w2_ref, w3_ref, index_s, feat_ref, wide_ref, xs):
    rows_total = points.shape[0] // 2
    group = chunk // quota
    wide_ref[...] = points[...].astype(F32)
    index_ready()

    def gather(c, buffer, first, last):
        for r in range(first, last):
            member = r // quota
            spot = (member * 2 + block_of(half_id, member % 2)) * quota + r % quota
            i = index_s[c * (2 * chunk // LANES) + spot // LANES, spot % LANES]
            buffer[pl.ds(r, 1), :] = wide_ref[pl.ds(i, 1), :]

    def layer(x, w, ahead, cuts):
        parts = []
        step = w.shape[1] // 2
        for k in range(2):
            ahead(cuts[k], cuts[k + 1])
            parts.append(silu(dot(x, w[:, k * step : (k + 1) * step])))
        return jnp.concatenate(parts, axis=1)

    def apply(c, buffer, ahead):
        cuts = [chunk * k // 5 for k in range(6)]
        hidden = layer(buffer[...].astype(BF), w1_ref, ahead, cuts[:3])
        hidden = layer(hidden, w2_ref.at[0], ahead, cuts[2:5])
        ahead(cuts[4], cuts[5])
        out = dot(hidden, w3_ref[...]).astype(BF)
        for k in range(group):
            feat_ref[c * group + k] = out[k * quota : (k + 1) * quota]

    chunks = rows_total // chunk
    gather(0, xs[0], 0, chunk)
    weights_ready()
    for c in range(chunks):

        def ahead(a, b):
            if c + 1 < chunks:
                gather(c + 1, xs[(c + 1) % 2], a, b)

        apply(c, xs[c % 2], ahead)


def encode_first_kernel(
    grid_y,
    along_y,
    quota,
    points_hbm,
    w1_hbm,
    w2_hbm,
    w3_hbm,
    counts_hbm,
    order_hbm,
    feat_ref,
    index_ref,
    counts_s,
    off_ref,
    index_s,
    wide_ref,
    xa_ref,
    xb_ref,
    points_ref,
    w1_ref,
    w2_ref,
    w3_ref,
    order_ref,
    sems,
):
    tx, zh, zl = place()
    own = tx * along_y + zh * (along_y // 2) + zl
    sources = (counts_hbm.at[own], order_hbm, points_hbm, w1_hbm, w2_hbm, w3_hbm)
    targets = (counts_s, order_ref, points_ref, w1_ref, w2_ref, w3_ref)
    copies = [
        pltpu.make_async_copy(a, b, sems.at[k]) for k, (a, b) in enumerate(zip(sources, targets))
    ]
    for copy in copies:
        copy.start()
    tiles = counts_s.shape[0]
    order_rows = order_ref.shape[0]
    rows_total = points_ref.shape[0]
    copies[0].wait()

    def add_up(g, total):
        off_ref[g] = total
        return total + counts_s[g]

    lax.fori_loop(0, tiles, add_up, jnp.int32(0), unroll=8)
    copies[1].wait()
    lane = lax.broadcasted_iota(jnp.int32, (1, LANES), 1)

    def run_of(start):
        line = start >> 7
        shift = start & (LANES - 1)
        first = order_ref[pl.ds(jnp.clip(line, 0, order_rows - 1), 1), :]
        second = order_ref[pl.ds(jnp.clip(line + 1, 0, order_rows - 1), 1), :]
        merged = jnp.where(lane < shift, second, first)
        return pltpu.roll(merged, (LANES - shift) & (LANES - 1), 1)

    per_line = LANES // quota

    def index_line(line, carry):
        value = jnp.zeros((1, LANES), jnp.int32)
        for k in range(per_line):
            d = line * per_line + k
            g1 = (d // along_y) * (TLX * grid_y) + (d % along_y) * TLY
            n1 = counts_s[g1] + counts_s[g1 + 1]
            run1 = run_of(off_ref[g1] - k * quota)
            run2 = run_of(off_ref[g1 + grid_y] - n1 - k * quota)
            both = jnp.where(lane < k * quota + n1, run1, run2)
            value = both if k == 0 else jnp.where(lane >= k * quota, both, value)
        index_ref[pl.ds(line, 1), :] = value
        return carry

    lax.fori_loop(0, rows_total // LANES, index_line, 0, unroll=8)
    copy = pltpu.make_async_copy(index_ref, index_s, sems.at[6])
    copy.start()
    copies[2].wait()

    def weights_ready():
        for k in (3, 4, 5):
            copies[k].wait()

    encode_rows(
        0, quota, xa_ref.shape[0], points_ref, copy.wait, weights_ready, w1_ref, w2_ref, w3_ref, index_s,
        feat_ref, wide_ref, (xa_ref, xb_ref),
    )


def encode_second_kernel(
    quota, points_ref, w1_ref, w2_ref, w3_ref, index_any, feat_ref, index_s, wide_ref, xa_ref, xb_ref, sem
):
    copy = pltpu.make_async_copy(index_any, index_s, sem)
    copy.start()
    encode_rows(
        1, quota, xa_ref.shape[0], points_ref, copy.wait, lambda: None, w1_ref, w2_ref, w3_ref, index_s,
        feat_ref, wide_ref, (xa_ref, xb_ref),
    )


def tile_of(position, counts_ref, pieces, piece_id, grid_y):
    bounds = [None, None, None]
    for k, (s, base) in enumerate(pieces):
        n0 = counts_ref[s, base]
        n1 = counts_ref[s, base + 1]
        n2 = counts_ref[s, base + grid_y]
        for i, found in enumerate((n0, n0 + n1, n0 + n1 + n2)):
            if k == 0:
                bounds[i] = jnp.full(position.shape, found, jnp.int32)
            else:
                bounds[i] = jnp.where(piece_id >= k, found, bounds[i])
    return sum((position >= b).astype(jnp.int32) for b in bounds)


def pieces_of(first, group, half_id, along_y):
    tx, zh, zl = place()
    lows = along_y // 2
    block = zl * 2 + block_of(half_id, zl)
    base = tx * (TLX * along_y * TLY) + block * TLY
    found = []
    for k in range(group):
        member = first + k
        found.append(((member // lows) * along_y + zh * lows + member % lows, base))
    return found


def row_bounds(piece, counts_ref, grid_y):
    s, base = piece
    n0 = counts_ref[s, base]
    n1 = n0 + counts_ref[s, base + 1]
    return n0, n1, n1 + counts_ref[s, base + grid_y]


def expand_queries(half_id, along_y, rows_ref, counts_ref, proj_ref, out_ref):
    ones = head_ones()
    members, quota, width = rows_ref.shape
    group = min(GROUP_ROWS // quota, members)
    row = lax.broadcasted_iota(jnp.int32, (quota, LANES), 0)
    for c in range(members // group):
        x = jnp.concatenate([rows_ref[c * group + k] for k in range(group)], axis=0)
        query = unit(dot(x, proj_ref[0]), ones)
        pieces = pieces_of(c * group, group, half_id, along_y)
        for k in range(group):
            bounds = row_bounds(pieces[k], counts_ref, along_y * TLY)
            past = [row >= b for b in bounds]
            mine = query[k * quota : (k + 1) * quota]
            masks = (~past[0], past[0] & ~past[1], past[1] & ~past[2], past[2])
            out_ref[c * group + k] = jnp.concatenate(
                [jnp.where(m, mine, 0.0).astype(BF) for m in masks], axis=1
            )


def partial_kernel(half_id, along_y, rows_ref, counts_ref, *rest):
    num_ref = rest[-1]
    if half_id:
        query_ref, wv_ref, proj_ref, own_ref, send_ref = rest[:-1]
    else:
        inducing_ref, proj_ref, second_ref, own_ref, send_ref, query_ref, wv_ref, point_ref = rest[:-1]
        expand_queries(0, along_y, rows_ref, counts_ref, second_ref, point_ref)
    members, quota, width = rows_ref.shape
    grid_y = along_y * TLY
    half = LANES // HEADS
    group = min(GROUP_ROWS // quota, members)
    chunk = group * quota
    ones = head_ones()
    lane = lax.broadcasted_iota(jnp.int32, (1, LANES), 1)
    left = lane < half
    if half_id:
        queries = query_ref[...]
        wv_t = wv_ref[...]
    else:
        queries = unit(dot(inducing_ref[...], proj_ref[0]), ones)
        queries = jnp.concatenate(
            [jnp.where(left, queries, 0.0), jnp.where(left, 0.0, queries)], axis=0
        ).astype(BF)
        wv_t = proj_ref[2].astype(F32).T.astype(BF)
        query_ref[...] = queries
        wv_ref[...] = wv_t
    spot = lax.broadcasted_iota(jnp.int32, (16, chunk), 1)
    tile_row = lax.broadcasted_iota(jnp.int32, (16, chunk), 0)
    for c in range(members // group):
        x = jnp.concatenate([rows_ref[c * group + k] for k in range(group)], axis=0)
        keys = unit(dot(x, proj_ref[1]), ones).astype(BF)
        weights = jnp.exp2(dot_t(keys, queries) * (sharpness * math.log2(math.e))).astype(BF)
        values = dot_t(wv_t, x).astype(BF)
        pieces = pieces_of(c * group, group, half_id, along_y)
        tile = tile_of(spot % quota, counts_ref, pieces, spot // quota, grid_y)
        stacked = []
        for t in range(4):
            mask = jnp.where(tile == t, 1.0, 0.0).astype(BF)
            stacked += [values[k : k + 16] * mask for k in range(0, LANES, 16)]
        stacked.append(jnp.where(tile_row == tile, 1.0, 0.0).astype(BF))
        sums = dot(jnp.concatenate(stacked, axis=0), weights)
        if c == 0:
            num_ref[...] = sums
        else:
            num_ref[...] += sums
    last = 4 * LANES
    for t in range(4):
        rows = slice(t * LANES, (t + 1) * LANES)
        value = jnp.concatenate(
            [
                num_ref[t * LANES : t * LANES + half, :LANES],
                num_ref[t * LANES + half : (t + 1) * LANES, LANES:],
            ],
            axis=0,
        )
        own_ref[rows, :] = value
        send_ref[rows, :] = value.astype(BF)
    totals = jnp.concatenate(
        [num_ref[last : last + 4, h * LANES : (h + 1) * LANES] for h in range(HEADS)]
        + [jnp.zeros((8, LANES), F32)],
        axis=0,
    )
    own_ref[last:, :] = totals
    send_ref[last:, :] = totals.astype(BF)

def queries_kernel(along_y, rows_ref, counts_ref, proj_ref, before_any, out_ref):
    expand_queries(1, along_y, rows_ref, counts_ref, proj_ref, out_ref)


def summarize(half_id, own_ref, other_ref, inducing_ref, proj_ref, store):
    half = LANES // HEADS
    last = 4 * LANES
    totals = own_ref[last:, :] + other_ref[last:, :].astype(F32)
    for t in range(4):
        rows = slice(t * LANES, (t + 1) * LANES)
        value = own_ref[rows, :] + other_ref[rows, :].astype(F32)
        attended = jnp.concatenate(
            [value[:half] / totals[t : t + 1], value[half:] / totals[t + 4 : t + 5]], axis=0
        )
        out = inducing_ref[...].astype(F32) + dot(attended.T.astype(BF), proj_ref[3])
        store(t // TLY, t % TLY, out.astype(BF))


def combine_first_kernel(
    own_ref, other_ref, inducing_ref, proj_ref, after_any, out_ref, column_ref
):
    def store(x, y, value):
        out_ref[x, y] = value

    summarize(0, own_ref, other_ref, inducing_ref, proj_ref, store)
    for x in range(TLX):
        column_ref[x] = jnp.where(lax.axis_index("zl") == 0, out_ref[x, TLY - 1], out_ref[x, 0])


def pair_lines(rows, near_ref, far_ref):
    even = lax.axis_index("tx") % 2 == 0
    for y, (low, high) in enumerate(zip(*rows)):
        near_ref[y] = jnp.where(even, high, low)
        far_ref[y] = jnp.where(even, low, high)


def early_lines_kernel(first_ref, column_ref, query_any, near_ref, far_ref):
    rows = [[first_ref[x, y] for y in range(TLY)] + [column_ref[x]] for x in range(TLX)]
    pair_lines(rows, near_ref, far_ref)


def combine_second_kernel(
    own_ref, other_ref, inducing_ref, proj_ref, query_any, out_ref, near_ref, far_ref
):
    def store(x, y, value):
        out_ref[x, y] = value

    summarize(1, own_ref, other_ref, inducing_ref, proj_ref, store)
    pair_lines([[out_ref[x, y] for y in range(TLY)] for x in range(TLX)], near_ref, far_ref)


def mixture_kernel(
    first_ref,
    column_ref,
    second_ref,
    near0_ref,
    far0_ref,
    near1_ref,
    far1_ref,
    proj_ref,
    mixing_ref,
    key_ref,
    value_ref,
    grid_ref,
    mid_ref,
    side_ref,
):
    half = LANES // HEADS
    blocks = key_ref.shape[0]
    tall = blocks * TLY
    low = lax.axis_index("zl")

    row = lax.broadcasted_iota(jnp.int32, (LANES, LANES), 0)
    col = lax.broadcasted_iota(jnp.int32, (LANES, LANES), 1)
    eye = jnp.where(row == col, 1.0, 0.0).astype(BF)
    blank = jnp.zeros((LANES, LANES), BF)

    def mix(a, b):
        return eye if (a, b) == (0, 0) else mixing_ref[neighbour_steps.index((a, b))]

    for k, a in enumerate((-1, 0, 1)):
        rows = slice(k * 2 * LANES, (k + 1) * 2 * LANES)
        mid_ref[rows, :] = jnp.concatenate(
            [
                jnp.concatenate([mix(a, 0), mix(a, -1)], axis=1),
                jnp.concatenate([mix(a, 1), mix(a, 0)], axis=1),
            ],
            axis=0,
        )
    for k, b in enumerate((-1, 1)):
        side_ref[k] = jnp.concatenate(
            [
                jnp.concatenate([mix(0, b), mix(-1, b)], axis=1),
                jnp.concatenate([mix(1, b), mix(0, b)], axis=1),
                jnp.concatenate([mix(-1, b), blank], axis=1),
                jnp.concatenate([blank, mix(1, b)], axis=1),
            ],
            axis=0,
        )
    ones = head_ones()
    lane = lax.broadcasted_iota(jnp.int32, (1, LANES), 1)
    left = lane < half
    even = lax.axis_index("tx") % 2
    near_row = (1 - even) * (TLX + 1)
    far_row = even * (TLX + 1)
    border = (1 - low) * (tall + 1)
    outside = low * (tall + 1)
    for x in range(TLX):
        for y in range(TLY):
            grid_ref[1 + x, 1 + block_of(0, low) * TLY + y] = first_ref[x, y]
            grid_ref[1 + x, 1 + block_of(1, low) * TLY + y] = second_ref[x, y]
        grid_ref[1 + x, border] = column_ref[x]
    for line, early_ref, late_ref in ((near_row, near0_ref, near1_ref), (far_row, far0_ref, far1_ref)):
        for y in range(TLY):
            grid_ref[line, 1 + block_of(0, low) * TLY + y] = early_ref[y]
            grid_ref[line, 1 + block_of(1, low) * TLY + y] = late_ref[y]
        grid_ref[line, border] = early_ref[TLY]
    for x in range(TLX + 2):
        grid_ref[x, outside] = blank

    def tile(i, j):
        return grid_ref[i, j + 1]

    mids, lefts, rights = [], [], []
    for i in range(2):
        for b in range(blocks):
            mids.append(
                jnp.concatenate(
                    [tile(i + r, 2 * b + s) for r in range(3) for s in range(2)], axis=1
                )
            )
    for b in range(blocks):
        lefts.append(jnp.concatenate([tile(i, 2 * b - 1) for i in (1, 2, 0, 3)], axis=1))
        rights.append(jnp.concatenate([tile(i, 2 * b + 2) for i in (1, 2, 0, 3)], axis=1))
    middle = dot(jnp.concatenate(mids, axis=0), mid_ref[...])
    from_left = dot(jnp.concatenate(lefts, axis=0), side_ref[0])
    from_right = dot(jnp.concatenate(rights, axis=0), side_ref[1])
    mixtures = []
    for b in range(blocks):
        span = slice(b * LANES, (b + 1) * LANES)
        for i in range(2):
            m = middle[(i * blocks + b) * LANES : (i * blocks + b + 1) * LANES]
            cols = slice(i * LANES, (i + 1) * LANES)
            mixtures.append((m[:, :LANES] + from_left[span, cols]).astype(BF))
            mixtures.append((m[:, LANES:] + from_right[span, cols]).astype(BF))
    mixtures = jnp.concatenate(mixtures, axis=0)
    keys = unit(dot(mixtures, proj_ref[1]), ones)
    values = dot(mixtures, proj_ref[2])
    for b in range(blocks):
        spans = [slice((b * 4 + t) * LANES, (b * 4 + t + 1) * LANES) for t in range(4)]
        for h in range(HEADS):
            mine = left if h == 0 else ~left
            key_ref[b, h * LANES : (h + 1) * LANES, :] = jnp.concatenate(
                [jnp.where(mine, keys[s], 0.0) for s in spans], axis=1
            ).astype(BF)
            turned = [pltpu.roll(values[s], LANES // HEADS, 1) for s in spans]
            value_ref[b, h] = jnp.concatenate(
                [
                    jnp.where(left, values[spans[p]], turned[p + 1])
                    if h == 0
                    else jnp.where(left, turned[p + 1], values[spans[p]])
                    for p in (0, 2)
                ],
                axis=1,
            ).astype(BF)


def attend_kernel(
    along_y,
    rows0_ref,
    rows1_ref,
    query0_ref,
    query1_ref,
    counts_ref,
    key_ref,
    value_ref,
    proj_ref,
    out_ref,
):
    members, quota, width = rows0_ref.shape
    group = min(GROUP_ROWS // quota, members)
    row = lax.broadcasted_iota(jnp.int32, (quota, LANES), 0)
    left = lax.broadcasted_iota(jnp.int32, (1, LANES), 1) < LANES // HEADS
    for half_id, (rows_ref, query_ref) in enumerate(
        ((rows0_ref, query0_ref), (rows1_ref, query1_ref))
    ):
        block = block_of(half_id, lax.axis_index("zl"))
        for c in range(members // group):
            expanded = jnp.concatenate([query_ref[c * group + k] for k in range(group)], axis=0)
            scores = dot_t(expanded, key_ref[block])
            weights = jnp.exp2(scores * (sharpness * math.log2(math.e)))
            totals = [
                jnp.sum(weights[:, h * LANES : (h + 1) * LANES], axis=1, keepdims=True)
                for h in range(HEADS)
            ]
            every = [
                dot(weights[:, h * LANES : (h + 1) * LANES].astype(BF), value_ref[block, h])
                for h in range(HEADS)
            ]
            pieces = pieces_of(c * group, group, half_id, along_y)
            attended = []
            for k in range(group):
                first, second, third = row_bounds(pieces[k], counts_ref, along_y * TLY)
                span = slice(k * quota, (k + 1) * quota)
                upper = row >= second
                odd = ((row >= first) & (row < second)) | (row >= third)
                part = [jnp.where(upper, e[span, LANES:], e[span, :LANES]) for e in every]
                even_tile = jnp.where(left, part[0], part[1])
                odd_tile = pltpu.roll(jnp.where(left, part[1], part[0]), LANES // HEADS, 1)
                total = jnp.where(left, totals[0][span], totals[1][span])
                picked = jnp.where(odd, odd_tile, even_tile)
                attended.append(quotient(picked, total).astype(BF))
            x = jnp.concatenate([rows_ref[c * group + k] for k in range(group)], axis=0)
            added = dot(jnp.concatenate(attended, axis=0), proj_ref[3])
            result = (x.astype(F32) + added).astype(BF)
            for k in range(group):
                out_ref[c * group + k, half_id] = result[k * quota : (k + 1) * quota]


def scatter_kernel(rows_ref, index_ref, out_hbm, wide_ref, part_ref, out_ref, sems):
    chunk = part_ref.shape[0]
    members, halves, quota, width = rows_ref.shape
    group = chunk // (halves * quota)

    def step(c, carry):
        for k in range(group):
            for half_id in range(halves):
                row = (k * halves + block_of(half_id, k % 2)) * quota
                part_ref[row : row + quota, :] = rows_ref[c * group + k, half_id].astype(F32)
        for r in range(chunk):
            i = index_ref[c * (chunk // LANES) + r // LANES, r % LANES]
            wide_ref[pl.ds(i, 1), :] = part_ref[pl.ds(r, 1), :]
        return carry

    lax.fori_loop(0, members // group, step, 0)
    count = sems.shape[0]
    size = wide_ref.shape[0] // count
    copies = []
    for k in range(count):
        span = pl.ds(k * size, size)
        out_ref[span, :] = wide_ref[span, :].astype(BF)
        copies.append(pltpu.make_async_copy(out_ref.at[span], out_hbm.at[span], sems.at[k]))
        copies[k].start()
    for copy in copies:
        copy.wait()


def call(kernel, name, out_shape, in_specs, scratch, micros, operands, megabytes=20, out_space=pltpu.VMEM):
    spaces = {"v": pltpu.VMEM, "s": pltpu.SMEM, "a": pl.ANY}
    many = isinstance(out_shape, tuple)
    whole = pl.BlockSpec(memory_space=out_space)
    return pl.pallas_call(
        kernel,
        out_shape=out_shape,
        in_specs=[pl.BlockSpec(memory_space=spaces[c]) for c in in_specs],
        out_specs=(whole,) * len(out_shape) if many else whole,
        scratch_shapes=scratch,
        compiler_params=pltpu.CompilerParams(vmem_limit_bytes=megabytes * 1024 * 1024),
        cost_estimate=pl.CostEstimate(
            flops=int(micros * 5e8), bytes_accessed=int(micros * 1e6), transcendentals=0
        ),
        name=name,
    )(*operands)


def body(
    points,
    embed_weight,
    inner_weights,
    output_weight,
    counts,
    point_order,
    inducing,
    first_proj,
    second_proj,
    mixing,
):
    along_x = lax.axis_size("tx")
    highs = lax.axis_size("zh")
    lows = lax.axis_size("zl")
    along_y = highs * lows
    point_count, width = points.shape
    quota = point_count // (along_x * along_y)
    grid_y = along_y * TLY
    blocks = 2
    members = along_x * lows
    tall = blocks * TLY
    lines = point_count // LANES
    chunk = 1024
    half_rows = (members, quota, width)

    def shape(sizes, dtype=BF):
        return jax.ShapeDtypeStruct(sizes, dtype)

    weights = (embed_weight, inner_weights, output_weight)
    buffers = [
        VMEM((point_count, width), F32),
        VMEM((chunk, width), F32),
        VMEM((chunk, width), F32),
    ]
    first, index = call(
        functools.partial(encode_first_kernel, grid_y, along_y, quota),
        "encode_first",
        (shape(half_rows), shape((lines, LANES), jnp.int32)),
        "aaaaaa",
        [
            SMEM((counts.shape[1],), jnp.int32),
            SMEM((counts.shape[1],), jnp.int32),
            SMEM((lines, LANES), jnp.int32),
        ]
        + buffers
        + [VMEM(a.shape, BF) for a in (points, *weights)]
        + [VMEM((lines, LANES), jnp.int32), pltpu.SemaphoreType.DMA((7,))],
        8,
        (points, *weights, counts, point_order.reshape(lines, LANES)),
        megabytes=56,
    )
    second = call(
        functools.partial(encode_second_kernel, quota),
        "encode_second",
        shape(half_rows),
        "vvvva",
        [SMEM((lines, LANES), jnp.int32)] + buffers + [pltpu.SemaphoreType.DMA],
        6,
        (points, *weights, index),
    )

    def exchange(rows):
        return lax.all_to_all(rows, ("tx", "zl"), split_axis=0, concat_axis=0, tiled=True)

    rows0 = exchange(first)
    rows1 = exchange(second)

    part_rows = 4 * LANES + 16
    parts = (shape((part_rows, LANES), F32), shape((part_rows, LANES)))
    sums = [VMEM((part_rows, HEADS * LANES), F32)]
    expanded = shape((members, quota, 4 * width))
    own0, send0, first_queries, value_weight, query0 = call(
        functools.partial(partial_kernel, 0, along_y),
        "partial_first",
        parts
        + (shape((HEADS * LANES, width)), shape((LANES, width)), expanded),
        "vsvvv",
        sums,
        3,
        (rows0, counts, inducing, first_proj, second_proj),
    )
    pairs = [(h, l) for h in range(highs) for l in range(lows)]

    def swap(value, flip_high, flip_low):
        steps = []
        for h, l in pairs:
            other_h = highs - 1 - h if flip_high else h
            other_l = lows - 1 - l if flip_low else l
            steps.append((h * lows + l, other_h * lows + other_l))
        return lax.ppermute(value, ("zh", "zl"), steps)

    other0 = swap(send0, True, False)
    own1, send1 = call(
        functools.partial(partial_kernel, 1, along_y),
        "partial_second",
        parts,
        "vsvvv",
        sums,
        3,
        (rows1, counts, first_queries, value_weight, first_proj),
    )
    other1 = swap(send1, True, False)
    first_half, border = call(
        combine_first_kernel,
        "combine_first",
        (shape((TLX, TLY, LANES, width)), shape((TLX, LANES, width))),
        "vvvva",
        [],
        0.01,
        (own0, other0, inducing, first_proj, send1),
    )
    column = swap(border, False, True)
    query1 = call(
        functools.partial(queries_kernel, along_y),
        "queries_second",
        expanded,
        "vsva",
        [],
        0.01,
        (rows1, counts, second_proj, border),
    )
    near_pairs = [(i, i ^ 1) for i in range(along_x)]
    far_pairs = [(i, ((i + 1) ^ 1) - 1) for i in range(1, along_x - 1)]

    def halo(near, far):
        far = lax.ppermute(far, "tx", far_pairs)
        return lax.ppermute(near, "tx", near_pairs), far

    early = shape((TLY + 1, LANES, width))
    near0, far0 = halo(
        *call(
            early_lines_kernel,
            "early_lines",
            (early,) * 2,
            "vva",
            [],
            0.01,
            (first_half, column, query1),
        )
    )
    late = shape((TLY, LANES, width))
    second_half, near1, far1 = call(
        combine_second_kernel,
        "combine_second",
        (shape((TLX, TLY, LANES, width)), late, late),
        "vvvva",
        [],
        0.01,
        (own1, other1, inducing, first_proj, query1),
    )
    near1, far1 = halo(near1, far1)

    keys, values = call(
        mixture_kernel,
        "mix_tiles",
        (shape((blocks, HEADS * LANES, 4 * LANES)), shape((blocks, HEADS, LANES, 2 * LANES))),
        "v" * 9,
        [
            VMEM((TLX + 2, tall + 2, LANES, width), BF),
            VMEM((6 * LANES, 2 * LANES), BF),
            VMEM((2, 4 * LANES, 2 * LANES), BF),
        ],
        1,
        (first_half, column, second_half, near0, far0, near1, far1, second_proj, mixing),
    )

    result = call(
        functools.partial(attend_kernel, along_y),
        "attend_points",
        shape((members, 2, quota, width)),
        "vvvvsvvv",
        [],
        7,
        (rows0, rows1, query0, query1, counts, keys, values, second_proj),
    )
    return call(
        scatter_kernel,
        "scatter_rows",
        shape((point_count, width)),
        "vs",
        [
            VMEM((point_count, width), F32),
            VMEM((512, width), F32),
            VMEM((point_count, width), BF),
            pltpu.SemaphoreType.DMA((4,)),
        ],
        5,
        (exchange(result), index),
        out_space=pl.ANY,
    )


def solution(mesh):
    along_x, along_y = mesh.devices.shape
    split = jax.sharding.Mesh(mesh.devices.reshape(along_x, 2, along_y // 2), ("tx", "zh", "zl"))
    rows = P(("tx", "zh", "zl"), None)
    placed = (rows, P(), P(), P(), P(), rows, P(), P(), P(), P())
    return jax.shard_map(body, mesh=split, in_specs=placed, out_specs=rows, check_vma=False)
```

```python
import functools
import math

import jax
import jax.numpy as jnp
from jax import lax
from jax.experimental import pallas as pl
from jax.experimental.pallas import tpu as pltpu
from jax.sharding import PartitionSpec as P

HEADS = 2
TLX = 2
TLY = 2
LANES = 128
GROUP_ROWS = 2048
BF = jnp.bfloat16
F32 = jnp.float32

sharpness = 32.0
epsilon = 1e-06
neighbour_steps = ((-1, -1), (-1, 0), (-1, 1), (0, -1), (0, 1), (1, -1), (1, 0), (1, 1))
VMEM = pltpu.VMEM
SMEM = pltpu.SMEM


def dot(a, b):
    return jnp.dot(a, b, preferred_element_type=F32)


def dot_t(a, b):
    return lax.dot_general(a, b, (((1,), (1,)), ((), ())), preferred_element_type=F32)


def head_ones():
    row = lax.broadcasted_iota(jnp.int32, (LANES, LANES), 0)
    col = lax.broadcasted_iota(jnp.int32, (LANES, LANES), 1)
    half = LANES // HEADS
    return jnp.where((row // half) == (col // half), 1.0, 0.0).astype(BF)


def unit(v, ones):
    return v * lax.rsqrt(dot((v * v).astype(BF), ones) + epsilon)


def silu(v):
    half = 0.5 * v
    return (half + half * jnp.tanh(half)).astype(BF)


def quotient(a, b):
    guess = pl.reciprocal(b, approx=True)
    return a * (guess * (2.0 - b * guess))


def place():
    return lax.axis_index("tx"), lax.axis_index("zh"), lax.axis_index("zl")


def block_of(half_id, low):
    return low if half_id else 1 - low


def encode_rows(half_id, quota, chunk, points, index_ready, weights_ready, w1_ref, w2_ref, w3_ref, index_s, feat_ref, wide_ref, xs):
    rows_total = points.shape[0] // 2
    group = chunk // quota
    wide_ref[...] = points[...].astype(F32)
    index_ready()

    def gather(c, buffer, first, last):
        for r in range(first, last):
            member = r // quota
            spot = (member * 2 + block_of(half_id, member % 2)) * quota + r % quota
            i = index_s[c * (2 * chunk // LANES) + spot // LANES, spot % LANES]
            buffer[pl.ds(r, 1), :] = wide_ref[pl.ds(i, 1), :]

    def layer(x, w, ahead, cuts):
        parts = []
        step = w.shape[1] // 2
        for k in range(2):
            ahead(cuts[k], cuts[k + 1])
            parts.append(silu(dot(x, w[:, k * step : (k + 1) * step])))
        return jnp.concatenate(parts, axis=1)

    def apply(c, buffer, ahead):
        cuts = [chunk * k // 5 for k in range(6)]
        hidden = layer(buffer[...].astype(BF), w1_ref, ahead, cuts[:3])
        hidden = layer(hidden, w2_ref.at[0], ahead, cuts[2:5])
        ahead(cuts[4], cuts[5])
        out = dot(hidden, w3_ref[...]).astype(BF)
        for k in range(group):
            feat_ref[c * group + k] = out[k * quota : (k + 1) * quota]

    chunks = rows_total // chunk
    gather(0, xs[0], 0, chunk)
    weights_ready()
    for c in range(chunks):

        def ahead(a, b):
            if c + 1 < chunks:
                gather(c + 1, xs[(c + 1) % 2], a, b)

        apply(c, xs[c % 2], ahead)


def encode_first_kernel(
    grid_y,
    along_y,
    quota,
    points_hbm,
    w1_hbm,
    w2_hbm,
    w3_hbm,
    counts_hbm,
    order_hbm,
    feat_ref,
    index_ref,
    counts_s,
    off_ref,
    index_s,
    wide_ref,
    xa_ref,
    xb_ref,
    points_ref,
    w1_ref,
    w2_ref,
    w3_ref,
    order_ref,
    sems,
):
    tx, zh, zl = place()
    own = tx * along_y + zh * (along_y // 2) + zl
    sources = (counts_hbm.at[own], order_hbm, points_hbm, w1_hbm, w2_hbm, w3_hbm)
    targets = (counts_s, order_ref, points_ref, w1_ref, w2_ref, w3_ref)
    copies = [
        pltpu.make_async_copy(a, b, sems.at[k]) for k, (a, b) in enumerate(zip(sources, targets))
    ]
    for copy in copies:
        copy.start()
    tiles = counts_s.shape[0]
    order_rows = order_ref.shape[0]
    rows_total = points_ref.shape[0]
    copies[0].wait()

    def add_up(g, total):
        off_ref[g] = total
        return total + counts_s[g]

    lax.fori_loop(0, tiles, add_up, jnp.int32(0), unroll=8)
    copies[1].wait()
    lane = lax.broadcasted_iota(jnp.int32, (1, LANES), 1)

    def run_of(start):
        line = start >> 7
        shift = start & (LANES - 1)
        first = order_ref[pl.ds(jnp.clip(line, 0, order_rows - 1), 1), :]
        second = order_ref[pl.ds(jnp.clip(line + 1, 0, order_rows - 1), 1), :]
        merged = jnp.where(lane < shift, second, first)
        return pltpu.roll(merged, (LANES - shift) & (LANES - 1), 1)

    per_line = LANES // quota

    def index_line(line, carry):
        value = jnp.zeros((1, LANES), jnp.int32)
        for k in range(per_line):
            d = line * per_line + k
            g1 = (d // along_y) * (TLX * grid_y) + (d % along_y) * TLY
            n1 = counts_s[g1] + counts_s[g1 + 1]
            run1 = run_of(off_ref[g1] - k * quota)
            run2 = run_of(off_ref[g1 + grid_y] - n1 - k * quota)
            both = jnp.where(lane < k * quota + n1, run1, run2)
            value = both if k == 0 else jnp.where(lane >= k * quota, both, value)
        index_ref[pl.ds(line, 1), :] = value
        return carry

    lax.fori_loop(0, rows_total // LANES, index_line, 0, unroll=8)
    copy = pltpu.make_async_copy(index_ref, index_s, sems.at[6])
    copy.start()
    copies[2].wait()

    def weights_ready():
        for k in (3, 4, 5):
            copies[k].wait()

    encode_rows(
        0, quota, xa_ref.shape[0], points_ref, copy.wait, weights_ready, w1_ref, w2_ref, w3_ref, index_s,
        feat_ref, wide_ref, (xa_ref, xb_ref),
    )


def encode_second_kernel(
    quota, points_ref, w1_ref, w2_ref, w3_ref, index_any, feat_ref, index_s, wide_ref, xa_ref, xb_ref, sem
):
    copy = pltpu.make_async_copy(index_any, index_s, sem)
    copy.start()
    encode_rows(
        1, quota, xa_ref.shape[0], points_ref, copy.wait, lambda: None, w1_ref, w2_ref, w3_ref, index_s,
        feat_ref, wide_ref, (xa_ref, xb_ref),
    )


def tile_of(position, counts_ref, pieces, piece_id, grid_y):
    bounds = [None, None, None]
    for k, (s, base) in enumerate(pieces):
        n0 = counts_ref[s, base]
        n1 = counts_ref[s, base + 1]
        n2 = counts_ref[s, base + grid_y]
        for i, found in enumerate((n0, n0 + n1, n0 + n1 + n2)):
            if k == 0:
                bounds[i] = jnp.full(position.shape, found, jnp.int32)
            else:
                bounds[i] = jnp.where(piece_id >= k, found, bounds[i])
    return sum((position >= b).astype(jnp.int32) for b in bounds)


def pieces_of(first, group, half_id, along_y):
    tx, zh, zl = place()
    lows = along_y // 2
    block = zl * 2 + block_of(half_id, zl)
    base = tx * (TLX * along_y * TLY) + block * TLY
    found = []
    for k in range(group):
        member = first + k
        found.append(((member // lows) * along_y + zh * lows + member % lows, base))
    return found


def row_bounds(piece, counts_ref, grid_y):
    s, base = piece
    n0 = counts_ref[s, base]
    n1 = n0 + counts_ref[s, base + 1]
    return n0, n1, n1 + counts_ref[s, base + grid_y]


def expand_queries(half_id, along_y, rows_ref, counts_ref, proj_ref, out_ref):
    ones = head_ones()
    members, quota, width = rows_ref.shape
    group = min(GROUP_ROWS // quota, members)
    row = lax.broadcasted_iota(jnp.int32, (quota, LANES), 0)
    for c in range(members // group):
        x = jnp.concatenate([rows_ref[c * group + k] for k in range(group)], axis=0)
        query = unit(dot(x, proj_ref[0]), ones)
        pieces = pieces_of(c * group, group, half_id, along_y)
        for k in range(group):
            bounds = row_bounds(pieces[k], counts_ref, along_y * TLY)
            past = [row >= b for b in bounds]
            mine = query[k * quota : (k + 1) * quota]
            masks = (~past[0], past[0] & ~past[1], past[1] & ~past[2], past[2])
            out_ref[c * group + k] = jnp.concatenate(
                [jnp.where(m, mine, 0.0).astype(BF) for m in masks], axis=1
            )


def partial_kernel(half_id, along_y, rows_ref, counts_ref, *rest):
    num_ref = rest[-1]
    if half_id:
        query_ref, wv_ref, proj_ref, own_ref, send_ref = rest[:-1]
    else:
        inducing_ref, proj_ref, second_ref, own_ref, send_ref, query_ref, wv_ref, point_ref = rest[:-1]
        expand_queries(0, along_y, rows_ref, counts_ref, second_ref, point_ref)
    members, quota, width = rows_ref.shape
    grid_y = along_y * TLY
    half = LANES // HEADS
    group = min(GROUP_ROWS // quota, members)
    chunk = group * quota
    ones = head_ones()
    lane = lax.broadcasted_iota(jnp.int32, (1, LANES), 1)
    left = lane < half
    if half_id:
        queries = query_ref[...]
        wv_t = wv_ref[...]
    else:
        queries = unit(dot(inducing_ref[...], proj_ref[0]), ones)
        queries = jnp.concatenate(
            [jnp.where(left, queries, 0.0), jnp.where(left, 0.0, queries)], axis=0
        ).astype(BF)
        wv_t = proj_ref[2].astype(F32).T.astype(BF)
        query_ref[...] = queries
        wv_ref[...] = wv_t
    spot = lax.broadcasted_iota(jnp.int32, (16, chunk), 1)
    tile_row = lax.broadcasted_iota(jnp.int32, (16, chunk), 0)
    for c in range(members // group):
        x = jnp.concatenate([rows_ref[c * group + k] for k in range(group)], axis=0)
        keys = unit(dot(x, proj_ref[1]), ones).astype(BF)
        weights = jnp.exp2(dot_t(keys, queries) * (sharpness * math.log2(math.e))).astype(BF)
        values = dot_t(wv_t, x).astype(BF)
        pieces = pieces_of(c * group, group, half_id, along_y)
        tile = tile_of(spot % quota, counts_ref, pieces, spot // quota, grid_y)
        stacked = []
        for t in range(4):
            mask = jnp.where(tile == t, 1.0, 0.0).astype(BF)
            stacked += [values[k : k + 16] * mask for k in range(0, LANES, 16)]
        stacked.append(jnp.where(tile_row == tile, 1.0, 0.0).astype(BF))
        sums = dot(jnp.concatenate(stacked, axis=0), weights)
        if c == 0:
            num_ref[...] = sums
        else:
            num_ref[...] += sums
    last = 4 * LANES
    for t in range(4):
        rows = slice(t * LANES, (t + 1) * LANES)
        value = jnp.concatenate(
            [
                num_ref[t * LANES : t * LANES + half, :LANES],
                num_ref[t * LANES + half : (t + 1) * LANES, LANES:],
            ],
            axis=0,
        )
        own_ref[rows, :] = value
        send_ref[rows, :] = value.astype(BF)
    totals = jnp.concatenate(
        [num_ref[last : last + 4, h * LANES : (h + 1) * LANES] for h in range(HEADS)]
        + [jnp.zeros((8, LANES), F32)],
        axis=0,
    )
    own_ref[last:, :] = totals
    send_ref[last:, :] = totals.astype(BF)

def queries_kernel(along_y, rows_ref, counts_ref, proj_ref, before_any, out_ref):
    expand_queries(1, along_y, rows_ref, counts_ref, proj_ref, out_ref)


def summarize(half_id, own_ref, other_ref, inducing_ref, proj_ref, store):
    half = LANES // HEADS
    last = 4 * LANES
    totals = own_ref[last:, :] + other_ref[last:, :].astype(F32)
    for t in range(4):
        rows = slice(t * LANES, (t + 1) * LANES)
        value = own_ref[rows, :] + other_ref[rows, :].astype(F32)
        attended = jnp.concatenate(
            [value[:half] / totals[t : t + 1], value[half:] / totals[t + 4 : t + 5]], axis=0
        )
        out = inducing_ref[...].astype(F32) + dot(attended.T.astype(BF), proj_ref[3])
        store(t // TLY, t % TLY, out.astype(BF))


def combine_first_kernel(
    own_ref, other_ref, inducing_ref, proj_ref, after_any, out_ref, column_ref
):
    def store(x, y, value):
        out_ref[x, y] = value

    summarize(0, own_ref, other_ref, inducing_ref, proj_ref, store)
    for x in range(TLX):
        column_ref[x] = jnp.where(lax.axis_index("zl") == 0, out_ref[x, TLY - 1], out_ref[x, 0])


def pair_lines(rows, near_ref, far_ref):
    even = lax.axis_index("tx") % 2 == 0
    for y, (low, high) in enumerate(zip(*rows)):
        near_ref[y] = jnp.where(even, high, low)
        far_ref[y] = jnp.where(even, low, high)


def combine_second_kernel(
    own_ref, other_ref, inducing_ref, proj_ref, first_ref, column_ref, query_any, out_ref, near_ref, far_ref
):
    def store(x, y, value):
        out_ref[x, y] = value

    summarize(1, own_ref, other_ref, inducing_ref, proj_ref, store)
    rows = [
        [out_ref[x, y] for y in range(TLY)] + [first_ref[x, y] for y in range(TLY)] + [column_ref[x]]
        for x in range(TLX)
    ]
    pair_lines(rows, near_ref, far_ref)


def mixture_kernel(
    first_ref,
    column_ref,
    second_ref,
    near_ref,
    far_ref,
    proj_ref,
    mixing_ref,
    key_ref,
    value_ref,
    grid_ref,
    mid_ref,
    side_ref,
):
    half = LANES // HEADS
    blocks = key_ref.shape[0]
    tall = blocks * TLY
    low = lax.axis_index("zl")

    row = lax.broadcasted_iota(jnp.int32, (LANES, LANES), 0)
    col = lax.broadcasted_iota(jnp.int32, (LANES, LANES), 1)
    eye = jnp.where(row == col, 1.0, 0.0).astype(BF)
    blank = jnp.zeros((LANES, LANES), BF)

    def mix(a, b):
        return eye if (a, b) == (0, 0) else mixing_ref[neighbour_steps.index((a, b))]

    for k, a in enumerate((-1, 0, 1)):
        rows = slice(k * 2 * LANES, (k + 1) * 2 * LANES)
        mid_ref[rows, :] = jnp.concatenate(
            [
                jnp.concatenate([mix(a, 0), mix(a, -1)], axis=1),
                jnp.concatenate([mix(a, 1), mix(a, 0)], axis=1),
            ],
            axis=0,
        )
    for k, b in enumerate((-1, 1)):
        side_ref[k] = jnp.concatenate(
            [
                jnp.concatenate([mix(0, b), mix(-1, b)], axis=1),
                jnp.concatenate([mix(1, b), mix(0, b)], axis=1),
                jnp.concatenate([mix(-1, b), blank], axis=1),
                jnp.concatenate([blank, mix(1, b)], axis=1),
            ],
            axis=0,
        )
    ones = head_ones()
    lane = lax.broadcasted_iota(jnp.int32, (1, LANES), 1)
    left = lane < half
    even = lax.axis_index("tx") % 2
    near_row = (1 - even) * (TLX + 1)
    far_row = even * (TLX + 1)
    border = (1 - low) * (tall + 1)
    outside = low * (tall + 1)
    for x in range(TLX):
        for y in range(TLY):
            grid_ref[1 + x, 1 + block_of(0, low) * TLY + y] = first_ref[x, y]
            grid_ref[1 + x, 1 + block_of(1, low) * TLY + y] = second_ref[x, y]
        grid_ref[1 + x, border] = column_ref[x]
    for line, line_ref in ((near_row, near_ref), (far_row, far_ref)):
        for y in range(TLY):
            grid_ref[line, 1 + block_of(1, low) * TLY + y] = line_ref[y]
            grid_ref[line, 1 + block_of(0, low) * TLY + y] = line_ref[TLY + y]
        grid_ref[line, border] = line_ref[2 * TLY]
    for x in range(TLX + 2):
        grid_ref[x, outside] = blank

    def tile(i, j):
        return grid_ref[i, j + 1]

    mids, lefts, rights = [], [], []
    for i in range(2):
        for b in range(blocks):
            mids.append(
                jnp.concatenate(
                    [tile(i + r, 2 * b + s) for r in range(3) for s in range(2)], axis=1
                )
            )
    for b in range(blocks):
        lefts.append(jnp.concatenate([tile(i, 2 * b - 1) for i in (1, 2, 0, 3)], axis=1))
        rights.append(jnp.concatenate([tile(i, 2 * b + 2) for i in (1, 2, 0, 3)], axis=1))
    middle = dot(jnp.concatenate(mids, axis=0), mid_ref[...])
    from_left = dot(jnp.concatenate(lefts, axis=0), side_ref[0])
    from_right = dot(jnp.concatenate(rights, axis=0), side_ref[1])
    mixtures = []
    for b in range(blocks):
        span = slice(b * LANES, (b + 1) * LANES)
        for i in range(2):
            m = middle[(i * blocks + b) * LANES : (i * blocks + b + 1) * LANES]
            cols = slice(i * LANES, (i + 1) * LANES)
            mixtures.append((m[:, :LANES] + from_left[span, cols]).astype(BF))
            mixtures.append((m[:, LANES:] + from_right[span, cols]).astype(BF))
    mixtures = jnp.concatenate(mixtures, axis=0)
    keys = unit(dot(mixtures, proj_ref[1]), ones)
    values = dot(mixtures, proj_ref[2])
    for b in range(blocks):
        spans = [slice((b * 4 + t) * LANES, (b * 4 + t + 1) * LANES) for t in range(4)]
        for h in range(HEADS):
            mine = left if h == 0 else ~left
            key_ref[b, h * LANES : (h + 1) * LANES, :] = jnp.concatenate(
                [jnp.where(mine, keys[s], 0.0) for s in spans], axis=1
            ).astype(BF)
            value_ref[b, h * LANES : (h + 1) * LANES, :] = jnp.concatenate(
                [jnp.where(mine, values[s], 0.0) for s in spans], axis=1
            ).astype(BF)


def attend_kernel(
    along_y,
    rows0_ref,
    rows1_ref,
    query0_ref,
    query1_ref,
    counts_ref,
    key_ref,
    value_ref,
    proj_ref,
    out_ref,
):
    members, quota, width = rows0_ref.shape
    group = min(GROUP_ROWS // quota, members)
    row = lax.broadcasted_iota(jnp.int32, (quota, LANES), 0)
    left = lax.broadcasted_iota(jnp.int32, (1, LANES), 1) < LANES // HEADS
    for half_id, (rows_ref, query_ref) in enumerate(
        ((rows0_ref, query0_ref), (rows1_ref, query1_ref))
    ):
        block = block_of(half_id, lax.axis_index("zl"))
        for c in range(members // group):
            expanded = jnp.concatenate([query_ref[c * group + k] for k in range(group)], axis=0)
            scores = dot_t(expanded, key_ref[block])
            weights = jnp.exp2(scores * (sharpness * math.log2(math.e)))
            totals = [
                jnp.sum(weights[:, h * LANES : (h + 1) * LANES], axis=1, keepdims=True)
                for h in range(HEADS)
            ]
            every = dot(weights.astype(BF), value_ref[block])
            pieces = pieces_of(c * group, group, half_id, along_y)
            attended = []
            for k in range(group):
                bounds = row_bounds(pieces[k], counts_ref, along_y * TLY)
                span = slice(k * quota, (k + 1) * quota)
                part = every[span]
                picked = part[:, :LANES]
                for t, bound in enumerate(bounds):
                    tile = part[:, (t + 1) * LANES : (t + 2) * LANES]
                    picked = jnp.where(row >= bound, tile, picked)
                total = jnp.where(left, totals[0][span], totals[1][span])
                attended.append(quotient(picked, total).astype(BF))
            x = jnp.concatenate([rows_ref[c * group + k] for k in range(group)], axis=0)
            added = dot(jnp.concatenate(attended, axis=0), proj_ref[3])
            result = (x.astype(F32) + added).astype(BF)
            for k in range(group):
                out_ref[c * group + k, half_id] = result[k * quota : (k + 1) * quota]


def scatter_kernel(rows_ref, index_ref, out_hbm, wide_ref, part_ref, out_ref, sems):
    chunk = part_ref.shape[0]
    members, halves, quota, width = rows_ref.shape
    group = chunk // (halves * quota)

    def step(c, carry):
        for k in range(group):
            for half_id in range(halves):
                row = (k * halves + block_of(half_id, k % 2)) * quota
                part_ref[row : row + quota, :] = rows_ref[c * group + k, half_id].astype(F32)
        for r in range(chunk):
            i = index_ref[c * (chunk // LANES) + r // LANES, r % LANES]
            wide_ref[pl.ds(i, 1), :] = part_ref[pl.ds(r, 1), :]
        return carry

    lax.fori_loop(0, members // group, step, 0)
    count = sems.shape[0]
    size = wide_ref.shape[0] // count
    copies = []
    for k in range(count):
        span = pl.ds(k * size, size)
        out_ref[span, :] = wide_ref[span, :].astype(BF)
        copies.append(pltpu.make_async_copy(out_ref.at[span], out_hbm.at[span], sems.at[k]))
        copies[k].start()
    for copy in copies:
        copy.wait()


def call(kernel, name, out_shape, in_specs, scratch, micros, operands, megabytes=20, out_space=pltpu.VMEM):
    spaces = {"v": pltpu.VMEM, "s": pltpu.SMEM, "a": pl.ANY}
    many = isinstance(out_shape, tuple)
    whole = pl.BlockSpec(memory_space=out_space)
    return pl.pallas_call(
        kernel,
        out_shape=out_shape,
        in_specs=[pl.BlockSpec(memory_space=spaces[c]) for c in in_specs],
        out_specs=(whole,) * len(out_shape) if many else whole,
        scratch_shapes=scratch,
        compiler_params=pltpu.CompilerParams(vmem_limit_bytes=megabytes * 1024 * 1024),
        cost_estimate=pl.CostEstimate(
            flops=int(micros * 5e8), bytes_accessed=int(micros * 1e6), transcendentals=0
        ),
        name=name,
    )(*operands)


def body(
    points,
    embed_weight,
    inner_weights,
    output_weight,
    counts,
    point_order,
    inducing,
    first_proj,
    second_proj,
    mixing,
):
    along_x = lax.axis_size("tx")
    highs = lax.axis_size("zh")
    lows = lax.axis_size("zl")
    along_y = highs * lows
    point_count, width = points.shape
    quota = point_count // (along_x * along_y)
    grid_y = along_y * TLY
    blocks = 2
    members = along_x * lows
    tall = blocks * TLY
    lines = point_count // LANES
    chunk = 1024
    half_rows = (members, quota, width)

    def shape(sizes, dtype=BF):
        return jax.ShapeDtypeStruct(sizes, dtype)

    weights = (embed_weight, inner_weights, output_weight)
    buffers = [
        VMEM((point_count, width), F32),
        VMEM((chunk, width), F32),
        VMEM((chunk, width), F32),
    ]
    first, index = call(
        functools.partial(encode_first_kernel, grid_y, along_y, quota),
        "encode_first",
        (shape(half_rows), shape((lines, LANES), jnp.int32)),
        "aaaaaa",
        [
            SMEM((counts.shape[1],), jnp.int32),
            SMEM((counts.shape[1],), jnp.int32),
            SMEM((lines, LANES), jnp.int32),
        ]
        + buffers
        + [VMEM(a.shape, BF) for a in (points, *weights)]
        + [VMEM((lines, LANES), jnp.int32), pltpu.SemaphoreType.DMA((7,))],
        8,
        (points, *weights, counts, point_order.reshape(lines, LANES)),
        megabytes=56,
    )
    second = call(
        functools.partial(encode_second_kernel, quota),
        "encode_second",
        shape(half_rows),
        "vvvva",
        [SMEM((lines, LANES), jnp.int32)] + buffers + [pltpu.SemaphoreType.DMA],
        6,
        (points, *weights, index),
    )

    def exchange(rows):
        return lax.all_to_all(rows, ("tx", "zl"), split_axis=0, concat_axis=0, tiled=True)

    rows0 = exchange(first)
    rows1 = exchange(second)

    part_rows = 4 * LANES + 16
    parts = (shape((part_rows, LANES), F32), shape((part_rows, LANES)))
    sums = [VMEM((part_rows, HEADS * LANES), F32)]
    expanded = shape((members, quota, 4 * width))
    own0, send0, first_queries, value_weight, query0 = call(
        functools.partial(partial_kernel, 0, along_y),
        "partial_first",
        parts
        + (shape((HEADS * LANES, width)), shape((LANES, width)), expanded),
        "vsvvv",
        sums,
        3,
        (rows0, counts, inducing, first_proj, second_proj),
    )
    pairs = [(h, l) for h in range(highs) for l in range(lows)]

    def swap(value, flip_high, flip_low):
        steps = []
        for h, l in pairs:
            other_h = highs - 1 - h if flip_high else h
            other_l = lows - 1 - l if flip_low else l
            steps.append((h * lows + l, other_h * lows + other_l))
        return lax.ppermute(value, ("zh", "zl"), steps)

    other0 = swap(send0, True, False)
    own1, send1 = call(
        functools.partial(partial_kernel, 1, along_y),
        "partial_second",
        parts,
        "vsvvv",
        sums,
        3,
        (rows1, counts, first_queries, value_weight, first_proj),
    )
    other1 = swap(send1, True, False)
    first_half, border = call(
        combine_first_kernel,
        "combine_first",
        (shape((TLX, TLY, LANES, width)), shape((TLX, LANES, width))),
        "vvvva",
        [],
        0.01,
        (own0, other0, inducing, first_proj, send1),
    )
    column = swap(border, False, True)
    query1 = call(
        functools.partial(queries_kernel, along_y),
        "queries_second",
        expanded,
        "vsva",
        [],
        0.01,
        (rows1, counts, second_proj, border),
    )
    near_pairs = [(i, i ^ 1) for i in range(along_x)]
    far_pairs = [(i, ((i + 1) ^ 1) - 1) for i in range(1, along_x - 1)]

    line = shape((2 * TLY + 1, LANES, width))
    second_half, near, far = call(
        combine_second_kernel,
        "combine_second",
        (shape((TLX, TLY, LANES, width)), line, line),
        "vvvvvva",
        [],
        0.01,
        (own1, other1, inducing, first_proj, first_half, column, query1),
    )
    near = lax.ppermute(near, "tx", near_pairs)
    far = lax.ppermute(far, "tx", far_pairs)

    keys, values = call(
        mixture_kernel,
        "mix_tiles",
        (shape((blocks, HEADS * LANES, 4 * LANES)), shape((blocks, HEADS * LANES, 4 * LANES))),
        "v" * 7,
        [
            VMEM((TLX + 2, tall + 2, LANES, width), BF),
            VMEM((6 * LANES, 2 * LANES), BF),
            VMEM((2, 4 * LANES, 2 * LANES), BF),
        ],
        1,
        (first_half, column, second_half, near, far, second_proj, mixing),
    )

    result = call(
        functools.partial(attend_kernel, along_y),
        "attend_points",
        shape((members, 2, quota, width)),
        "vvvvsvvv",
        [],
        7,
        (rows0, rows1, query0, query1, counts, keys, values, second_proj),
    )
    return call(
        scatter_kernel,
        "scatter_rows",
        shape((point_count, width)),
        "vs",
        [
            VMEM((point_count, width), F32),
            VMEM((512, width), F32),
            VMEM((point_count, width), BF),
            pltpu.SemaphoreType.DMA((4,)),
        ],
        5,
        (exchange(result), index),
        out_space=pl.ANY,
    )


def solution(mesh):
    along_x, along_y = mesh.devices.shape
    split = jax.sharding.Mesh(mesh.devices.reshape(along_x, 2, along_y // 2), ("tx", "zh", "zl"))
    rows = P(("tx", "zh", "zl"), None)
    placed = (rows, P(), P(), P(), P(), rows, P(), P(), P(), P())
    return jax.shard_map(body, mesh=split, in_specs=placed, out_specs=rows, check_vma=False)
```

```python
import functools
import math

import jax
import jax.numpy as jnp
from jax import lax
from jax.experimental import pallas as pl
from jax.experimental.pallas import tpu as pltpu
from jax.sharding import PartitionSpec as P

HEADS = 2
TLX = 2
TLY = 2
LANES = 128
GROUP_ROWS = 2048
BF = jnp.bfloat16
F32 = jnp.float32

sharpness = 32.0
epsilon = 1e-06
neighbour_steps = ((-1, -1), (-1, 0), (-1, 1), (0, -1), (0, 1), (1, -1), (1, 0), (1, 1))
VMEM = pltpu.VMEM
SMEM = pltpu.SMEM


def dot(a, b):
    return jnp.dot(a, b, preferred_element_type=F32)


def dot_t(a, b):
    return lax.dot_general(a, b, (((1,), (1,)), ((), ())), preferred_element_type=F32)


def head_ones():
    row = lax.broadcasted_iota(jnp.int32, (LANES, LANES), 0)
    col = lax.broadcasted_iota(jnp.int32, (LANES, LANES), 1)
    half = LANES // HEADS
    return jnp.where((row // half) == (col // half), 1.0, 0.0).astype(BF)


def unit(v, ones):
    return v * lax.rsqrt(dot((v * v).astype(BF), ones) + epsilon)


def silu(v):
    half = 0.5 * v
    return (half + half * jnp.tanh(half)).astype(BF)


def quotient(a, b):
    guess = pl.reciprocal(b, approx=True)
    return a * (guess * (2.0 - b * guess))


def place():
    return lax.axis_index("tx"), lax.axis_index("zh"), lax.axis_index("zl")


def block_of(half_id, low):
    return low if half_id else 1 - low


def encode_rows(half_id, quota, chunk, points, index_ready, weights_ready, w1_ref, w2_ref, w3_ref, index_s, feat_ref, wide_ref, xs):
    rows_total = points.shape[0] // 2
    group = chunk // quota
    wide_ref[...] = points[...].astype(F32)
    index_ready()

    def gather(c, buffer, first, last):
        for r in range(first, last):
            member = r // quota
            spot = (member * 2 + block_of(half_id, member % 2)) * quota + r % quota
            i = index_s[c * (2 * chunk // LANES) + spot // LANES, spot % LANES]
            buffer[pl.ds(r, 1), :] = wide_ref[pl.ds(i, 1), :]

    def layer(x, w, ahead, cuts):
        parts = []
        step = w.shape[1] // 2
        for k in range(2):
            ahead(cuts[k], cuts[k + 1])
            parts.append(silu(dot(x, w[:, k * step : (k + 1) * step])))
        return jnp.concatenate(parts, axis=1)

    def apply(c, buffer, ahead):
        cuts = [chunk * k // 5 for k in range(6)]
        hidden = layer(buffer[...].astype(BF), w1_ref, ahead, cuts[:3])
        hidden = layer(hidden, w2_ref.at[0], ahead, cuts[2:5])
        ahead(cuts[4], cuts[5])
        out = dot(hidden, w3_ref[...]).astype(BF)
        for k in range(group):
            feat_ref[c * group + k] = out[k * quota : (k + 1) * quota]

    chunks = rows_total // chunk
    gather(0, xs[0], 0, chunk)
    weights_ready()
    for c in range(chunks):

        def ahead(a, b):
            if c + 1 < chunks:
                gather(c + 1, xs[(c + 1) % 2], a, b)

        apply(c, xs[c % 2], ahead)


def encode_first_kernel(
    grid_y,
    along_y,
    quota,
    points_hbm,
    w1_hbm,
    w2_hbm,
    w3_hbm,
    counts_hbm,
    order_hbm,
    feat_ref,
    index_ref,
    counts_s,
    off_ref,
    index_s,
    wide_ref,
    xa_ref,
    xb_ref,
    points_ref,
    w1_ref,
    w2_ref,
    w3_ref,
    order_ref,
    sems,
):
    tx, zh, zl = place()
    own = tx * along_y + zh * (along_y // 2) + zl
    sources = (counts_hbm.at[own], order_hbm, points_hbm, w1_hbm, w2_hbm, w3_hbm)
    targets = (counts_s, order_ref, points_ref, w1_ref, w2_ref, w3_ref)
    copies = [
        pltpu.make_async_copy(a, b, sems.at[k]) for k, (a, b) in enumerate(zip(sources, targets))
    ]
    for copy in copies:
        copy.start()
    tiles = counts_s.shape[0]
    order_rows = order_ref.shape[0]
    rows_total = points_ref.shape[0]
    copies[0].wait()

    def add_up(g, total):
        off_ref[g] = total
        return total + counts_s[g]

    lax.fori_loop(0, tiles, add_up, jnp.int32(0), unroll=8)
    copies[1].wait()
    lane = lax.broadcasted_iota(jnp.int32, (1, LANES), 1)

    def run_of(start):
        line = start >> 7
        shift = start & (LANES - 1)
        first = order_ref[pl.ds(jnp.clip(line, 0, order_rows - 1), 1), :]
        second = order_ref[pl.ds(jnp.clip(line + 1, 0, order_rows - 1), 1), :]
        merged = jnp.where(lane < shift, second, first)
        return pltpu.roll(merged, (LANES - shift) & (LANES - 1), 1)

    per_line = LANES // quota

    def index_line(line, carry):
        value = jnp.zeros((1, LANES), jnp.int32)
        for k in range(per_line):
            d = line * per_line + k
            g1 = (d // along_y) * (TLX * grid_y) + (d % along_y) * TLY
            n1 = counts_s[g1] + counts_s[g1 + 1]
            run1 = run_of(off_ref[g1] - k * quota)
            run2 = run_of(off_ref[g1 + grid_y] - n1 - k * quota)
            both = jnp.where(lane < k * quota + n1, run1, run2)
            value = both if k == 0 else jnp.where(lane >= k * quota, both, value)
        index_ref[pl.ds(line, 1), :] = value
        return carry

    lax.fori_loop(0, rows_total // LANES, index_line, 0, unroll=8)
    copy = pltpu.make_async_copy(index_ref, index_s, sems.at[6])
    copy.start()
    copies[2].wait()

    def weights_ready():
        for k in (3, 4, 5):
            copies[k].wait()

    encode_rows(
        0, quota, xa_ref.shape[0], points_ref, copy.wait, weights_ready, w1_ref, w2_ref, w3_ref, index_s,
        feat_ref, wide_ref, (xa_ref, xb_ref),
    )


def encode_second_kernel(
    quota, points_ref, w1_ref, w2_ref, w3_ref, index_any, feat_ref, index_s, wide_ref, xa_ref, xb_ref, sem
):
    copy = pltpu.make_async_copy(index_any, index_s, sem)
    copy.start()
    encode_rows(
        1, quota, xa_ref.shape[0], points_ref, copy.wait, lambda: None, w1_ref, w2_ref, w3_ref, index_s,
        feat_ref, wide_ref, (xa_ref, xb_ref),
    )


def tile_of(position, counts_ref, pieces, piece_id, grid_y):
    bounds = [None, None, None]
    for k, (s, base) in enumerate(pieces):
        n0 = counts_ref[s, base]
        n1 = counts_ref[s, base + 1]
        n2 = counts_ref[s, base + grid_y]
        for i, found in enumerate((n0, n0 + n1, n0 + n1 + n2)):
            if k == 0:
                bounds[i] = jnp.full(position.shape, found, jnp.int32)
            else:
                bounds[i] = jnp.where(piece_id >= k, found, bounds[i])
    return sum((position >= b).astype(jnp.int32) for b in bounds)


def pieces_of(first, group, half_id, along_y):
    tx, zh, zl = place()
    lows = along_y // 2
    block = zl * 2 + block_of(half_id, zl)
    base = tx * (TLX * along_y * TLY) + block * TLY
    found = []
    for k in range(group):
        member = first + k
        found.append(((member // lows) * along_y + zh * lows + member % lows, base))
    return found


def row_bounds(piece, counts_ref, grid_y):
    s, base = piece
    n0 = counts_ref[s, base]
    n1 = n0 + counts_ref[s, base + 1]
    return n0, n1, n1 + counts_ref[s, base + grid_y]


def expand_queries(half_id, along_y, rows_ref, counts_ref, proj_ref, out_ref):
    ones = head_ones()
    members, quota, width = rows_ref.shape
    group = min(GROUP_ROWS // quota, members)
    row = lax.broadcasted_iota(jnp.int32, (quota, LANES), 0)
    for c in range(members // group):
        x = jnp.concatenate([rows_ref[c * group + k] for k in range(group)], axis=0)
        query = unit(dot(x, proj_ref[0]), ones)
        pieces = pieces_of(c * group, group, half_id, along_y)
        for k in range(group):
            bounds = row_bounds(pieces[k], counts_ref, along_y * TLY)
            past = [row >= b for b in bounds]
            mine = query[k * quota : (k + 1) * quota]
            masks = (~past[0], past[0] & ~past[1], past[1] & ~past[2], past[2])
            out_ref[c * group + k] = jnp.concatenate(
                [jnp.where(m, mine, 0.0).astype(BF) for m in masks], axis=1
            )


def partial_kernel(half_id, along_y, rows_ref, counts_ref, *rest):
    num_ref = rest[-1]
    if half_id:
        query_ref, wv_ref, proj_ref, own_ref, send_ref = rest[:-1]
    else:
        inducing_ref, proj_ref, second_ref, own_ref, send_ref, query_ref, wv_ref, point_ref = rest[:-1]
        expand_queries(0, along_y, rows_ref, counts_ref, second_ref, point_ref)
    members, quota, width = rows_ref.shape
    grid_y = along_y * TLY
    half = LANES // HEADS
    group = min(GROUP_ROWS // quota, members)
    chunk = group * quota
    ones = head_ones()
    lane = lax.broadcasted_iota(jnp.int32, (1, LANES), 1)
    left = lane < half
    if half_id:
        queries = query_ref[...]
        wv_t = wv_ref[...]
    else:
        queries = unit(dot(inducing_ref[...], proj_ref[0]), ones)
        queries = jnp.concatenate(
            [jnp.where(left, queries, 0.0), jnp.where(left, 0.0, queries)], axis=0
        ).astype(BF)
        wv_t = proj_ref[2].astype(F32).T.astype(BF)
        query_ref[...] = queries
        wv_ref[...] = wv_t
    spot = lax.broadcasted_iota(jnp.int32, (16, chunk), 1)
    tile_row = lax.broadcasted_iota(jnp.int32, (16, chunk), 0)
    for c in range(members // group):
        x = jnp.concatenate([rows_ref[c * group + k] for k in range(group)], axis=0)
        keys = unit(dot(x, proj_ref[1]), ones).astype(BF)
        weights = jnp.exp2(dot_t(keys, queries) * (sharpness * math.log2(math.e))).astype(BF)
        values = dot_t(wv_t, x).astype(BF)
        pieces = pieces_of(c * group, group, half_id, along_y)
        tile = tile_of(spot % quota, counts_ref, pieces, spot // quota, grid_y)
        stacked = []
        for t in range(4):
            mask = jnp.where(tile == t, 1.0, 0.0).astype(BF)
            stacked += [values[k : k + 16] * mask for k in range(0, LANES, 16)]
        stacked.append(jnp.where(tile_row == tile, 1.0, 0.0).astype(BF))
        sums = dot(jnp.concatenate(stacked, axis=0), weights)
        if c == 0:
            num_ref[...] = sums
        else:
            num_ref[...] += sums
    last = 4 * LANES
    for t in range(4):
        rows = slice(t * LANES, (t + 1) * LANES)
        value = jnp.concatenate(
            [
                num_ref[t * LANES : t * LANES + half, :LANES],
                num_ref[t * LANES + half : (t + 1) * LANES, LANES:],
            ],
            axis=0,
        )
        own_ref[rows, :] = value
        send_ref[rows, :] = value.astype(BF)
    totals = jnp.concatenate(
        [num_ref[last : last + 4, h * LANES : (h + 1) * LANES] for h in range(HEADS)]
        + [jnp.zeros((8, LANES), F32)],
        axis=0,
    )
    own_ref[last:, :] = totals
    send_ref[last:, :] = totals.astype(BF)

def queries_kernel(along_y, rows_ref, counts_ref, proj_ref, before_any, out_ref):
    expand_queries(1, along_y, rows_ref, counts_ref, proj_ref, out_ref)


def summarize(half_id, own_ref, other_ref, inducing_ref, proj_ref, store):
    half = LANES // HEADS
    last = 4 * LANES
    totals = own_ref[last:, :] + other_ref[last:, :].astype(F32)
    for t in range(4):
        rows = slice(t * LANES, (t + 1) * LANES)
        value = own_ref[rows, :] + other_ref[rows, :].astype(F32)
        attended = jnp.concatenate(
            [value[:half] / totals[t : t + 1], value[half:] / totals[t + 4 : t + 5]], axis=0
        )
        out = inducing_ref[...].astype(F32) + dot(attended.T.astype(BF), proj_ref[3])
        store(t // TLY, t % TLY, out.astype(BF))


def combine_first_kernel(
    own_ref, other_ref, inducing_ref, proj_ref, after_any, out_ref, column_ref
):
    def store(x, y, value):
        out_ref[x, y] = value

    summarize(0, own_ref, other_ref, inducing_ref, proj_ref, store)
    for x in range(TLX):
        column_ref[x] = jnp.where(lax.axis_index("zl") == 0, out_ref[x, TLY - 1], out_ref[x, 0])


def send_line(near, rows, out_ref):
    upper = lax.axis_index("tx") % 2 == (0 if near else 1)
    for y, (low, high) in enumerate(zip(*rows)):
        out_ref[y] = jnp.where(upper, high, low)


def combine_second_kernel(
    own_ref,
    other_ref,
    inducing_ref,
    proj_ref,
    first_ref,
    column_ref,
    query_any,
    out_ref,
    near0_ref,
    near1_ref,
    far_ref,
):
    def store(x, y, value):
        out_ref[x, y] = value

    summarize(1, own_ref, other_ref, inducing_ref, proj_ref, store)
    late = [[out_ref[x, y] for y in range(TLY)] for x in range(TLX)]
    early = [[first_ref[x, y] for y in range(TLY)] + [column_ref[x]] for x in range(TLX)]
    send_line(False, [a + b for a, b in zip(late, early)], far_ref)
    send_line(True, early, near0_ref)
    send_line(True, late, near1_ref)


def mixture_kernel(
    first_ref,
    column_ref,
    second_ref,
    near0_ref,
    near1_ref,
    far_ref,
    proj_ref,
    mixing_ref,
    key_ref,
    value_ref,
    grid_ref,
    mid_ref,
    side_ref,
):
    half = LANES // HEADS
    blocks = key_ref.shape[0]
    tall = blocks * TLY
    low = lax.axis_index("zl")

    row = lax.broadcasted_iota(jnp.int32, (LANES, LANES), 0)
    col = lax.broadcasted_iota(jnp.int32, (LANES, LANES), 1)
    eye = jnp.where(row == col, 1.0, 0.0).astype(BF)
    blank = jnp.zeros((LANES, LANES), BF)

    def mix(a, b):
        return eye if (a, b) == (0, 0) else mixing_ref[neighbour_steps.index((a, b))]

    for k, a in enumerate((-1, 0, 1)):
        rows = slice(k * 2 * LANES, (k + 1) * 2 * LANES)
        mid_ref[rows, :] = jnp.concatenate(
            [
                jnp.concatenate([mix(a, 0), mix(a, -1)], axis=1),
                jnp.concatenate([mix(a, 1), mix(a, 0)], axis=1),
            ],
            axis=0,
        )
    for k, b in enumerate((-1, 1)):
        side_ref[k] = jnp.concatenate(
            [
                jnp.concatenate([mix(0, b), mix(-1, b)], axis=1),
                jnp.concatenate([mix(1, b), mix(0, b)], axis=1),
                jnp.concatenate([mix(-1, b), blank], axis=1),
                jnp.concatenate([blank, mix(1, b)], axis=1),
            ],
            axis=0,
        )
    ones = head_ones()
    lane = lax.broadcasted_iota(jnp.int32, (1, LANES), 1)
    left = lane < half
    even = lax.axis_index("tx") % 2
    near_row = (1 - even) * (TLX + 1)
    far_row = even * (TLX + 1)
    border = (1 - low) * (tall + 1)
    outside = low * (tall + 1)
    for x in range(TLX):
        for y in range(TLY):
            grid_ref[1 + x, 1 + block_of(0, low) * TLY + y] = first_ref[x, y]
            grid_ref[1 + x, 1 + block_of(1, low) * TLY + y] = second_ref[x, y]
        grid_ref[1 + x, border] = column_ref[x]
    for y in range(TLY):
        grid_ref[near_row, 1 + block_of(1, low) * TLY + y] = near1_ref[y]
        grid_ref[near_row, 1 + block_of(0, low) * TLY + y] = near0_ref[y]
        grid_ref[far_row, 1 + block_of(1, low) * TLY + y] = far_ref[y]
        grid_ref[far_row, 1 + block_of(0, low) * TLY + y] = far_ref[TLY + y]
    grid_ref[near_row, border] = near0_ref[TLY]
    grid_ref[far_row, border] = far_ref[2 * TLY]
    for x in range(TLX + 2):
        grid_ref[x, outside] = blank

    def tile(i, j):
        return grid_ref[i, j + 1]

    mids, lefts, rights = [], [], []
    for i in range(2):
        for b in range(blocks):
            mids.append(
                jnp.concatenate(
                    [tile(i + r, 2 * b + s) for r in range(3) for s in range(2)], axis=1
                )
            )
    for b in range(blocks):
        lefts.append(jnp.concatenate([tile(i, 2 * b - 1) for i in (1, 2, 0, 3)], axis=1))
        rights.append(jnp.concatenate([tile(i, 2 * b + 2) for i in (1, 2, 0, 3)], axis=1))
    middle = dot(jnp.concatenate(mids, axis=0), mid_ref[...])
    from_left = dot(jnp.concatenate(lefts, axis=0), side_ref[0])
    from_right = dot(jnp.concatenate(rights, axis=0), side_ref[1])
    mixtures = []
    for b in range(blocks):
        span = slice(b * LANES, (b + 1) * LANES)
        for i in range(2):
            m = middle[(i * blocks + b) * LANES : (i * blocks + b + 1) * LANES]
            cols = slice(i * LANES, (i + 1) * LANES)
            mixtures.append((m[:, :LANES] + from_left[span, cols]).astype(BF))
            mixtures.append((m[:, LANES:] + from_right[span, cols]).astype(BF))
    mixtures = jnp.concatenate(mixtures, axis=0)
    keys = unit(dot(mixtures, proj_ref[1]), ones)
    values = dot(mixtures, proj_ref[2])
    for b in range(blocks):
        spans = [slice((b * 4 + t) * LANES, (b * 4 + t + 1) * LANES) for t in range(4)]
        for h in range(HEADS):
            mine = left if h == 0 else ~left
            key_ref[b, h * LANES : (h + 1) * LANES, :] = jnp.concatenate(
                [jnp.where(mine, keys[s], 0.0) for s in spans], axis=1
            ).astype(BF)
            value_ref[b, h * LANES : (h + 1) * LANES, :] = jnp.concatenate(
                [jnp.where(mine, values[s], 0.0) for s in spans], axis=1
            ).astype(BF)


def attend_kernel(
    along_y,
    rows0_ref,
    rows1_ref,
    query0_ref,
    query1_ref,
    counts_ref,
    key_ref,
    value_ref,
    proj_ref,
    out_ref,
):
    members, quota, width = rows0_ref.shape
    group = min(GROUP_ROWS // quota, members)
    row = lax.broadcasted_iota(jnp.int32, (quota, LANES), 0)
    left = lax.broadcasted_iota(jnp.int32, (1, LANES), 1) < LANES // HEADS
    for half_id, (rows_ref, query_ref) in enumerate(
        ((rows0_ref, query0_ref), (rows1_ref, query1_ref))
    ):
        block = block_of(half_id, lax.axis_index("zl"))
        for c in range(members // group):
            expanded = jnp.concatenate([query_ref[c * group + k] for k in range(group)], axis=0)
            scores = dot_t(expanded, key_ref[block])
            weights = jnp.exp2(scores * (sharpness * math.log2(math.e)))
            totals = [
                jnp.sum(weights[:, h * LANES : (h + 1) * LANES], axis=1, keepdims=True)
                for h in range(HEADS)
            ]
            every = dot(weights.astype(BF), value_ref[block])
            pieces = pieces_of(c * group, group, half_id, along_y)
            attended = []
            for k in range(group):
                bounds = row_bounds(pieces[k], counts_ref, along_y * TLY)
                span = slice(k * quota, (k + 1) * quota)
                part = every[span]
                picked = part[:, :LANES]
                for t, bound in enumerate(bounds):
                    tile = part[:, (t + 1) * LANES : (t + 2) * LANES]
                    picked = jnp.where(row >= bound, tile, picked)
                total = jnp.where(left, totals[0][span], totals[1][span])
                attended.append(quotient(picked, total).astype(BF))
            x = jnp.concatenate([rows_ref[c * group + k] for k in range(group)], axis=0)
            added = dot(jnp.concatenate(attended, axis=0), proj_ref[3])
            result = (x.astype(F32) + added).astype(BF)
            for k in range(group):
                out_ref[c * group + k, half_id] = result[k * quota : (k + 1) * quota]


def scatter_kernel(rows_ref, index_ref, out_hbm, wide_ref, part_ref, out_ref, sems):
    chunk = part_ref.shape[0]
    members, halves, quota, width = rows_ref.shape
    group = chunk // (halves * quota)

    def step(c, carry):
        for k in range(group):
            for half_id in range(halves):
                row = (k * halves + block_of(half_id, k % 2)) * quota
                part_ref[row : row + quota, :] = rows_ref[c * group + k, half_id].astype(F32)
        for r in range(chunk):
            i = index_ref[c * (chunk // LANES) + r // LANES, r % LANES]
            wide_ref[pl.ds(i, 1), :] = part_ref[pl.ds(r, 1), :]
        return carry

    lax.fori_loop(0, members // group, step, 0)
    count = sems.shape[0]
    size = wide_ref.shape[0] // count
    copies = []
    for k in range(count):
        span = pl.ds(k * size, size)
        out_ref[span, :] = wide_ref[span, :].astype(BF)
        copies.append(pltpu.make_async_copy(out_ref.at[span], out_hbm.at[span], sems.at[k]))
        copies[k].start()
    for copy in copies:
        copy.wait()


def call(kernel, name, out_shape, in_specs, scratch, micros, operands, megabytes=20, out_space=pltpu.VMEM):
    spaces = {"v": pltpu.VMEM, "s": pltpu.SMEM, "a": pl.ANY}
    many = isinstance(out_shape, tuple)
    whole = pl.BlockSpec(memory_space=out_space)
    return pl.pallas_call(
        kernel,
        out_shape=out_shape,
        in_specs=[pl.BlockSpec(memory_space=spaces[c]) for c in in_specs],
        out_specs=(whole,) * len(out_shape) if many else whole,
        scratch_shapes=scratch,
        compiler_params=pltpu.CompilerParams(vmem_limit_bytes=megabytes * 1024 * 1024),
        cost_estimate=pl.CostEstimate(
            flops=int(micros * 5e8), bytes_accessed=int(micros * 1e6), transcendentals=0
        ),
        name=name,
    )(*operands)


def body(
    points,
    embed_weight,
    inner_weights,
    output_weight,
    counts,
    point_order,
    inducing,
    first_proj,
    second_proj,
    mixing,
):
    along_x = lax.axis_size("tx")
    highs = lax.axis_size("zh")
    lows = lax.axis_size("zl")
    along_y = highs * lows
    point_count, width = points.shape
    quota = point_count // (along_x * along_y)
    grid_y = along_y * TLY
    blocks = 2
    members = along_x * lows
    tall = blocks * TLY
    lines = point_count // LANES
    chunk = 1024
    half_rows = (members, quota, width)

    def shape(sizes, dtype=BF):
        return jax.ShapeDtypeStruct(sizes, dtype)

    weights = (embed_weight, inner_weights, output_weight)
    buffers = [
        VMEM((point_count, width), F32),
        VMEM((chunk, width), F32),
        VMEM((chunk, width), F32),
    ]
    first, index = call(
        functools.partial(encode_first_kernel, grid_y, along_y, quota),
        "encode_first",
        (shape(half_rows), shape((lines, LANES), jnp.int32)),
        "aaaaaa",
        [
            SMEM((counts.shape[1],), jnp.int32),
            SMEM((counts.shape[1],), jnp.int32),
            SMEM((lines, LANES), jnp.int32),
        ]
        + buffers
        + [VMEM(a.shape, BF) for a in (points, *weights)]
        + [VMEM((lines, LANES), jnp.int32), pltpu.SemaphoreType.DMA((7,))],
        8,
        (points, *weights, counts, point_order.reshape(lines, LANES)),
        megabytes=56,
    )
    second = call(
        functools.partial(encode_second_kernel, quota),
        "encode_second",
        shape(half_rows),
        "vvvva",
        [SMEM((lines, LANES), jnp.int32)] + buffers + [pltpu.SemaphoreType.DMA],
        6,
        (points, *weights, index),
    )

    def exchange(rows):
        return lax.all_to_all(rows, ("tx", "zl"), split_axis=0, concat_axis=0, tiled=True)

    rows0 = exchange(first)
    rows1 = exchange(second)

    part_rows = 4 * LANES + 16
    parts = (shape((part_rows, LANES), F32), shape((part_rows, LANES)))
    sums = [VMEM((part_rows, HEADS * LANES), F32)]
    expanded = shape((members, quota, 4 * width))
    own0, send0, first_queries, value_weight, query0 = call(
        functools.partial(partial_kernel, 0, along_y),
        "partial_first",
        parts
        + (shape((HEADS * LANES, width)), shape((LANES, width)), expanded),
        "vsvvv",
        sums,
        3,
        (rows0, counts, inducing, first_proj, second_proj),
    )
    pairs = [(h, l) for h in range(highs) for l in range(lows)]

    def swap(value, flip_high, flip_low):
        steps = []
        for h, l in pairs:
            other_h = highs - 1 - h if flip_high else h
            other_l = lows - 1 - l if flip_low else l
            steps.append((h * lows + l, other_h * lows + other_l))
        return lax.ppermute(value, ("zh", "zl"), steps)

    other0 = swap(send0, True, False)
    own1, send1 = call(
        functools.partial(partial_kernel, 1, along_y),
        "partial_second",
        parts,
        "vsvvv",
        sums,
        3,
        (rows1, counts, first_queries, value_weight, first_proj),
    )
    other1 = swap(send1, True, False)
    first_half, border = call(
        combine_first_kernel,
        "combine_first",
        (shape((TLX, TLY, LANES, width)), shape((TLX, LANES, width))),
        "vvvva",
        [],
        0.01,
        (own0, other0, inducing, first_proj, send1),
    )
    column = swap(border, False, True)
    query1 = call(
        functools.partial(queries_kernel, along_y),
        "queries_second",
        expanded,
        "vsva",
        [],
        0.01,
        (rows1, counts, second_proj, border),
    )
    near_pairs = [(i, i ^ 1) for i in range(along_x)]
    far_pairs = [(i, ((i + 1) ^ 1) - 1) for i in range(1, along_x - 1)]

    def tiles(count):
        return shape((count, LANES, width))

    second_half, near0, near1, far = call(
        combine_second_kernel,
        "combine_second",
        (shape((TLX, TLY, LANES, width)), tiles(TLY + 1), tiles(TLY), tiles(2 * TLY + 1)),
        "vvvvvva",
        [],
        0.01,
        (own1, other1, inducing, first_proj, first_half, column, query1),
    )
    far = lax.ppermute(far, "tx", far_pairs)
    near0 = lax.ppermute(near0, "tx", near_pairs)
    near1 = lax.ppermute(near1, "tx", near_pairs)

    keys, values = call(
        mixture_kernel,
        "mix_tiles",
        (shape((blocks, HEADS * LANES, 4 * LANES)), shape((blocks, HEADS * LANES, 4 * LANES))),
        "v" * 8,
        [
            VMEM((TLX + 2, tall + 2, LANES, width), BF),
            VMEM((6 * LANES, 2 * LANES), BF),
            VMEM((2, 4 * LANES, 2 * LANES), BF),
        ],
        1,
        (first_half, column, second_half, near0, near1, far, second_proj, mixing),
    )

    result = call(
        functools.partial(attend_kernel, along_y),
        "attend_points",
        shape((members, 2, quota, width)),
        "vvvvsvvv",
        [],
        7,
        (rows0, rows1, query0, query1, counts, keys, values, second_proj),
    )
    return call(
        scatter_kernel,
        "scatter_rows",
        shape((point_count, width)),
        "vs",
        [
            VMEM((point_count, width), F32),
            VMEM((512, width), F32),
            VMEM((point_count, width), BF),
            pltpu.SemaphoreType.DMA((4,)),
        ],
        5,
        (exchange(result), index),
        out_space=pl.ANY,
    )


def solution(mesh):
    along_x, along_y = mesh.devices.shape
    split = jax.sharding.Mesh(mesh.devices.reshape(along_x, 2, along_y // 2), ("tx", "zh", "zl"))
    rows = P(("tx", "zh", "zl"), None)
    placed = (rows, P(), P(), P(), P(), rows, P(), P(), P(), P())
    return jax.shard_map(body, mesh=split, in_specs=placed, out_specs=rows, check_vma=False)
```

```python
import functools
import math

import jax
import jax.numpy as jnp
from jax import lax
from jax.experimental import pallas as pl
from jax.experimental.pallas import tpu as pltpu
from jax.sharding import PartitionSpec as P

HEADS = 2
TLX = 2
TLY = 2
LANES = 128
GROUP_ROWS = 2048
BF = jnp.bfloat16
F32 = jnp.float32

sharpness = 32.0
epsilon = 1e-06
neighbour_steps = ((-1, -1), (-1, 0), (-1, 1), (0, -1), (0, 1), (1, -1), (1, 0), (1, 1))
VMEM = pltpu.VMEM
SMEM = pltpu.SMEM


def dot(a, b):
    return jnp.dot(a, b, preferred_element_type=F32)


def dot_t(a, b):
    return lax.dot_general(a, b, (((1,), (1,)), ((), ())), preferred_element_type=F32)


def head_ones():
    row = lax.broadcasted_iota(jnp.int32, (LANES, LANES), 0)
    col = lax.broadcasted_iota(jnp.int32, (LANES, LANES), 1)
    half = LANES // HEADS
    return jnp.where((row // half) == (col // half), 1.0, 0.0).astype(BF)


def unit(v, ones):
    return v * lax.rsqrt(dot((v * v).astype(BF), ones) + epsilon)


def silu(v):
    half = 0.5 * v
    return (half + half * jnp.tanh(half)).astype(BF)


def quotient(a, b):
    guess = pl.reciprocal(b, approx=True)
    return a * (guess * (2.0 - b * guess))


def place():
    return lax.axis_index("tx"), lax.axis_index("zh"), lax.axis_index("zl")


def block_of(half_id, low):
    return low if half_id else 1 - low


def encode_rows(half_id, quota, chunk, points, index_ready, weights_ready, w1_ref, w2_ref, w3_ref, index_s, feat_ref, wide_ref, xs):
    rows_total = points.shape[0] // 2
    group = chunk // quota
    wide_ref[...] = points[...].astype(F32)
    index_ready()

    def gather(c, buffer, first, last):
        for r in range(first, last):
            member = r // quota
            spot = (member * 2 + block_of(half_id, member % 2)) * quota + r % quota
            i = index_s[c * (2 * chunk // LANES) + spot // LANES, spot % LANES]
            buffer[pl.ds(r, 1), :] = wide_ref[pl.ds(i, 1), :]

    def layer(x, w, ahead, cuts):
        parts = []
        step = w.shape[1] // 2
        for k in range(2):
            ahead(cuts[k], cuts[k + 1])
            parts.append(silu(dot(x, w[:, k * step : (k + 1) * step])))
        return jnp.concatenate(parts, axis=1)

    def apply(c, buffer, ahead):
        cuts = [chunk * k // 5 for k in range(6)]
        hidden = layer(buffer[...].astype(BF), w1_ref, ahead, cuts[:3])
        hidden = layer(hidden, w2_ref.at[0], ahead, cuts[2:5])
        ahead(cuts[4], cuts[5])
        out = dot(hidden, w3_ref[...]).astype(BF)
        for k in range(group):
            feat_ref[c * group + k] = out[k * quota : (k + 1) * quota]

    chunks = rows_total // chunk
    gather(0, xs[0], 0, chunk)
    weights_ready()
    for c in range(chunks):

        def ahead(a, b):
            if c + 1 < chunks:
                gather(c + 1, xs[(c + 1) % 2], a, b)

        apply(c, xs[c % 2], ahead)


def encode_first_kernel(
    grid_y,
    along_y,
    quota,
    points_hbm,
    w1_hbm,
    w2_hbm,
    w3_hbm,
    counts_hbm,
    order_hbm,
    feat_ref,
    index_ref,
    counts_s,
    off_ref,
    index_s,
    wide_ref,
    xa_ref,
    xb_ref,
    points_ref,
    w1_ref,
    w2_ref,
    w3_ref,
    order_ref,
    sems,
):
    tx, zh, zl = place()
    own = tx * along_y + zh * (along_y // 2) + zl
    sources = (counts_hbm.at[own], order_hbm, points_hbm, w1_hbm, w2_hbm, w3_hbm)
    targets = (counts_s, order_ref, points_ref, w1_ref, w2_ref, w3_ref)
    copies = [
        pltpu.make_async_copy(a, b, sems.at[k]) for k, (a, b) in enumerate(zip(sources, targets))
    ]
    for copy in copies:
        copy.start()
    tiles = counts_s.shape[0]
    order_rows = order_ref.shape[0]
    rows_total = points_ref.shape[0]
    copies[0].wait()

    def add_up(g, total):
        off_ref[g] = total
        return total + counts_s[g]

    lax.fori_loop(0, tiles, add_up, jnp.int32(0), unroll=8)
    copies[1].wait()
    lane = lax.broadcasted_iota(jnp.int32, (1, LANES), 1)

    def run_of(start):
        line = start >> 7
        shift = start & (LANES - 1)
        first = order_ref[pl.ds(jnp.clip(line, 0, order_rows - 1), 1), :]
        second = order_ref[pl.ds(jnp.clip(line + 1, 0, order_rows - 1), 1), :]
        merged = jnp.where(lane < shift, second, first)
        return pltpu.roll(merged, (LANES - shift) & (LANES - 1), 1)

    per_line = LANES // quota

    def index_line(line, carry):
        value = jnp.zeros((1, LANES), jnp.int32)
        for k in range(per_line):
            d = line * per_line + k
            g1 = (d // along_y) * (TLX * grid_y) + (d % along_y) * TLY
            n1 = counts_s[g1] + counts_s[g1 + 1]
            run1 = run_of(off_ref[g1] - k * quota)
            run2 = run_of(off_ref[g1 + grid_y] - n1 - k * quota)
            both = jnp.where(lane < k * quota + n1, run1, run2)
            value = both if k == 0 else jnp.where(lane >= k * quota, both, value)
        index_ref[pl.ds(line, 1), :] = value
        return carry

    lax.fori_loop(0, rows_total // LANES, index_line, 0, unroll=8)
    copy = pltpu.make_async_copy(index_ref, index_s, sems.at[6])
    copy.start()
    copies[2].wait()

    def weights_ready():
        for k in (3, 4, 5):
            copies[k].wait()

    encode_rows(
        0, quota, xa_ref.shape[0], points_ref, copy.wait, weights_ready, w1_ref, w2_ref, w3_ref, index_s,
        feat_ref, wide_ref, (xa_ref, xb_ref),
    )


def encode_second_kernel(
    quota, points_ref, w1_ref, w2_ref, w3_ref, index_any, feat_ref, index_s, wide_ref, xa_ref, xb_ref, sem
):
    copy = pltpu.make_async_copy(index_any, index_s, sem)
    copy.start()
    encode_rows(
        1, quota, xa_ref.shape[0], points_ref, copy.wait, lambda: None, w1_ref, w2_ref, w3_ref, index_s,
        feat_ref, wide_ref, (xa_ref, xb_ref),
    )


def tile_of(position, counts_ref, pieces, piece_id, grid_y):
    bounds = [None, None, None]
    for k, (s, base) in enumerate(pieces):
        n0 = counts_ref[s, base]
        n1 = counts_ref[s, base + 1]
        n2 = counts_ref[s, base + grid_y]
        for i, found in enumerate((n0, n0 + n1, n0 + n1 + n2)):
            if k == 0:
                bounds[i] = jnp.full(position.shape, found, jnp.int32)
            else:
                bounds[i] = jnp.where(piece_id >= k, found, bounds[i])
    return sum((position >= b).astype(jnp.int32) for b in bounds)


def pieces_of(first, group, half_id, along_y):
    tx, zh, zl = place()
    lows = along_y // 2
    block = zl * 2 + block_of(half_id, zl)
    base = tx * (TLX * along_y * TLY) + block * TLY
    found = []
    for k in range(group):
        member = first + k
        found.append(((member // lows) * along_y + zh * lows + member % lows, base))
    return found


def row_bounds(piece, counts_ref, grid_y):
    s, base = piece
    n0 = counts_ref[s, base]
    n1 = n0 + counts_ref[s, base + 1]
    return n0, n1, n1 + counts_ref[s, base + grid_y]


def expand_queries(half_id, along_y, rows_ref, counts_ref, proj_ref, out_ref):
    ones = head_ones()
    members, quota, width = rows_ref.shape
    group = min(GROUP_ROWS // quota, members)
    row = lax.broadcasted_iota(jnp.int32, (quota, LANES), 0)
    for c in range(members // group):
        x = jnp.concatenate([rows_ref[c * group + k] for k in range(group)], axis=0)
        query = unit(dot(x, proj_ref[0]), ones)
        pieces = pieces_of(c * group, group, half_id, along_y)
        for k in range(group):
            bounds = row_bounds(pieces[k], counts_ref, along_y * TLY)
            past = [row >= b for b in bounds]
            mine = query[k * quota : (k + 1) * quota]
            masks = (~past[0], past[0] & ~past[1], past[1] & ~past[2], past[2])
            out_ref[c * group + k] = jnp.concatenate(
                [jnp.where(m, mine, 0.0).astype(BF) for m in masks], axis=1
            )


def partial_kernel(half_id, along_y, rows_ref, counts_ref, *rest):
    num_ref = rest[-1]
    if half_id:
        query_ref, wv_ref, proj_ref, own_ref, send_ref = rest[:-1]
    else:
        inducing_ref, proj_ref, second_ref, own_ref, send_ref, query_ref, wv_ref, point_ref = rest[:-1]
        expand_queries(0, along_y, rows_ref, counts_ref, second_ref, point_ref)
    members, quota, width = rows_ref.shape
    grid_y = along_y * TLY
    half = LANES // HEADS
    group = min(GROUP_ROWS // quota, members)
    chunk = group * quota
    ones = head_ones()
    lane = lax.broadcasted_iota(jnp.int32, (1, LANES), 1)
    left = lane < half
    if half_id:
        queries = query_ref[...]
        wv_t = wv_ref[...]
    else:
        queries = unit(dot(inducing_ref[...], proj_ref[0]), ones)
        queries = jnp.concatenate(
            [jnp.where(left, queries, 0.0), jnp.where(left, 0.0, queries)], axis=0
        ).astype(BF)
        wv_t = proj_ref[2].astype(F32).T.astype(BF)
        query_ref[...] = queries
        wv_ref[...] = wv_t
    spot = lax.broadcasted_iota(jnp.int32, (16, chunk), 1)
    tile_row = lax.broadcasted_iota(jnp.int32, (16, chunk), 0)
    for c in range(members // group):
        x = jnp.concatenate([rows_ref[c * group + k] for k in range(group)], axis=0)
        keys = unit(dot(x, proj_ref[1]), ones).astype(BF)
        weights = jnp.exp2(dot_t(keys, queries) * (sharpness * math.log2(math.e))).astype(BF)
        values = dot_t(wv_t, x).astype(BF)
        pieces = pieces_of(c * group, group, half_id, along_y)
        tile = tile_of(spot % quota, counts_ref, pieces, spot // quota, grid_y)
        stacked = []
        for t in range(4):
            mask = jnp.where(tile == t, 1.0, 0.0).astype(BF)
            stacked += [values[k : k + 16] * mask for k in range(0, LANES, 16)]
        stacked.append(jnp.where(tile_row == tile, 1.0, 0.0).astype(BF))
        sums = dot(jnp.concatenate(stacked, axis=0), weights)
        if c == 0:
            num_ref[...] = sums
        else:
            num_ref[...] += sums
    last = 4 * LANES
    for t in range(4):
        rows = slice(t * LANES, (t + 1) * LANES)
        value = jnp.concatenate(
            [
                num_ref[t * LANES : t * LANES + half, :LANES],
                num_ref[t * LANES + half : (t + 1) * LANES, LANES:],
            ],
            axis=0,
        )
        own_ref[rows, :] = value
        send_ref[rows, :] = value.astype(BF)
    totals = jnp.concatenate(
        [num_ref[last : last + 4, h * LANES : (h + 1) * LANES] for h in range(HEADS)]
        + [jnp.zeros((8, LANES), F32)],
        axis=0,
    )
    own_ref[last:, :] = totals
    send_ref[last:, :] = totals.astype(BF)

def queries_kernel(along_y, rows_ref, counts_ref, proj_ref, before_any, out_ref):
    expand_queries(1, along_y, rows_ref, counts_ref, proj_ref, out_ref)


def summarize(half_id, own_ref, other_ref, inducing_ref, proj_ref, store):
    half = LANES // HEADS
    last = 4 * LANES
    totals = own_ref[last:, :] + other_ref[last:, :].astype(F32)
    for t in range(4):
        rows = slice(t * LANES, (t + 1) * LANES)
        value = own_ref[rows, :] + other_ref[rows, :].astype(F32)
        attended = jnp.concatenate(
            [value[:half] / totals[t : t + 1], value[half:] / totals[t + 4 : t + 5]], axis=0
        )
        out = inducing_ref[...].astype(F32) + dot(attended.T.astype(BF), proj_ref[3])
        store(t // TLY, t % TLY, out.astype(BF))


def combine_first_kernel(
    own_ref, other_ref, inducing_ref, proj_ref, after_any, out_ref, column_ref
):
    def store(x, y, value):
        out_ref[x, y] = value

    summarize(0, own_ref, other_ref, inducing_ref, proj_ref, store)
    for x in range(TLX):
        column_ref[x] = jnp.where(lax.axis_index("zl") == 0, out_ref[x, TLY - 1], out_ref[x, 0])


def send_line(near, rows, out_ref):
    upper = lax.axis_index("tx") % 2 == (0 if near else 1)
    for y, (low, high) in enumerate(zip(*rows)):
        out_ref[y] = jnp.where(upper, high, low)


def combine_second_kernel(
    own_ref,
    other_ref,
    inducing_ref,
    proj_ref,
    first_ref,
    column_ref,
    query_any,
    out_ref,
    near0_ref,
    near1_ref,
    far_ref,
):
    def store(x, y, value):
        out_ref[x, y] = value

    summarize(1, own_ref, other_ref, inducing_ref, proj_ref, store)
    late = [[out_ref[x, y] for y in range(TLY)] for x in range(TLX)]
    early = [[first_ref[x, y] for y in range(TLY)] + [column_ref[x]] for x in range(TLX)]
    send_line(False, [a + b for a, b in zip(late, early)], far_ref)
    send_line(True, early, near0_ref)
    send_line(True, late, near1_ref)


def row_of(near):
    odd = lax.axis_index("tx") % 2
    return 1 - odd if near else odd


def mixture_kernel(near, first_ref, column_ref, second_ref, *rest):
    if near:
        early_ref, late_ref = rest[:2]
        rest = rest[2:]
        line = [late_ref[y] for y in range(TLY)] + [early_ref[y] for y in range(TLY + 1)]
    else:
        line_ref = rest[0]
        rest = rest[1:]
        line = [line_ref[y] for y in range(2 * TLY + 1)]
    proj_ref, mixing_ref, key_ref, value_ref, grid_ref, mid_ref = rest
    half = LANES // HEADS
    blocks = key_ref.shape[0]
    tall = blocks * TLY
    low = lax.axis_index("zl")
    above = row_of(near)
    row = lax.broadcasted_iota(jnp.int32, (LANES, LANES), 0)
    col = lax.broadcasted_iota(jnp.int32, (LANES, LANES), 1)
    eye = jnp.where(row == col, 1.0, 0.0).astype(BF)
    blank = jnp.zeros((LANES, LANES), BF)

    def mix(a, b):
        if abs(b) > 1:
            return blank
        return eye if (a, b) == (0, 0) else mixing_ref[neighbour_steps.index((a, b))]

    for k, (a, c) in enumerate((a, c) for a in (-1, 0, 1) for c in range(4)):
        mid_ref[k * LANES : (k + 1) * LANES, :] = jnp.concatenate(
            [mix(a, c - 1), mix(a, c - 2)], axis=1
        )
    border = (1 - low) * (tall + 1)
    outside = low * (tall + 1)
    nb = 2 * above
    for y in range(TLY):
        for x in range(TLX):
            grid_ref[1 - above + x, 1 + block_of(0, low) * TLY + y] = first_ref[x, y]
            grid_ref[1 - above + x, 1 + block_of(1, low) * TLY + y] = second_ref[x, y]
        grid_ref[nb, 1 + block_of(1, low) * TLY + y] = line[y]
        grid_ref[nb, 1 + block_of(0, low) * TLY + y] = line[TLY + y]
    for x in range(TLX):
        grid_ref[1 - above + x, border] = column_ref[x]
    grid_ref[nb, border] = line[2 * TLY]
    for x in range(TLX + 1):
        grid_ref[x, outside] = blank
    around = [
        jnp.concatenate([grid_ref[r, 2 * b + c] for r in range(3) for c in range(4)], axis=1)
        for b in range(blocks)
    ]
    mixed = dot(jnp.concatenate(around, axis=0), mid_ref[...]).astype(BF)
    mixtures = jnp.concatenate(
        [
            mixed[b * LANES : (b + 1) * LANES, y * LANES : (y + 1) * LANES]
            for b in range(blocks)
            for y in range(TLY)
        ],
        axis=0,
    )
    keys = unit(dot(mixtures, proj_ref[1]), head_ones())
    values = dot(mixtures, proj_ref[2])
    left = lax.broadcasted_iota(jnp.int32, (1, LANES), 1) < half
    for b in range(blocks):
        spans = [slice((b * TLY + y) * LANES, (b * TLY + y + 1) * LANES) for y in range(TLY)]
        for h in range(HEADS):
            mine = left if h == 0 else ~left
            rows = slice(h * LANES, (h + 1) * LANES)
            key_ref[b, rows, :] = jnp.concatenate(
                [jnp.where(mine, keys[s], 0.0) for s in spans], axis=1
            ).astype(BF)
            value_ref[b, rows, :] = jnp.concatenate(
                [jnp.where(mine, values[s], 0.0) for s in spans], axis=1
            ).astype(BF)


def attend_kernel(
    near, along_y, query0_ref, query1_ref, counts_ref, key_ref, value_ref, *rest
):
    if near:
        (out_ref,) = rest
    else:
        rows0_ref, rows1_ref, before_ref, proj_ref, out_ref = rest
    members, quota, wide = query0_ref.shape
    group = min(GROUP_ROWS // quota, members)
    row = lax.broadcasted_iota(jnp.int32, (quota, LANES), 0)
    left = lax.broadcasted_iota(jnp.int32, (1, LANES), 1) < LANES // HEADS
    side = row_of(near)
    for half_id, query_ref in enumerate((query0_ref, query1_ref)):
        block = block_of(half_id, lax.axis_index("zl"))
        for c in range(members // group):
            expanded = jnp.concatenate([query_ref[c * group + k] for k in range(group)], axis=0)
            expanded = jnp.where(side == 1, expanded[:, 2 * LANES :], expanded[:, : 2 * LANES])
            scores = dot_t(expanded, key_ref[block])
            weights = jnp.exp2(scores * (sharpness * math.log2(math.e)))
            totals = [
                jnp.sum(weights[:, h * LANES : (h + 1) * LANES], axis=1, keepdims=True)
                for h in range(HEADS)
            ]
            every = dot(weights.astype(BF), value_ref[block])
            pieces = pieces_of(c * group, group, half_id, along_y)
            attended = []
            for k in range(group):
                first, second, third = row_bounds(pieces[k], counts_ref, along_y * TLY)
                span = slice(k * quota, (k + 1) * quota)
                bound = jnp.where(side == 1, third, first)
                picked = jnp.where(row >= bound, every[span, LANES:], every[span, :LANES])
                total = jnp.where(left, totals[0][span], totals[1][span])
                value = quotient(picked, total)
                if not near:
                    inside = (row >= second).astype(jnp.int32) == side
                    other = before_ref[c * group + k, half_id].astype(F32)
                    value = jnp.where(inside, value, other)
                attended.append(value.astype(BF))
            if near:
                for k in range(group):
                    out_ref[c * group + k, half_id] = attended[k]
                continue
            rows_ref = (rows0_ref, rows1_ref)[half_id]
            x = jnp.concatenate([rows_ref[c * group + k] for k in range(group)], axis=0)
            added = dot(jnp.concatenate(attended, axis=0), proj_ref[3])
            result = (x.astype(F32) + added).astype(BF)
            for k in range(group):
                out_ref[c * group + k, half_id] = result[k * quota : (k + 1) * quota]


def scatter_kernel(rows_ref, index_ref, out_hbm, wide_ref, part_ref, out_ref, sems):
    chunk = part_ref.shape[0]
    members, halves, quota, width = rows_ref.shape
    group = chunk // (halves * quota)

    def step(c, carry):
        for k in range(group):
            for half_id in range(halves):
                row = (k * halves + block_of(half_id, k % 2)) * quota
                part_ref[row : row + quota, :] = rows_ref[c * group + k, half_id].astype(F32)
        for r in range(chunk):
            i = index_ref[c * (chunk // LANES) + r // LANES, r % LANES]
            wide_ref[pl.ds(i, 1), :] = part_ref[pl.ds(r, 1), :]
        return carry

    lax.fori_loop(0, members // group, step, 0)
    count = sems.shape[0]
    size = wide_ref.shape[0] // count
    copies = []
    for k in range(count):
        span = pl.ds(k * size, size)
        out_ref[span, :] = wide_ref[span, :].astype(BF)
        copies.append(pltpu.make_async_copy(out_ref.at[span], out_hbm.at[span], sems.at[k]))
        copies[k].start()
    for copy in copies:
        copy.wait()


def call(kernel, name, out_shape, in_specs, scratch, micros, operands, megabytes=20, out_space=pltpu.VMEM):
    spaces = {"v": pltpu.VMEM, "s": pltpu.SMEM, "a": pl.ANY}
    many = isinstance(out_shape, tuple)
    whole = pl.BlockSpec(memory_space=out_space)
    return pl.pallas_call(
        kernel,
        out_shape=out_shape,
        in_specs=[pl.BlockSpec(memory_space=spaces[c]) for c in in_specs],
        out_specs=(whole,) * len(out_shape) if many else whole,
        scratch_shapes=scratch,
        compiler_params=pltpu.CompilerParams(vmem_limit_bytes=megabytes * 1024 * 1024),
        cost_estimate=pl.CostEstimate(
            flops=int(micros * 5e8), bytes_accessed=int(micros * 1e6), transcendentals=0
        ),
        name=name,
    )(*operands)


def body(
    points,
    embed_weight,
    inner_weights,
    output_weight,
    counts,
    point_order,
    inducing,
    first_proj,
    second_proj,
    mixing,
):
    along_x = lax.axis_size("tx")
    highs = lax.axis_size("zh")
    lows = lax.axis_size("zl")
    along_y = highs * lows
    point_count, width = points.shape
    quota = point_count // (along_x * along_y)
    grid_y = along_y * TLY
    blocks = 2
    members = along_x * lows
    tall = blocks * TLY
    lines = point_count // LANES
    chunk = 1024
    half_rows = (members, quota, width)

    def shape(sizes, dtype=BF):
        return jax.ShapeDtypeStruct(sizes, dtype)

    weights = (embed_weight, inner_weights, output_weight)
    buffers = [
        VMEM((point_count, width), F32),
        VMEM((chunk, width), F32),
        VMEM((chunk, width), F32),
    ]
    first, index = call(
        functools.partial(encode_first_kernel, grid_y, along_y, quota),
        "encode_first",
        (shape(half_rows), shape((lines, LANES), jnp.int32)),
        "aaaaaa",
        [
            SMEM((counts.shape[1],), jnp.int32),
            SMEM((counts.shape[1],), jnp.int32),
            SMEM((lines, LANES), jnp.int32),
        ]
        + buffers
        + [VMEM(a.shape, BF) for a in (points, *weights)]
        + [VMEM((lines, LANES), jnp.int32), pltpu.SemaphoreType.DMA((7,))],
        8,
        (points, *weights, counts, point_order.reshape(lines, LANES)),
        megabytes=56,
    )
    second = call(
        functools.partial(encode_second_kernel, quota),
        "encode_second",
        shape(half_rows),
        "vvvva",
        [SMEM((lines, LANES), jnp.int32)] + buffers + [pltpu.SemaphoreType.DMA],
        6,
        (points, *weights, index),
    )

    def exchange(rows):
        return lax.all_to_all(rows, ("tx", "zl"), split_axis=0, concat_axis=0, tiled=True)

    rows0 = exchange(first)
    rows1 = exchange(second)

    part_rows = 4 * LANES + 16
    parts = (shape((part_rows, LANES), F32), shape((part_rows, LANES)))
    sums = [VMEM((part_rows, HEADS * LANES), F32)]
    expanded = shape((members, quota, 4 * width))
    own0, send0, first_queries, value_weight, query0 = call(
        functools.partial(partial_kernel, 0, along_y),
        "partial_first",
        parts
        + (shape((HEADS * LANES, width)), shape((LANES, width)), expanded),
        "vsvvv",
        sums,
        3,
        (rows0, counts, inducing, first_proj, second_proj),
    )
    pairs = [(h, l) for h in range(highs) for l in range(lows)]

    def swap(value, flip_high, flip_low):
        steps = []
        for h, l in pairs:
            other_h = highs - 1 - h if flip_high else h
            other_l = lows - 1 - l if flip_low else l
            steps.append((h * lows + l, other_h * lows + other_l))
        return lax.ppermute(value, ("zh", "zl"), steps)

    other0 = swap(send0, True, False)
    own1, send1 = call(
        functools.partial(partial_kernel, 1, along_y),
        "partial_second",
        parts,
        "vsvvv",
        sums,
        3,
        (rows1, counts, first_queries, value_weight, first_proj),
    )
    other1 = swap(send1, True, False)
    first_half, border = call(
        combine_first_kernel,
        "combine_first",
        (shape((TLX, TLY, LANES, width)), shape((TLX, LANES, width))),
        "vvvva",
        [],
        0.01,
        (own0, other0, inducing, first_proj, send1),
    )
    column = swap(border, False, True)
    query1 = call(
        functools.partial(queries_kernel, along_y),
        "queries_second",
        expanded,
        "vsva",
        [],
        0.01,
        (rows1, counts, second_proj, border),
    )
    near_pairs = [(i, i ^ 1) for i in range(along_x)]
    far_pairs = [(i, ((i + 1) ^ 1) - 1) for i in range(1, along_x - 1)]

    def tiles(count):
        return shape((count, LANES, width))

    second_half, near0, near1, far = call(
        combine_second_kernel,
        "combine_second",
        (shape((TLX, TLY, LANES, width)), tiles(TLY + 1), tiles(TLY), tiles(2 * TLY + 1)),
        "vvvvvva",
        [],
        0.01,
        (own1, other1, inducing, first_proj, first_half, column, query1),
    )
    far = lax.ppermute(far, "tx", far_pairs)
    near0 = lax.ppermute(near0, "tx", near_pairs)
    near1 = lax.ppermute(near1, "tx", near_pairs)

    both_halves = shape((members, 2, quota, width))
    kv = shape((blocks, HEADS * LANES, TLY * LANES))

    def mix(is_near, name, lines):
        return call(
            functools.partial(mixture_kernel, is_near),
            name,
            (kv, kv),
            "v" * (5 + len(lines)),
            [
                VMEM((TLX + 1, tall + 2, LANES, width), BF),
                VMEM((12 * LANES, TLY * LANES), BF),
            ],
            0.01 if is_near else 1,
            (first_half, column, second_half, *lines, second_proj, mixing),
        )

    def attend(is_near, name, pair, more):
        return call(
            functools.partial(attend_kernel, is_near, along_y),
            name,
            both_halves,
            "vvsvv" + "v" * len(more),
            [],
            0.01 if is_near else 2,
            (query0, query1, counts, *pair, *more),
        )

    before = attend(True, "attend_near", mix(True, "mix_near", (near0, near1)), ())
    result = attend(
        False, "attend_far", mix(False, "mix_far", (far,)), (rows0, rows1, before, second_proj)
    )
    return call(
        scatter_kernel,
        "scatter_rows",
        shape((point_count, width)),
        "vs",
        [
            VMEM((point_count, width), F32),
            VMEM((512, width), F32),
            VMEM((point_count, width), BF),
            pltpu.SemaphoreType.DMA((4,)),
        ],
        5,
        (exchange(result), index),
        out_space=pl.ANY,
    )


def solution(mesh):
    along_x, along_y = mesh.devices.shape
    split = jax.sharding.Mesh(mesh.devices.reshape(along_x, 2, along_y // 2), ("tx", "zh", "zl"))
    rows = P(("tx", "zh", "zl"), None)
    placed = (rows, P(), P(), P(), P(), rows, P(), P(), P(), P())
    return jax.shard_map(body, mesh=split, in_specs=placed, out_specs=rows, check_vma=False)
```
